32 devices in a mesh: row: 8 (over y, x, core), head: 4 (over z).
Axes of the slice: x: 2, y: 2, z: 4, core: 2. Of those that a mesh axis runs over, the one named last changes fastest.
Arguments:
- activations: bfloat16 [16384, 768], P('row', 'head'), may hold values from -6 to 6
- segment_ids: int32 [16, 1024], P('row'), may hold values from 0 to 31, never falling along the last dimension, each value on 1 to 512 neighbouring positions
- block_lists: int32 [16, 12, 16, 4], P('row', 'head'), may hold values from -1 to 15, as said below
- feature_proj: bfloat16 [64, 256], replicated, may hold values from -5 to 5
- input_norm_gain: float32 [768], replicated, may hold values from 0.1 to 1.9
- input_norm_bias: float32 [768], replicated, may hold values from -1.5 to 1.5
- qkv_weight: bfloat16 [768, 2304], P(None, 'head'), may hold values from -0.21875 to 0.21875
- out_weight: bfloat16 [768, 768], P('head'), may hold values from -0.875 to 0.875
- middle_norm_gain: float32 [768], replicated, may hold values from 0.2 to 6
- middle_norm_bias: float32 [768], replicated, may hold values from -1.5 to 1.5
- up_weight: bfloat16 [768, 3072], P(None, 'head'), may hold values from -0.21875 to 0.21875
- down_weight: bfloat16 [3072, 768], P('head'), may hold values from -0.109375 to 0.109375
- out_grad: bfloat16 [16384, 768], P('row', 'head'), may hold values from -6 to 6
Outputs:
- block_out: bfloat16 [16384, 768], P('row', 'head')
- input_grad: float32 [16384, 768], P('row', 'head')
- norm_gain_grad: float32 [768], P('head')
- norm_shift_grad: float32 [768], P('head')
- qkv_weight_grad: float32 [768, 2304], P(None, 'head')
- out_weight_grad: float32 [768, 768], P('head')
- middle_norm_gain_gradient: float32 [768], P('head')
- middle_norm_bias_gradient: float32 [768], P('head')
- up_weight_grad: float32 [768, 3072], P(None, 'head')
- down_weight_grad: float32 [3072, 768], P('head')
The draws below stay inside these ranges and needn't reach their ends.
Inputs may be any that keep to these rules, and one draw needn't show every extreme that they name: `segment_ids`: never falling along a sequence; equal numbers in one sequence mark one document, which may be as long as 512 tokens. `block_lists`: each list holds its used entries first, at least one, and -1 in the slots after them; used entries are key blocks of the same sequence and may repeat.
All inputs are finite; a program needn't handle non-finite values.
Results may differ from the reference program's by a relative error of at most 0.018.
Values may be sent and summed in bfloat16 or wider, within the bound.
No kernel may reach another device: no remote copies, remote signals or barrier semaphores. Data moves between devices by JAX's collectives and lax.ppermute only.
A program may use at most 192 MiB of HBM per device.

```python
import math
from functools import partial
import jax
import jax.numpy as jnp
import numpy as np
from jax import lax

D = 768
HEADS = 12
DH = 64
FF = 3072
FEATS = 256
BLK = 64
KMAX = 4
LEN = 1024
DOCS = 32
SEQS = 16
TOKENS = 16384
NB = 16


def draw_block_lists(key, part):
    key = jax.random.fold_in(key, 7)
    count_key, pick_key = jax.random.split(key)
    used = jax.random.randint(count_key, (SEQS, HEADS, NB, 1), 1, KMAX + 1)
    picks = jax.random.randint(pick_key, (SEQS, HEADS, NB, KMAX), 0, NB)
    slot = lax.broadcasted_iota(jnp.int32, (SEQS, HEADS, NB, KMAX), 3)
    return jnp.where(slot < used, picks, -1).astype(jnp.int32)


def draw_middle_norm_gain(key, part):
    key = jax.random.fold_in(key, 11)
    place = lax.broadcasted_iota(jnp.float32, (D,), 0) / (D - 1)
    level = jnp.exp(jnp.log(0.4) + jnp.log(8.0) * place)
    rough = jnp.exp(jax.random.uniform(key, (D,), jnp.float32, jnp.log(0.8), jnp.log(1.25)))
    return (level * rough).astype(jnp.float32)


def block_scale(key, extent, pieces, least, high):
    loudness, own = 1.0, jax.random.fold_in(key, 6)
    for position, shards_of in pieces:
        draws = jnp.exp(jax.random.uniform(jax.random.fold_in(own, position), (shards_of,), jnp.float32, least / len(pieces), high / len(pieces)))
        loudness = loudness * jnp.repeat(draws, extent[position] // shards_of).reshape([-1 if axis == position else 1 for axis in range(len(extent))])
    return loudness


def length_profile(count, total, reach, skew):
    portions = [(1 << 20) // math.isqrt(rank ** skew) + 1 for rank in range(2, count + 1)]
    surplus, given = total - reach - (count - 1), [1] * (count - 1)
    while surplus > 0:
        free = [i for i in range(count - 1) if given[i] < reach]
        whole, budget = sum([portions[i] for i in free]), surplus
        for i in free:
            extra = min(reach - given[i], max(1, budget * portions[i] // whole), surplus)
            given[i] = given[i] + extra
            surplus = surplus - extra
    return np.array([reach] + given)


def ragged_sizes(rng, number_of, total, bound, lean):
    if number_of == 2:
        one = jax.random.randint(rng, (), max(1, total - bound), min(bound, total - 1) + 1)
        return jnp.stack([one, total - one])
    tallies = jnp.asarray(length_profile(number_of, total, bound, lean), jnp.int32)
    pairs = (number_of - 1) // 2
    donor, receiver = tallies[1:1 + 2 * pairs:2], tallies[2:2 + 2 * pairs:2]
    slack = jnp.minimum(donor - 1, bound - receiver)
    moved = jax.random.randint(jax.random.fold_in(rng, 1), (pairs,), 0, 1 << 20) % (slack + 1)
    tallies = tallies.at[1:1 + 2 * pairs:2].set(donor - moved).at[2:2 + 2 * pairs:2].set(receiver + moved)
    return tallies[jax.random.permutation(jax.random.fold_in(rng, 2), number_of)]


def scatter_about(key, shape, scale, limit, pieces=(), kind=jnp.bfloat16):
    level = block_scale(key, shape, pieces, -0.22, 0.18) if pieces else 1.0
    array = jax.random.normal(key, shape, jnp.float32) * scale * level
    return jnp.minimum(jnp.maximum(array, -limit), limit).astype(kind)


def setup_inputs(seed: int = 0) -> dict:
    streams_of = jax.random.split(jax.random.key(seed), 14)
    activations = scatter_about(streams_of[0], (TOKENS, D), 1.0, 6.0, ((0, 8), (1, 4)))
    segment_ids = jax.vmap(lambda own: jnp.searchsorted(jnp.cumsum(ragged_sizes(own, DOCS, LEN, LEN // 2, 2)), jnp.arange(LEN), side="right"))(jax.random.split(streams_of[1], SEQS)).reshape((SEQS, LEN)).astype(jnp.int32)
    block_lists = draw_block_lists(jax.random.fold_in(streams_of[13], 71), 0)
    feature_proj = scatter_about(streams_of[3], (DH, FEATS), 1.0, 5.0)
    input_norm_gain = jnp.clip(1.0 + 0.18 * jax.random.normal(streams_of[4], (D,), jnp.float32), 0.1, 1.9)
    input_norm_bias = scatter_about(streams_of[5], (D,), 0.3, 1.5, (), jnp.float32)
    qkv_weight = scatter_about(streams_of[6], (D, 3 * HEADS * DH), D ** -0.5, 0.21875, ((1, 4),))
    out_weight = scatter_about(streams_of[7], (HEADS * DH, D), (HEADS * DH // 16) ** -0.5, 0.875, ((0, 4),))
    middle_norm_gain = draw_middle_norm_gain(jax.random.fold_in(streams_of[13], 71), 0)
    middle_norm_bias = scatter_about(streams_of[9], (D,), 0.3, 1.5, (), jnp.float32)
    up_weight = scatter_about(streams_of[10], (D, FF), D ** -0.5, 0.21875, ((1, 4),))
    down_weight = scatter_about(streams_of[11], (FF, D), FF ** -0.5, 0.109375, ((0, 4),))
    out_grad = scatter_about(streams_of[12], (TOKENS, D), 1.0, 6.0, ((0, 8), (1, 4)))
    return {"activations": activations, "segment_ids": segment_ids, "block_lists": block_lists, "feature_proj": feature_proj, "input_norm_gain": input_norm_gain, "input_norm_bias": input_norm_bias, "qkv_weight": qkv_weight, "out_weight": out_weight, "middle_norm_gain": middle_norm_gain, "middle_norm_bias": middle_norm_bias, "up_weight": up_weight, "down_weight": down_weight, "out_grad": out_grad}


highest_precision = lax.Precision.HIGHEST

@jax.custom_vjp
def low(v):
    return lax.optimization_barrier(v.astype(jnp.bfloat16)).astype(jnp.float32)

@jax.custom_vjp
def lowrank_backward(v):
    return v

def low_keep(v):
    return (low(v), None)

def low_pass(kept, grad):
    return (grad,)

def back_keep(v):
    return (v, None)

def back_low(kept, grad):
    return (low(grad),)
low.defvjp(low_keep, low_pass)
lowrank_backward.defvjp(back_keep, back_low)

def layer_norm(values, gain, shift):
    center = values - lax.optimization_barrier(jnp.mean(values, axis=-1, keepdims=True))
    spread = lax.optimization_barrier(jnp.mean(center * center, axis=-1, keepdims=True))
    return center * lax.rsqrt(spread + 1e-05) * gain + shift

def feature_map(values, proj):
    quarter = DH ** (-0.25)
    linear = jnp.einsum('lhe,ef->lhf', values, proj, precision=highest_precision)
    pre = quarter * linear - 0.5 * quarter * quarter * lax.optimization_barrier(jnp.sum(values * values, axis=-1, keepdims=True))
    return lowrank_backward(low(jnp.exp(pre) * FEATS ** (-0.5)))

def one_sequence(packed, proj):
    queries, key_rows, val_rows, doc_ids, block_sets = packed
    query_feature_rows = feature_map(queries, proj)
    key_feature_rows = feature_map(key_rows, proj)
    scores = lowrank_backward(jnp.einsum('qhe,khe->hqk', queries, key_rows, precision=highest_precision) * DH ** (-0.5))
    exp_score = jnp.exp(scores)
    lowrank_estimate = lowrank_backward(jnp.einsum('wtl,xtl->twx', query_feature_rows, key_feature_rows, precision=highest_precision))
    same_doc = (doc_ids[:, None] == doc_ids[None, :]).astype(jnp.float32)
    hit_blocks = lax.optimization_barrier(jnp.sum((block_sets[:, :, :, None] == jnp.arange(NB)[None, None, None, :]).astype(jnp.float32), axis=2))
    hit_blocks = jnp.minimum(hit_blocks, 1.0)
    sparse = jnp.repeat(jnp.repeat(hit_blocks, BLK, axis=1), BLK, axis=2) * same_doc[None]
    combined = sparse * exp_score + (same_doc[None] - sparse) * lowrank_estimate
    weights = lowrank_backward(low(combined / lax.optimization_barrier(jnp.sum(combined, axis=-1, keepdims=True))))
    return lowrank_backward(low(jnp.einsum('hqk,khe->qhe', weights, val_rows, precision=highest_precision)))

def forward(inputs, gain_in, shift_in, qkv_w, out_w, gain_mid, shift_mid, up_w, down_w, doc_ids, block_sets, proj):
    normalized_input = low(layer_norm(inputs, gain_in, shift_in))
    qkv = jnp.dot(normalized_input, qkv_w, precision=highest_precision).reshape(SEQS, LEN, HEADS, 3, DH)
    queries = lowrank_backward(low(qkv[:, :, :, 0]))
    key_rows = lowrank_backward(low(qkv[:, :, :, 1]))
    val_rows = lowrank_backward(low(qkv[:, :, :, 2]))
    attend = jax.checkpoint(partial(one_sequence, proj=proj))
    heads_out = lax.map(attend, (queries, key_rows, val_rows, doc_ids, block_sets))
    heads_out = heads_out.reshape(TOKENS, HEADS * DH)
    resid = inputs + lowrank_backward(jnp.dot(heads_out, out_w, precision=highest_precision))
    mid_in = low(resid)
    normalized_middle = low(layer_norm(mid_in, gain_mid, shift_mid))
    pre_act = lowrank_backward(jnp.dot(normalized_middle, up_w, precision=highest_precision))
    acted = low(jax.nn.gelu(pre_act, approximate=False))
    return resid + lowrank_backward(jnp.dot(acted, down_w, precision=highest_precision))

def reference(activations, segment_ids, block_lists, feature_proj, input_norm_gain, input_norm_bias, qkv_weight, out_weight, middle_norm_gain, middle_norm_bias, up_weight, down_weight, out_grad):
    proj = feature_proj.astype(jnp.float32)
    params = (activations.astype(jnp.float32), input_norm_gain.astype(jnp.float32), input_norm_bias.astype(jnp.float32), qkv_weight.astype(jnp.float32), out_weight.astype(jnp.float32), middle_norm_gain.astype(jnp.float32), middle_norm_bias.astype(jnp.float32), up_weight.astype(jnp.float32), down_weight.astype(jnp.float32))

    def layer(*values):
        return forward(*values, segment_ids, block_lists, proj)
    result, pull = jax.vjp(layer, *params)
    grads = pull(out_grad.astype(jnp.float32))
    return (result.astype(jnp.bfloat16), grads[0], grads[1], grads[2], grads[3], grads[4], grads[5], grads[6], grads[7], grads[8])
```

```python
from functools import partial

import math
import jax, jax.numpy as jnp
from jax import lax
from jax.experimental import pallas as pl
from jax.experimental.pallas import tpu as pltpu

BLK = 64
LOG2E = 1.4426950408889634

def dot(a, b, dims):
    return lax.dot_general(a, b, (dims, ((), ())), preferred_element_type=jnp.float32)

def key_span(seg_ref, first_row, rows, tk, length):
    first = seg_ref[0, first_row]
    last = seg_ref[0, first_row + rows - 1]
    lo = jnp.int32(0)
    hi = jnp.int32(0)
    for j in range(length // tk):
        lo += (seg_ref[0, j * tk + tk - 1] < first).astype(jnp.int32)
        hi += (seg_ref[0, j * tk] <= last).astype(jnp.int32)
    return lo, hi

def fwd_kernel(seg_s, qkv_ref, segc_ref, segr_ref, hit_ref, proj_ref,
               out_ref, qf_ref, kf_ref, rinv_ref, vext, *, tq, tk, dh):
    length = qkv_ref.shape[0]
    feats = proj_ref.shape[1]
    quarter = dh ** (-0.25)
    nh = 2
    for h in range(nh):
        base = h * 3 * dh
        for j, f_ref in ((0, qf_ref), (1, kf_ref)):
            def feat_body(i, _, base=base, j=j, f_ref=f_ref, h=h):
                rows = pl.ds(pl.multiple_of(i * 256, 256), 256)
                t = qkv_ref[rows, base + j * dh: base + (j + 1) * dh]
                lin = dot(t, proj_ref[...], ((1,), (0,)))
                tw = t.astype(jnp.float32)
                sq = jnp.sum(tw * tw, axis=1, keepdims=True) * (0.5 * quarter * quarter * LOG2E) + 0.5 * math.log2(feats)
                f_ref[h, rows, :] = jnp.exp2(lin * (quarter * LOG2E) - sq).astype(jnp.bfloat16)
                return 0
            lax.fori_loop(0, length // 256, feat_body, 0)
        v = qkv_ref[:, base + 2 * dh: base + 3 * dh]
        lane = lax.broadcasted_iota(jnp.int32, (length, dh), 1)
        vext[h, :, :] = jnp.concatenate([v, (lane < 1).astype(jnp.bfloat16)], axis=1)

    def q_body(i, _):
        r0 = pl.multiple_of(i * tq, tq)
        lo, hi = key_span(seg_s, r0, tq, tk, length)
        qs = [qkv_ref[pl.ds(r0, tq), h * 3 * dh: h * 3 * dh + dh] for h in range(nh)]
        qfs = [qf_ref[h, pl.ds(r0, tq), :] for h in range(nh)]
        segq = segc_ref[pl.ds(r0, tq), :]
        def k_body(j, acc):
            c0 = pl.multiple_of(j * tk, tk)
            same = segq == segr_ref[:, pl.ds(c0, tk)]
            new = []
            for h in range(nh):
                k = qkv_ref[pl.ds(c0, tk), h * 3 * dh + dh: h * 3 * dh + 2 * dh]
                s = dot(qs[h], k, ((1,), (1,)))
                e = jnp.exp2(s * (LOG2E * dh ** -0.5))
                a = dot(qfs[h], kf_ref[h, pl.ds(c0, tk), :], ((1,), (1,)))
                parts = []
                for b in range(tq // BLK):
                    hit = hit_ref[h, pl.ds(i * (tq // BLK) + b, 1), pl.ds(c0, tk)] > 0.5
                    rs = slice(b * BLK, (b + 1) * BLK)
                    parts.append(jnp.where(jnp.broadcast_to(hit, (BLK, tk)), e[rs], a[rs]))
                comb = jnp.where(same, jnp.concatenate(parts, axis=0), 0.0).astype(jnp.bfloat16)
                new.append(acc[h] + dot(comb, vext[h, pl.ds(c0, tk), :], ((1,), (0,))))
            return tuple(new)
        acc = lax.fori_loop(lo, hi, k_body, tuple(jnp.zeros((tq, 2 * dh), jnp.float32) for _ in range(nh)))
        for h in range(nh):
            rinv = 1.0 / acc[h][:, dh:dh + 1]
            out_ref[pl.ds(r0, tq), h * dh:(h + 1) * dh] = (acc[h][:, :dh] * rinv).astype(jnp.bfloat16)
            rinv_ref[h, pl.ds(r0, tq), :] = rinv
        return 0
    lax.fori_loop(0, length // tq, q_body, 0)

def attn_fwd(qkv, seg, hit, proj, *, tq=256, tk=256):
    length = qkv.shape[0]
    dh, feats = proj.shape
    heads = qkv.shape[1] // (3 * dh)
    pairs = heads // 2
    seg2 = seg.reshape(1, length)
    return pl.pallas_call(
        partial(fwd_kernel, tq=tq, tk=tk, dh=dh),
        grid=(pairs,),
        in_specs=[
            pl.BlockSpec(memory_space=pltpu.SMEM),
            pl.BlockSpec((length, 6 * dh), lambda p: (0, p)),
            pl.BlockSpec((length, 1), lambda p: (0, 0)),
            pl.BlockSpec((1, length), lambda p: (0, 0)),
            pl.BlockSpec((2, length // BLK, length), lambda p: (p, 0, 0)),
            pl.BlockSpec((dh, feats), lambda p: (0, 0)),
        ],
        out_specs=[
            pl.BlockSpec((length, 2 * dh), lambda p: (0, p)),
            pl.BlockSpec((2, length, feats), lambda p: (p, 0, 0)),
            pl.BlockSpec((2, length, feats), lambda p: (p, 0, 0)),
            pl.BlockSpec((2, length, 1), lambda p: (p, 0, 0)),
        ],
        out_shape=[
            jax.ShapeDtypeStruct((length, heads * dh), jnp.bfloat16),
            jax.ShapeDtypeStruct((heads, length, feats), jnp.bfloat16),
            jax.ShapeDtypeStruct((heads, length, feats), jnp.bfloat16),
            jax.ShapeDtypeStruct((heads, length, 1), jnp.float32),
        ],
        scratch_shapes=[pltpu.VMEM((2, length, 2 * dh), jnp.bfloat16)],
        compiler_params=pltpu.CompilerParams(vmem_limit_bytes=48 * 1024 * 1024),
        cost_estimate=pl.CostEstimate(flops=6 * 10**9, bytes_accessed=10**7, transcendentals=10**6),
        name="attn_fwd",
    )(seg2, qkv, seg.reshape(length, 1), seg2, hit, proj)

def bwd_kernel(seg_s, qkv_ref, segc_ref, segr_ref, hit_ref, proj_ref, pext_ref, qf_ref, kf_ref, rinv_ref, o_ref, do_ref,
               dqkv_ref, vext, doext, dq, dk, dv, dqf, dkf, *, tq, tk, dh):
    length = qkv_ref.shape[0]
    quarter = dh ** (-0.25)
    nh = 2
    lane = lax.broadcasted_iota(jnp.int32, (length, dh), 1)
    for h in range(nh):
        base = h * 3 * dh
        v = qkv_ref[:, base + 2 * dh: base + 3 * dh]
        vext[h, :, :] = jnp.concatenate([v, (lane < 2).astype(jnp.bfloat16)], axis=1)
        d_o = do_ref[:, h * dh:(h + 1) * dh].astype(jnp.float32)
        o = o_ref[:, h * dh:(h + 1) * dh].astype(jnp.float32)
        rinv = rinv_ref[h]
        delta = -jnp.sum(d_o * o, axis=1, keepdims=True) * rinv
        high = delta.astype(jnp.bfloat16).astype(jnp.float32)
        low = delta - high
        tail = jnp.where(lane == 0, high, jnp.where(lane == 1, low, 0.0))
        doext[h, :, :] = jnp.concatenate([d_o * rinv, tail], axis=1).astype(jnp.bfloat16)
    dq[...] = jnp.zeros_like(dq)
    dk[...] = jnp.zeros_like(dk)
    dv[...] = jnp.zeros_like(dv)
    dqf[...] = jnp.zeros_like(dqf)
    dkf[...] = jnp.zeros_like(dkf)

    def q_body(i, _):
        r0 = pl.multiple_of(i * tq, tq)
        lo, hi = key_span(seg_s, r0, tq, tk, length)
        rows = pl.ds(r0, tq)
        segq = segc_ref[rows, :]
        def k_body(j, _):
            c0 = pl.multiple_of(j * tk, tk)
            cols = pl.ds(c0, tk)
            same = segq == segr_ref[:, cols]
            for h in range(nh):
                base = h * 3 * dh
                q = qkv_ref[rows, base: base + dh]
                k = qkv_ref[cols, base + dh: base + 2 * dh]
                qf = qf_ref[h, rows, :]
                kf = kf_ref[h, cols, :]
                s = dot(q, k, ((1,), (1,)))
                e = jnp.exp2(s * (LOG2E * dh ** -0.5))
                a = dot(qf, kf, ((1,), (1,)))
                dc = dot(doext[h, rows, :], vext[h, cols, :], ((1,), (1,)))
                dc = jnp.where(same, dc, 0.0)
                combs, dss, das = [], [], []
                for b in range(tq // BLK):
                    hit = hit_ref[h, pl.ds(i * (tq // BLK) + b, 1), cols] > 0.5
                    hit = jnp.broadcast_to(hit, (BLK, tk))
                    rs = slice(b * BLK, (b + 1) * BLK)
                    combs.append(jnp.where(hit, e[rs], a[rs]))
                    dss.append(jnp.where(hit, dc[rs] * e[rs], 0.0))
                    das.append(jnp.where(hit, 0.0, dc[rs]))
                comb = jnp.where(same, jnp.concatenate(combs, axis=0), 0.0).astype(jnp.bfloat16)
                ds = jnp.concatenate(dss, axis=0).astype(jnp.bfloat16)
                da = jnp.concatenate(das, axis=0).astype(jnp.bfloat16)
                dq[h, rows, :] += dot(ds, k, ((1,), (0,)))
                dqf[h, rows, :] += dot(da, kf, ((1,), (0,)))
                dk[h, cols, :] += dot(ds, q, ((0,), (0,)))
                dkf[h, cols, :] += dot(da, qf, ((0,), (0,)))
                dv[h, cols, :] += dot(comb, doext[h, rows, :dh], ((0,), (0,)))
            return 0
        lax.fori_loop(lo, hi, k_body, 0)
        return 0
    lax.fori_loop(0, length // tq, q_body, 0)

    for h in range(nh):
        base = h * 3 * dh
        for j, dt, dfeat, f_ref in ((0, dq, dqf, qf_ref), (1, dk, dkf, kf_ref)):
            def back(i, _, base=base, j=j, dt=dt, dfeat=dfeat, f_ref=f_ref, h=h):
                rows = pl.ds(pl.multiple_of(i * 256, 256), 256)
                dpre = dfeat[h, rows, :] * f_ref[h, rows, :].astype(jnp.float32)
                hi_ = dpre.astype(jnp.bfloat16)
                lo_ = (dpre - hi_.astype(jnp.float32)).astype(jnp.bfloat16)
                thr = dot(hi_, pext_ref[...], ((1,), (0,))) + dot(lo_, pext_ref[...], ((1,), (0,)))
                t = qkv_ref[rows, base + j * dh: base + (j + 1) * dh].astype(jnp.float32)
                g = dt[h, rows, :] * dh ** -0.5 + quarter * thr[:, :dh] - (quarter * quarter) * t * thr[:, dh:dh + 1]
                dqkv_ref[rows, base + j * dh: base + (j + 1) * dh] = g.astype(jnp.bfloat16)
                return 0
            lax.fori_loop(0, length // 256, back, 0)
        dqkv_ref[:, base + 2 * dh: base + 3 * dh] = dv[h].astype(jnp.bfloat16)

def attn_bwd(qkv, seg, hit, proj, qf, kf, rinv, o, d_o, *, tq=256, tk=256):
    length = qkv.shape[0]
    dh, feats = proj.shape
    heads = qkv.shape[1] // (3 * dh)
    pairs = heads // 2
    seg2 = seg.reshape(1, length)
    pext = jnp.concatenate([proj.T, jnp.ones((feats, 1), proj.dtype), jnp.zeros((feats, dh - 1), proj.dtype)], axis=1)
    f32 = jnp.float32
    return pl.pallas_call(
        partial(bwd_kernel, tq=tq, tk=tk, dh=dh),
        grid=(pairs,),
        in_specs=[
            pl.BlockSpec(memory_space=pltpu.SMEM),
            pl.BlockSpec((length, 6 * dh), lambda p: (0, p)),
            pl.BlockSpec((length, 1), lambda p: (0, 0)),
            pl.BlockSpec((1, length), lambda p: (0, 0)),
            pl.BlockSpec((2, length // BLK, length), lambda p: (p, 0, 0)),
            pl.BlockSpec((dh, feats), lambda p: (0, 0)),
            pl.BlockSpec((feats, 2 * dh), lambda p: (0, 0)),
            pl.BlockSpec((2, length, feats), lambda p: (p, 0, 0)),
            pl.BlockSpec((2, length, feats), lambda p: (p, 0, 0)),
            pl.BlockSpec((2, length, 1), lambda p: (p, 0, 0)),
            pl.BlockSpec((length, 2 * dh), lambda p: (0, p)),
            pl.BlockSpec((length, 2 * dh), lambda p: (0, p)),
        ],
        out_specs=pl.BlockSpec((length, 6 * dh), lambda p: (0, p)),
        out_shape=jax.ShapeDtypeStruct((length, heads * 3 * dh), jnp.bfloat16),
        scratch_shapes=[
            pltpu.VMEM((2, length, 2 * dh), jnp.bfloat16),
            pltpu.VMEM((2, length, 2 * dh), jnp.bfloat16),
            pltpu.VMEM((2, length, dh), f32),
            pltpu.VMEM((2, length, dh), f32),
            pltpu.VMEM((2, length, dh), f32),
            pltpu.VMEM((2, length, feats), f32),
            pltpu.VMEM((2, length, feats), f32),
        ],
        compiler_params=pltpu.CompilerParams(vmem_limit_bytes=48 * 1024 * 1024),
        cost_estimate=pl.CostEstimate(flops=15 * 10**9, bytes_accessed=2 * 10**7, transcendentals=10**6),
        name="attn_bwd",
    )(seg2, qkv, seg.reshape(length, 1), seg2, hit, proj, pext, qf, kf, rinv, o, d_o)

def hit_lanes(lists, length):
    nb = lists.shape[1]
    ids = lax.broadcasted_iota(jnp.int32, (1, 1, length), 2) // BLK
    out = lists[:, :, 0:1] == ids
    for s in range(1, lists.shape[2]):
        out = out | (lists[:, :, s:s + 1] == ids)
    return out.astype(jnp.float32)

from jax.sharding import PartitionSpec as P


norm_eps = 1e-05


def xor_move(value, mask, total, only=None):
    pairs = [(i, i ^ mask) for i in range(total) if only is None or only(i)]
    return lax.ppermute(value, ("row", "head"), pairs)


def own_group(i):
    return (i & 3) // 2 == (i >> 2) & 1


def far_group(i):
    return not own_group(i)


def norm_rows(values):
    center = values - jnp.mean(values, axis=1, keepdims=True)
    scale = lax.rsqrt(jnp.mean(center * center, axis=1, keepdims=True) + norm_eps)
    return center * scale, scale


def norm_back(grad, xhat, scale, gain):
    dx = grad * gain
    return scale * (
        dx - jnp.mean(dx, axis=1, keepdims=True) - xhat * jnp.mean(dx * xhat, axis=1, keepdims=True)
    )


def place(pieces, index, mask_of):
    count = len(pieces)
    out = jnp.zeros((count,) + pieces[0].shape, pieces[0].dtype)
    for d, piece in enumerate(pieces):
        out = lax.dynamic_update_index_in_dim(out, piece, index ^ d, 0)
    return out


def shards(
    activations, segment_ids, block_lists, feature_proj, input_norm_gain, input_norm_bias, qkv_weight,
    out_weight, middle_norm_gain, middle_norm_bias, up_weight, down_weight, out_grad,
):
    rows_n, heads_n = lax.axis_size("row"), lax.axis_size("head")
    total = rows_n * heads_n
    r, z = lax.axis_index("row"), lax.axis_index("head")
    c, p = r % 2, (r // 2) % 4
    groups = rows_n // 8
    width = input_norm_gain.shape[0]
    quarter = width // heads_n
    seq_count, length = segment_ids.shape
    half = length // 2
    bf16, f32 = jnp.bfloat16, jnp.float32
    local = (z // 2) == c
    par = z % 2

    def core_swap(v):
        return xor_move(v, 4, total)

    def pick(v, i, axis=0):
        return lax.dynamic_index_in_dim(v, i, axis, keepdims=False)

    def halves(own, other):
        return jnp.where(c == 0, jnp.concatenate([own, other], 0), jnp.concatenate([other, own], 0))

    def spread(v):
        v = v.reshape(seq_count, 2, half, quarter)
        keep, send = pick(v, c, 1), pick(v, 1 - c, 1)
        got = core_swap(send)
        four = halves(keep, got)
        parts = [pick(four, z)] + [xor_move(pick(four, z ^ d), d, total) for d in (1, 2, 3)]
        return place(parts, z, None).transpose(1, 0, 2).reshape(half, width)

    def collect(v):
        v = v.reshape(half, heads_n, quarter).transpose(1, 0, 2)
        parts = [pick(v, z)] + [xor_move(pick(v, z ^ d), d, total) for d in (1, 2, 3)]
        four = place(parts, z, None)
        four = four.reshape(2, seq_count, half, quarter)
        keep, send = pick(four, c), pick(four, 1 - c)
        got = core_swap(send)
        both = jnp.where(c == 0, jnp.stack([keep, got], 1), jnp.stack([got, keep], 1))
        return both.reshape(seq_count * length, quarter)

    def gather_weights(piece):
        mine = pick(piece, p)
        got1 = xor_move(mine, 1, total, own_group)
        got2 = xor_move(mine, 2, total, own_group)
        got3 = xor_move(mine, 3, total, own_group)
        same = jnp.where(local, mine, got2)
        other = jnp.where(local, got1, got3)
        same_all = [same] + [xor_move(same, 8 * d, total, far_group) for d in (1, 2, 3)]
        other_all = [other] + [xor_move(other, 8 * d, total) for d in (1, 2, 3)]
        same_full = jnp.where(local, piece, place(same_all, p, None))
        other_full = place(other_all, p, None)
        return (
            jnp.where(par == 0, same_full, other_full),
            jnp.where(par == 0, other_full, same_full),
        )

    def reduce_grads(parts):
        low = parts.astype(bf16)
        acc = pick(low, p, 1).astype(f32)
        for d in (1, 2, 3):
            acc = acc + xor_move(pick(low, p ^ d, 1), 8 * d, total).astype(f32)
        low = acc.astype(bf16)
        fin = pick(low, par).astype(f32)
        fin = fin + xor_move(pick(low, 1 - par), 1, total, own_group).astype(f32)
        fin = fin + xor_move(pick(low, par), 2, total, far_group).astype(f32)
        fin = fin + xor_move(pick(low, 1 - par), 3, total, far_group).astype(f32)
        for b in range((groups - 1).bit_length()):
            fin = fin + xor_move(fin, 32 << b, total)
        fin = fin.astype(bf16)
        swapped = core_swap(fin)
        fin = jnp.where(local, fin, swapped)
        pieces = [fin] + [xor_move(fin, 8 * d, total) for d in (1, 2, 3)]
        return place(pieces, p, None).astype(f32)

    def sum_all(v):
        for b in range((total - 1).bit_length()):
            v = v + xor_move(v, 1 << b, total)
        return lax.dynamic_slice_in_dim(v, z * quarter, quarter, 1)

    x = spread(activations).astype(f32)
    wq_a, wq_b = gather_weights(qkv_weight.reshape(4, width // 4, -1))
    wq = jnp.concatenate([wq_a.reshape(width, -1), wq_b.reshape(width, -1)], 1)
    pack = jnp.concatenate(
        [
            up_weight.reshape(4, -1, width),
            down_weight.reshape(4, -1, width),
            out_weight.reshape(4, -1, width),
        ],
        1,
    )
    mlp_a, mlp_b = gather_weights(pack)
    hid = up_weight.shape[1]
    n_up, n_down, n_out = width // 4, hid // 4, out_weight.shape[0] // 4
    up = jnp.concatenate([w[:, :n_up].reshape(width, hid) for w in (mlp_a, mlp_b)], 1)
    down = jnp.concatenate([w[:, n_up:n_up + n_down].reshape(hid, width) for w in (mlp_a, mlp_b)], 0)
    outw = jnp.concatenate([w[:, n_up + n_down:].reshape(-1, width) for w in (mlp_a, mlp_b)], 0)

    seg_other = core_swap(segment_ids)
    lists_all = lax.all_gather(block_lists, "head", axis=1, tiled=True)
    lists_other = core_swap(lists_all)
    seg = pick(halves(segment_ids, seg_other), z)
    lists = pick(halves(lists_all, lists_other), z)
    heads_here = lists.shape[0] // 2
    lists = lax.dynamic_slice_in_dim(lists, c * heads_here, heads_here, 0)
    hit = hit_lanes(lists, length)

    xhat1, scale1 = norm_rows(x)
    n1_half = (xhat1 * input_norm_gain + input_norm_bias).astype(bf16)
    n1 = halves(n1_half, core_swap(n1_half))
    qkv = jnp.dot(n1, wq, preferred_element_type=f32).astype(bf16)
    heads_out, qf, kf, rinv = attn_fwd(qkv, seg, hit, feature_proj)

    def half_sum(left, right, dims):
        own = lax.dynamic_slice_in_dim(left, c * half, half, 0)
        oth = lax.dynamic_slice_in_dim(left, (1 - c) * half, half, 0)
        away = lax.dot_general(oth, right, (dims, ((), ())), preferred_element_type=f32).astype(bf16)
        got = core_swap(away)
        return lax.dot_general(own, right, (dims, ((), ())), preferred_element_type=f32) + got.astype(f32)

    nn, nt, tn = ((1,), (0,)), ((1,), (1,)), ((0,), (0,))
    resid = x + half_sum(heads_out, outw, nn)
    xhat2, scale2 = norm_rows(resid.astype(bf16).astype(f32))
    n2_half = (xhat2 * middle_norm_gain + middle_norm_bias).astype(bf16)
    n2 = halves(n2_half, core_swap(n2_half))
    dy_half = spread(out_grad)
    dy = halves(dy_half, core_swap(dy_half))
    pre_act = jnp.dot(n2, up, preferred_element_type=f32)
    act_full, gelu_pull = jax.vjp(partial(jax.nn.gelu, approximate=False), pre_act)
    acted = act_full.astype(bf16)
    d_acted = lax.dot_general(dy, down, (nt, ((), ())), preferred_element_type=f32)
    d_pre = gelu_pull(d_acted)[0].astype(bf16)
    d_n2 = half_sum(d_pre, up, nt)
    block_half = (resid + half_sum(acted, down, nn)).astype(bf16)
    block_out = collect(block_half)
    mid_vec = jnp.stack([jnp.sum(d_n2 * xhat2, 0), jnp.sum(d_n2, 0)])
    d_resid = dy_half.astype(f32) + norm_back(d_n2, xhat2, scale2, middle_norm_gain)
    d_half = d_resid.astype(bf16)
    d_branch = halves(d_half, core_swap(d_half))
    d_heads = lax.dot_general(d_branch, outw, (nt, ((), ())), preferred_element_type=f32).astype(bf16)
    up_g = lax.dot_general(n2, d_pre, (tn, ((), ())), preferred_element_type=f32)
    down_g = lax.dot_general(acted, dy, (tn, ((), ())), preferred_element_type=f32)
    out_g = lax.dot_general(heads_out, d_branch, (tn, ((), ())), preferred_element_type=f32)
    grads = jnp.concatenate(
        [
            up_g.astype(bf16).reshape(4, n_up, 2, hid).transpose(2, 0, 1, 3),
            down_g.astype(bf16).reshape(2, 4, n_down, width),
            out_g.astype(bf16).reshape(2, 4, n_out, width),
        ],
        2,
    )
    mlp_grads = reduce_grads(grads)
    up_grad = mlp_grads[:, :n_up].reshape(width, hid)
    down_grad = mlp_grads[:, n_up:n_up + n_down].reshape(hid, width)
    out_w_grad = mlp_grads[:, n_up + n_down:].reshape(-1, width)
    mid_vec = sum_all(mid_vec)

    d_qkv = attn_bwd(qkv, seg, hit, feature_proj, qf, kf, rinv, heads_out, d_heads)
    d_n1 = half_sum(d_qkv, wq, nt)
    qkv_g = lax.dot_general(n1, d_qkv, (tn, ((), ())), preferred_element_type=f32)
    qkv_g = qkv_g.astype(bf16).reshape(4, width // 4, 2, -1).transpose(2, 0, 1, 3)
    qkv_grad = reduce_grads(qkv_g).reshape(width, -1)
    in_vec = sum_all(jnp.stack([jnp.sum(d_n1 * xhat1, 0), jnp.sum(d_n1, 0)]))
    d_in = norm_back(d_n1, xhat1, scale1, input_norm_gain)
    input_grad = collect((d_resid + d_in).astype(bf16)).astype(f32)
    return (
        block_out, input_grad, in_vec[0], in_vec[1], qkv_grad, out_w_grad, mid_vec[0], mid_vec[1], up_grad, down_grad,
    )


def solution(mesh):
    return jax.shard_map(
        shards,
        mesh=mesh,
        in_specs=(
            P("row", "head"), P("row", None), P("row", "head", None, None), P(), P(), P(), P(None, "head"),
            P("head", None), P(), P(), P(None, "head"), P("head", None), P("row", "head"),
        ),
        out_specs=(
            P("row", "head"), P("row", "head"), P("head"), P("head"), P(None, "head"), P("head", None),
            P("head"), P("head"), P(None, "head"), P("head", None),
        ),
        check_vma=False,
    )
```

```python
from functools import partial

import math
import jax, jax.numpy as jnp
from jax import lax
from jax.experimental import pallas as pl
from jax.experimental.pallas import tpu as pltpu

BLK = 64
LOG2E = 1.4426950408889634

def dot(a, b, dims):
    return lax.dot_general(a, b, (dims, ((), ())), preferred_element_type=jnp.float32)

def meets(seg_ref, r0, tq, c0, tk):
    return (seg_ref[0, r0] <= seg_ref[0, c0 + tk - 1]) & (seg_ref[0, c0] <= seg_ref[0, r0 + tq - 1])

def fwd_kernel(at_ref, seg_s, n_ref, segc_ref, segr_ref, hit_ref, proj_ref, *rest, tq, tk, dh, part):
    out_ref, qf_ref, kf_ref, rinv_ref, qkv_ref, w_ref, vext, sems = rest[-8:]
    copies = [
        pltpu.make_async_copy(piece.at[part], w_ref.at[at_ref[0] ^ d], sems.at[d]) for d, piece in enumerate(rest[:4])
    ]
    for copy in copies:
        copy.start()
    for copy in copies:
        copy.wait()
    weights = w_ref[...].reshape(n_ref.shape[1], qkv_ref.shape[1])

    def project(i, _):
        rows = pl.ds(pl.multiple_of(i * 256, 256), 256)
        qkv_ref[rows, :] = dot(n_ref[rows, :], weights, ((1,), (0,))).astype(jnp.bfloat16)
        return 0

    lax.fori_loop(0, n_ref.shape[0] // 256, project, 0)
    length = qkv_ref.shape[0]
    feats = proj_ref.shape[1]
    quarter = dh ** (-0.25)
    nh = qkv_ref.shape[1] // (3 * dh)
    for h in range(nh):
        base = h * 3 * dh
        for j, f_ref in ((0, qf_ref), (1, kf_ref)):
            def feat_body(i, _, base=base, j=j, f_ref=f_ref, h=h):
                rows = pl.ds(pl.multiple_of(i * 256, 256), 256)
                t = qkv_ref[rows, base + j * dh: base + (j + 1) * dh]
                lin = dot(t, proj_ref[...], ((1,), (0,)))
                tw = t.astype(jnp.float32)
                sq = jnp.sum(tw * tw, axis=1, keepdims=True) * (0.5 * quarter * quarter * LOG2E) + 0.5 * math.log2(feats)
                f_ref[h, rows, :] = jnp.exp2(lin * (quarter * LOG2E) - sq).astype(jnp.bfloat16)
                return 0
            lax.fori_loop(0, length // 256, feat_body, 0)
        v = qkv_ref[:, base + 2 * dh: base + 3 * dh]
        lane = lax.broadcasted_iota(jnp.int32, (length, dh), 1)
        vext[h, :, :] = jnp.concatenate([v, (lane < 1).astype(jnp.bfloat16)], axis=1)

    def q_body(i, _):
        r0 = pl.multiple_of(i * tq, tq)
        qs = [qkv_ref[pl.ds(r0, tq), h * 3 * dh: h * 3 * dh + dh] for h in range(nh)]
        qfs = [qf_ref[h, pl.ds(r0, tq), :] for h in range(nh)]
        segq = segc_ref[pl.ds(r0, tq), :]
        def k_body(j, acc):
            c0 = pl.multiple_of(j * tk, tk)
            same = segq == segr_ref[:, pl.ds(c0, tk)]
            new = []
            for h in range(nh):
                k = qkv_ref[pl.ds(c0, tk), h * 3 * dh + dh: h * 3 * dh + 2 * dh]
                s = dot(qs[h], k, ((1,), (1,)))
                e = jnp.exp2(s * (LOG2E * dh ** -0.5))
                a = dot(qfs[h], kf_ref[h, pl.ds(c0, tk), :], ((1,), (1,)))
                parts = []
                for b in range(tq // BLK):
                    hit = hit_ref[h, pl.ds(i * (tq // BLK) + b, 1), pl.ds(c0, tk)] > 0.5
                    rs = slice(b * BLK, (b + 1) * BLK)
                    parts.append(jnp.where(jnp.broadcast_to(hit, (BLK, tk)), e[rs], a[rs]))
                comb = jnp.where(same, jnp.concatenate(parts, axis=0), 0.0).astype(jnp.bfloat16)
                new.append(acc[h] + dot(comb, vext[h, pl.ds(c0, tk), :], ((1,), (0,))))
            return tuple(new)
        def k_step(j, acc):
            return lax.cond(meets(seg_s, r0, tq, pl.multiple_of(j * tk, tk), tk), lambda a: k_body(j, a), lambda a: a, acc)
        acc = lax.fori_loop(0, length // tk, k_step, tuple(jnp.zeros((tq, 2 * dh), jnp.float32) for _ in range(nh)))
        for h in range(nh):
            rinv = 1.0 / acc[h][:, dh:dh + 1]
            out_ref[pl.ds(r0, tq), h * dh:(h + 1) * dh] = (acc[h][:, :dh] * rinv).astype(jnp.bfloat16)
            rinv_ref[h, pl.ds(r0, tq), :] = rinv
        return 0
    lax.fori_loop(0, length // tq, q_body, 0)

def attn_fwd(at, n1, pieces, part, seg, hit, proj, ahead=(), *, tq=512, tk=256):
    length, width = n1.shape
    dh, feats = proj.shape
    cols = pieces[0].shape[2]
    heads = cols // (3 * dh)
    seg2 = seg.reshape(1, length)
    smem = pl.BlockSpec(memory_space=pltpu.SMEM)
    vmem = pl.BlockSpec(memory_space=pltpu.VMEM)
    anywhere = pl.BlockSpec(memory_space=pl.ANY)
    return pl.pallas_call(
        partial(fwd_kernel, tq=tq, tk=tk, dh=dh, part=part),
        in_specs=[smem] * 2 + [vmem] * 5 + [anywhere] * (4 + len(ahead)),
        out_specs=[vmem] * 6,
        out_shape=[
            jax.ShapeDtypeStruct((length, heads * dh), jnp.bfloat16),
            jax.ShapeDtypeStruct((heads, length, feats), jnp.bfloat16),
            jax.ShapeDtypeStruct((heads, length, feats), jnp.bfloat16),
            jax.ShapeDtypeStruct((heads, length, 1), jnp.float32),
            jax.ShapeDtypeStruct((length, cols), jnp.bfloat16),
            jax.ShapeDtypeStruct((4, width // 4, cols), jnp.bfloat16),
        ],
        scratch_shapes=[pltpu.VMEM((heads, length, 2 * dh), jnp.bfloat16), pltpu.SemaphoreType.DMA((4,))],
        compiler_params=pltpu.CompilerParams(vmem_limit_bytes=48 * 1024 * 1024),
        cost_estimate=pl.CostEstimate(flops=27 * 10**9, bytes_accessed=10**7, transcendentals=10**6),
        name="attn_fwd",
    )(at, seg2, n1, seg.reshape(length, 1), seg2, hit, proj, *pieces, *ahead)


def bwd_kernel(seg_s, qkv_ref, segc_ref, segr_ref, hit_ref, proj_ref, pext_ref, qf_ref, kf_ref, rinv_ref, o_ref, do_ref, *rest, tq, tk, dh):
    dqkv_ref, vext, doext, dq, dk, dv, dqf, dkf = rest[-8:]
    length = qkv_ref.shape[0]
    quarter = dh ** (-0.25)
    nh = qkv_ref.shape[1] // (3 * dh)
    lane = lax.broadcasted_iota(jnp.int32, (length, dh), 1)
    for h in range(nh):
        base = h * 3 * dh
        v = qkv_ref[:, base + 2 * dh: base + 3 * dh]
        vext[h, :, :] = jnp.concatenate([v, (lane < 2).astype(jnp.bfloat16)], axis=1)
        d_o = do_ref[:, h * dh:(h + 1) * dh].astype(jnp.float32)
        o = o_ref[:, h * dh:(h + 1) * dh].astype(jnp.float32)
        rinv = rinv_ref[h]
        delta = -jnp.sum(d_o * o, axis=1, keepdims=True) * rinv
        high = delta.astype(jnp.bfloat16).astype(jnp.float32)
        low = delta - high
        tail = jnp.where(lane == 0, high, jnp.where(lane == 1, low, 0.0))
        doext[h, :, :] = jnp.concatenate([d_o * rinv, tail], axis=1).astype(jnp.bfloat16)
    dq[...] = jnp.zeros_like(dq)
    dk[...] = jnp.zeros_like(dk)
    dv[...] = jnp.zeros_like(dv)
    dqf[...] = jnp.zeros_like(dqf)
    dkf[...] = jnp.zeros_like(dkf)

    def q_body(i, _):
        r0 = pl.multiple_of(i * tq, tq)
        rows = pl.ds(r0, tq)
        segq = segc_ref[rows, :]
        def k_body(j, _):
            c0 = pl.multiple_of(j * tk, tk)
            cols = pl.ds(c0, tk)
            same = segq == segr_ref[:, cols]
            for h in range(nh):
                base = h * 3 * dh
                q = qkv_ref[rows, base: base + dh]
                k = qkv_ref[cols, base + dh: base + 2 * dh]
                qf = qf_ref[h, rows, :]
                kf = kf_ref[h, cols, :]
                s = dot(q, k, ((1,), (1,)))
                e = jnp.exp2(s * (LOG2E * dh ** -0.5))
                a = dot(qf, kf, ((1,), (1,)))
                dc = dot(doext[h, rows, :], vext[h, cols, :], ((1,), (1,)))
                dc = jnp.where(same, dc, 0.0)
                combs, dss, das = [], [], []
                for b in range(tq // BLK):
                    hit = hit_ref[h, pl.ds(i * (tq // BLK) + b, 1), cols] > 0.5
                    hit = jnp.broadcast_to(hit, (BLK, tk))
                    rs = slice(b * BLK, (b + 1) * BLK)
                    combs.append(jnp.where(hit, e[rs], a[rs]))
                    dss.append(jnp.where(hit, dc[rs] * e[rs], 0.0))
                    das.append(jnp.where(hit, 0.0, dc[rs]))
                comb = jnp.where(same, jnp.concatenate(combs, axis=0), 0.0).astype(jnp.bfloat16)
                ds = jnp.concatenate(dss, axis=0).astype(jnp.bfloat16)
                da = jnp.concatenate(das, axis=0).astype(jnp.bfloat16)
                dq[h, rows, :] += dot(ds, k, ((1,), (0,)))
                dqf[h, rows, :] += dot(da, kf, ((1,), (0,)))
                dk[h, cols, :] += dot(ds, q, ((0,), (0,)))
                dkf[h, cols, :] += dot(da, qf, ((0,), (0,)))
                dv[h, cols, :] += dot(comb, doext[h, rows, :dh], ((0,), (0,)))
            return 0
        def k_step(j, _):
            @pl.when(meets(seg_s, r0, tq, pl.multiple_of(j * tk, tk), tk))
            def _():
                k_body(j, 0)
            return 0
        lax.fori_loop(0, length // tk, k_step, 0)
        return 0
    lax.fori_loop(0, length // tq, q_body, 0)

    for h in range(nh):
        base = h * 3 * dh
        for j, dt, dfeat, f_ref in ((0, dq, dqf, qf_ref), (1, dk, dkf, kf_ref)):
            def back(i, _, base=base, j=j, dt=dt, dfeat=dfeat, f_ref=f_ref, h=h):
                rows = pl.ds(pl.multiple_of(i * 256, 256), 256)
                dpre = dfeat[h, rows, :] * f_ref[h, rows, :].astype(jnp.float32)
                hi_ = dpre.astype(jnp.bfloat16)
                lo_ = (dpre - hi_.astype(jnp.float32)).astype(jnp.bfloat16)
                thr = dot(hi_, pext_ref[...], ((1,), (0,))) + dot(lo_, pext_ref[...], ((1,), (0,)))
                t = qkv_ref[rows, base + j * dh: base + (j + 1) * dh].astype(jnp.float32)
                g = dt[h, rows, :] * dh ** -0.5 + quarter * thr[:, :dh] - (quarter * quarter) * t * thr[:, dh:dh + 1]
                dqkv_ref[rows, base + j * dh: base + (j + 1) * dh] = g.astype(jnp.bfloat16)
                return 0
            lax.fori_loop(0, length // 256, back, 0)
        dqkv_ref[:, base + 2 * dh: base + 3 * dh] = dv[h].astype(jnp.bfloat16)

def attn_bwd(qkv, seg, hit, proj, qf, kf, rinv, o, d_o, ahead=(), *, tq=512, tk=256):
    length = qkv.shape[0]
    dh, feats = proj.shape
    heads = qkv.shape[1] // (3 * dh)
    seg2 = seg.reshape(1, length)
    pext = jnp.concatenate([proj.T, jnp.ones((feats, 1), proj.dtype), jnp.zeros((feats, dh - 1), proj.dtype)], axis=1)
    f32 = jnp.float32
    vmem = pl.BlockSpec(memory_space=pltpu.VMEM)
    return pl.pallas_call(
        partial(bwd_kernel, tq=tq, tk=tk, dh=dh),
        in_specs=[pl.BlockSpec(memory_space=pltpu.SMEM)] + [vmem] * 11 + [pl.BlockSpec(memory_space=pl.ANY)] * len(ahead),
        out_specs=vmem,
        out_shape=jax.ShapeDtypeStruct((length, heads * 3 * dh), jnp.bfloat16),
        scratch_shapes=[
            pltpu.VMEM((heads, length, 2 * dh), jnp.bfloat16),
            pltpu.VMEM((heads, length, 2 * dh), jnp.bfloat16),
            pltpu.VMEM((heads, length, dh), f32),
            pltpu.VMEM((heads, length, dh), f32),
            pltpu.VMEM((heads, length, dh), f32),
            pltpu.VMEM((heads, length, feats), f32),
            pltpu.VMEM((heads, length, feats), f32),
        ],
        compiler_params=pltpu.CompilerParams(vmem_limit_bytes=52 * 1024 * 1024),
        cost_estimate=pl.CostEstimate(flops=38 * 10**9, bytes_accessed=2 * 10**7, transcendentals=10**6),
        name="attn_bwd",
    )(seg2, qkv, seg.reshape(length, 1), seg2, hit, proj, pext, qf, kf, rinv, o, d_o, *ahead)


def hit_lanes(lists, length):
    nb = lists.shape[1]
    ids = lax.broadcasted_iota(jnp.int32, (1, 1, length), 2) // BLK
    out = lists[:, :, 0:1] == ids
    for s in range(1, lists.shape[2]):
        out = out | (lists[:, :, s:s + 1] == ids)
    return out.astype(jnp.float32)

from jax.sharding import PartitionSpec as P


def gelu_pair(u):
    mag = jnp.abs(u)
    t = 1.0 / (1.0 + (0.3275911 * 0.7071067811865476) * mag)
    bell = jnp.exp2(u * u * (-0.5 * LOG2E))
    poly = t * (0.127414796 + t * (-0.142248368 + t * (0.7107068705 + t * (-0.7265760135 + t * 0.5307027145))))
    tail = poly * bell
    cdf = jnp.where(u >= 0.0, 1.0 - tail, tail)
    return u * cdf, cdf + u * bell * 0.3989422804014327


def mlp_kernel(n_ref, dy_ref, up_ref, down_ref, act_ref, dpre_ref, own_ref, oth_ref, acc, *, tile, rows):
    x = pl.program_id(0)
    tokens, width = n_ref.shape
    hid = act_ref.shape[1]
    up = up_ref[...].reshape(width, hid)
    down = down_ref[...].reshape(hid, width)
    for j in range(hid // tile):
        up_t = up[:, j * tile:(j + 1) * tile]
        down_t = down[j * tile:(j + 1) * tile, :]
        def body(i, _, j=j, up_t=up_t, down_t=down_t):
            rs = pl.ds(pl.multiple_of(i * rows, rows), rows)
            pre = dot(n_ref[rs, :], up_t, ((1,), (0,)))
            d_act = dot(dy_ref[rs, :], down_t, ((1,), (1,)))
            act, slope = gelu_pair(pre)
            d_pre = (d_act * slope).astype(jnp.bfloat16)
            act_ref[rs, j * tile:(j + 1) * tile] = act.astype(jnp.bfloat16)
            dpre_ref[rs, j * tile:(j + 1) * tile] = d_pre
            part = dot(d_pre, up_t, ((1,), (1,)))
            if j == 0:
                @pl.when(x == 0)
                def _():
                    acc[rs, :] = part
                @pl.when(x > 0)
                def _():
                    acc[rs, :] += part
            else:
                acc[rs, :] += part
            return 0
        lax.fori_loop(0, tokens // rows, body, 0)

    @pl.when(x == pl.num_programs(0) - 1)
    def _():
        own_ref[...] = acc[:tokens // 2, :]
        oth_ref[...] = acc[tokens // 2:, :].astype(jnp.bfloat16)


def mlp_first(n2, dy, pack, piece, *, tile=256, rows=256):
    tokens, width = n2.shape
    cuts, parts = pack.shape[0], pack.shape[1]
    hid = cuts * piece
    half = tokens // 2
    bf16, f32 = jnp.bfloat16, jnp.float32
    whole = pl.BlockSpec((tokens, width), lambda x: (0, 0))
    return pl.pallas_call(
        partial(mlp_kernel, tile=tile, rows=rows),
        grid=(parts,),
        in_specs=[
            whole,
            whole,
            pl.BlockSpec((cuts, 1, piece, width), lambda x: (0, x, 0, 0)),
            pl.BlockSpec((cuts, 1, piece, width), lambda x: (0, x, 1, 0)),
        ],
        out_specs=[
            pl.BlockSpec((tokens, hid), lambda x: (0, x)),
            pl.BlockSpec((tokens, hid), lambda x: (0, x)),
            pl.BlockSpec((half, width), lambda x: (0, 0)),
            pl.BlockSpec((half, width), lambda x: (0, 0)),
        ],
        out_shape=[
            jax.ShapeDtypeStruct((tokens, parts * hid), bf16),
            jax.ShapeDtypeStruct((tokens, parts * hid), bf16),
            jax.ShapeDtypeStruct((half, width), f32),
            jax.ShapeDtypeStruct((half, width), bf16),
        ],
        scratch_shapes=[pltpu.VMEM((tokens, width), f32)],
        compiler_params=pltpu.CompilerParams(vmem_limit_bytes=48 * 1024 * 1024),
        cost_estimate=pl.CostEstimate(flops=25 * 10**9, bytes_accessed=2 * 10**7, transcendentals=3 * 10**6),
        name="mlp_first",
    )(n2, dy, pack, pack)


def mlp_grad_kernel(n_ref, dy_ref, act_ref, dpre_ref, down_ref, own_ref, oth_ref, grad_ref, acc, *, tile, piece):
    x = pl.program_id(0)
    tokens, width = n_ref.shape
    hid = act_ref.shape[1]
    half = tokens // 2
    down = down_ref[...].reshape(hid, width)
    tn = ((0,), (0,))
    def out_rows(i, _):
        rs = pl.ds(pl.multiple_of(i * tile, tile), tile)
        part = dot(act_ref[rs, :], down, ((1,), (0,)))
        @pl.when(x == 0)
        def _():
            acc[rs, :] = part
        @pl.when(x > 0)
        def _():
            acc[rs, :] += part
        return 0
    lax.fori_loop(0, tokens // tile, out_rows, 0)
    for j in range(width // (4 * piece)):
        cut = slice(4 * j * piece, 4 * (j + 1) * piece)
        up_g = dot(n_ref[:, cut], dpre_ref[...], tn).astype(jnp.bfloat16)
        grad_ref[2 * j:2 * j + 2, :, 0, :piece, :] = up_g.reshape(2, 2, piece, hid)
        down_g = dot(act_ref[:, cut], dy_ref[...], tn).astype(jnp.bfloat16)
        grad_ref[2 * j:2 * j + 2, :, 0, piece:2 * piece, :] = down_g.reshape(2, 2, piece, width)

    @pl.when(x == pl.num_programs(0) - 1)
    def _():
        own_ref[...] = acc[:half, :]
        oth_ref[...] = acc[half:, :].astype(jnp.bfloat16)


def mlp_second(n2, dy, acted, d_pre, pack, piece, *, tile=256):
    tokens, width = n2.shape
    cuts, parts = pack.shape[0], pack.shape[1]
    hid = cuts * piece
    half = tokens // 2
    bf16, f32 = jnp.bfloat16, jnp.float32
    whole = pl.BlockSpec((tokens, width), lambda x: (0, 0))
    cols = pl.BlockSpec((tokens, hid), lambda x: (0, x))
    side = pl.BlockSpec((half, width), lambda x: (0, 0))
    return pl.pallas_call(
        partial(mlp_grad_kernel, tile=tile, piece=piece),
        grid=(parts,),
        in_specs=[whole, whole, cols, cols, pl.BlockSpec((cuts, 1, piece, width), lambda x: (0, x, 1, 0))],
        out_specs=[side, side, pl.BlockSpec((4, 2, 1, 2 * piece, width), lambda x: (0, 0, x, 0, 0))],
        out_shape=[
            jax.ShapeDtypeStruct((half, width), f32),
            jax.ShapeDtypeStruct((half, width), bf16),
            jax.ShapeDtypeStruct((4, 2, parts, 2 * piece, width), bf16),
        ],
        scratch_shapes=[pltpu.VMEM((tokens, width), f32)],
        compiler_params=pltpu.CompilerParams(vmem_limit_bytes=48 * 1024 * 1024),
        cost_estimate=pl.CostEstimate(flops=17 * 10**9, bytes_accessed=2 * 10**7, transcendentals=0),
        name="mlp_second",
    )(n2, dy, acted, d_pre, pack)


norm_eps = 1e-05


def norm_rows(values):
    center = values - jnp.mean(values, axis=1, keepdims=True)
    scale = lax.rsqrt(jnp.mean(center * center, axis=1, keepdims=True) + norm_eps)
    return center * scale, scale


def norm_back(grad, xhat, scale, gain):
    dx = grad * gain
    return scale * (
        dx - jnp.mean(dx, axis=1, keepdims=True) - xhat * jnp.mean(dx * xhat, axis=1, keepdims=True)
    )


def own_group(i):
    return (i & 3) // 2 == (i >> 2) & 1


def far_group(i):
    return not own_group(i)


def shards(
    activations, segment_ids, block_lists, feature_proj, input_norm_gain, input_norm_bias, qkv_weight,
    out_weight, middle_norm_gain, middle_norm_bias, up_weight, down_weight, out_grad,
):
    rows_n, heads_n = lax.axis_size("row"), lax.axis_size("head")
    total = rows_n * heads_n
    r, z = lax.axis_index("row"), lax.axis_index("head")
    c, p = r % 2, (r // 2) % 4
    groups = rows_n // 8
    pairs = [[2 * i, 2 * i + 1] for i in range(rows_n // 2)]
    planes = [[8 * g + i for i in range(8)] for g in range(groups)]
    quads = [[8 * g + 2 * i + k for i in range(4)] for g in range(groups) for k in range(2)]
    width = input_norm_gain.shape[0]
    quarter = width // heads_n
    seq_count, length = segment_ids.shape
    half = length // 2
    lists_here = block_lists.shape[1]
    bf16, f32 = jnp.bfloat16, jnp.float32
    nn, nt, tn = ((1,), (0,)), ((1,), (1,)), ((0,), (0,))
    local = (z // 2) == c
    par = z % 2

    def move(v, mask, only=None):
        moves = [(i, i ^ mask) for i in range(total) if only is None or only(i)]
        return lax.ppermute(v, ("row", "head"), moves)

    def later(i, dep):
        one = dep.reshape(-1)[0]
        return i + (one != one).astype(jnp.int32)

    def deal_z(v):
        return lax.all_to_all(v, "head", 0, 0, tiled=True)

    def tied(v, dep):
        one = dep.reshape(-1)[0]
        return v + (one != one).astype(v.dtype)

    def deal(v, side):
        v = v.T

        def token_half(k):
            return jnp.stack([lax.dynamic_slice_in_dim(v, s * length + k * half, half, 1) for s in range(seq_count)])

        keep, got = token_half(side), move(token_half(1 - side), 4)
        return jnp.concatenate([jnp.where(side == 0, keep, got), jnp.where(side == 0, got, keep)], 0)

    def collect(v):
        v = v.reshape(2, seq_count, quarter, half)
        keep = lax.dynamic_index_in_dim(v, c, 0, keepdims=False)
        got = move(lax.dynamic_index_in_dim(v, 1 - c, 0, keepdims=False), 4)
        low, high = jnp.where(c == 0, keep, got), jnp.where(c == 0, got, keep)
        return jnp.concatenate([w[s] for s in range(seq_count) for w in (low, high)], 1).T

    def fetch_z(mine):
        return [mine] + [move(mine, d, own_group) for d in (1, 2, 3)]

    def choose(got, here):
        return jnp.stack([jnp.where(here, got[0], got[2]), jnp.where(here, got[1], got[3])])

    def fetch_plane(both):
        return [both] + [move(both, 8 * d) for d in (1, 2, 3)]

    def give_z(same, other):
        fin = same.astype(f32) + move(other, 1, own_group).astype(f32)
        fin = fin + move(same, 2, far_group).astype(f32) + move(other, 3, far_group).astype(f32)
        if groups > 1:
            fin = lax.psum(fin, "row", axis_index_groups=[[8 * g + i for g in range(groups)] for i in range(8)])
        fin = fin.astype(bf16)
        fin = jnp.where(local, fin, move(fin, 4))
        n = fin.shape[0] // 2
        return lax.dynamic_slice_in_dim(fin, c * n, n, 0)

    def gather_plane(v):
        return lax.all_gather(v, "row", axis=0, axis_index_groups=planes)

    cut = lambda w, n, at: lax.dynamic_slice_in_dim(w, at * n, n, 0)

    aux = jnp.concatenate([block_lists.reshape(seq_count, -1), segment_ids], 1).astype(bf16)
    aux_got = move(aux, 4)
    aux = jnp.where(c == 0, jnp.concatenate([aux, aux_got], 0), jnp.concatenate([aux_got, aux], 0))
    n_list = aux.shape[1] - length
    seg = lax.dynamic_index_in_dim(aux[:, n_list:], z, 0, keepdims=False).astype(jnp.int32)

    x_half = deal_z(deal(activations, c)).reshape(width, half).T
    x = x_half.astype(f32)

    n_qkv, n_hid, n_out = width // 4, down_weight.shape[0] // 8, out_weight.shape[0] // 8
    cols = qkv_weight.shape[1]
    extra = 16
    rider = aux[:, :n_list].reshape(-1)
    rider = jnp.pad(rider, (0, extra * cols - rider.shape[0])).reshape(extra, cols)
    both = choose(fetch_z(jnp.concatenate([cut(qkv_weight, n_qkv, p), rider], 0)), local)
    lists = both[:, n_qkv:].reshape(2, -1)[:, :4 * n_list].reshape(2, 4, n_list).astype(jnp.int32)
    lists = lax.dynamic_index_in_dim(lists, z, 1, keepdims=False).reshape((2, lists_here) + block_lists.shape[2:])
    wq_pieces = fetch_plane(both[:, :n_qkv])
    at = jnp.full((1,), p, jnp.int32)

    q8 = r % 8
    n_up = width // 8
    mine = jnp.concatenate([cut(up_weight, n_up, q8), cut(down_weight, n_hid, q8), cut(out_weight, n_out, q8)], 0)
    pack = lax.all_gather(mine, "head", axis=0)
    pack = jnp.broadcast_to(pack.reshape((1, 2, 2) + mine.shape), (4, 2, 2) + mine.shape).reshape((8, 2) + mine.shape)
    pack_send = pack
    pack = lax.all_to_all(pack, "row", 0, 0, axis_index_groups=planes, tiled=True)
    dy_four = deal(out_grad, later(c, x_half))
    dy_half = jnp.zeros((heads_n, quarter, half), bf16)
    for d in range(heads_n):
        part = lax.dynamic_index_in_dim(dy_four, z ^ d, 0, keepdims=False)
        dy_half = lax.dynamic_update_index_in_dim(dy_half, move(part, d) if d else part, z ^ d, 0)
    dy_half = dy_half.reshape(width, half).T

    shift = c * half
    seg = lax.dynamic_slice_in_dim(jnp.concatenate([seg, seg]), shift, length, 0)
    hits = []
    for own in lists:
        own = lax.dynamic_slice_in_dim(jnp.concatenate([own, own], 1), shift // BLK, length // BLK, 1)
        hit = hit_lanes(own, length)
        hits.append(lax.dynamic_slice_in_dim(jnp.concatenate([hit, hit], 2), shift, length, 2))

    def mm(a, b, dims):
        return lax.dot_general(a, b, (dims, ((), ())), preferred_element_type=f32)

    xhat1, scale1 = norm_rows(x)
    n1_half = (xhat1 * input_norm_gain + input_norm_bias).astype(bf16)
    n1 = jnp.concatenate([n1_half, move(n1_half, 4)], 0)
    att = []
    for i in range(2):
        att.append(attn_fwd(at, n1, wq_pieces, i, seg, hits[i], feature_proj, (pack_send, dy_half) if i else ()))
    qkv = [v[4] for v in att]
    wq = [v[5].reshape(width, -1) for v in att]
    outs = pack[:, :, n_up + n_hid:].transpose(1, 0, 2, 3).reshape(2, -1, width)
    outw = [lax.dynamic_index_in_dim(outs, i, 0, keepdims=False) for i in (par, 1 - par)]
    heads_out = [v[0] for v in att]

    away = (mm(heads_out[0][half:], outw[0], nn) + mm(heads_out[1][half:], outw[1], nn)).astype(bf16)
    near = mm(heads_out[0][:half], outw[0], nn) + mm(heads_out[1][:half], outw[1], nn)
    resid = x + near + move(away, 4).astype(f32)
    xhat2, scale2 = norm_rows(resid.astype(bf16).astype(f32))
    n2_half = (xhat2 * middle_norm_gain + middle_norm_bias).astype(bf16)
    n2 = jnp.concatenate([n2_half, move(n2_half, 4)], 0)
    dy = jnp.concatenate([dy_half, move(dy_half, 4)], 0)
    acted, d_pre, dn_own, dn_oth = mlp_first(n2, dy, pack, n_hid)
    d_n2 = dn_own + move(dn_oth, 4).astype(f32)
    mo_own, mo_oth, grads = mlp_second(n2, dy, acted, d_pre, pack, n_hid)
    block_half = (resid + mo_own + move(mo_oth, 4).astype(f32)).astype(bf16)
    block_got = deal_z(block_half.T.reshape(heads_n, quarter, half))
    block_out = collect(block_got)
    d_resid = dy_half.astype(f32) + norm_back(d_n2, xhat2, scale2, middle_norm_gain)
    d_half = d_resid.astype(bf16)
    d_branch = jnp.concatenate([d_half, move(d_half, 4)], 0)
    grads = lax.psum_scatter(
        grads.reshape(-1, width), "row", scatter_dimension=0, axis_index_groups=quads, tiled=True
    ).reshape(2, 2, -1, width)
    keep = lax.dynamic_index_in_dim(grads, c, 0, keepdims=False)
    got = move(lax.dynamic_index_in_dim(grads, 1 - c, 0, keepdims=False), 4)
    four = jnp.concatenate([jnp.where(c == 0, keep, got), jnp.where(c == 0, got, keep)], 0)
    four_flat = four.reshape(-1, width)
    mlp_slice = mlp_grads = lax.psum_scatter(four_flat, "head", scatter_dimension=0, tiled=True)
    if groups > 1:
        mlp_grads = lax.psum(mlp_grads, "row", axis_index_groups=[[8 * g + i for g in range(groups)] for i in range(8)])
    mlp_grads = gather_plane(mlp_grads)
    up_grad = mlp_grads[:, :n_up].reshape(width, -1).astype(f32)
    down_grad = mlp_grads[:, n_up:].reshape(-1, width).astype(f32)

    def sum_plane(v):
        v = lax.all_to_all(v, "row", 0, 0, axis_index_groups=quads, tiled=True)
        return jnp.sum(v.astype(f32), 0).astype(bf16)

    out_g = [mm(v, d_branch, tn).astype(bf16).reshape(4, -1, cols) for v in heads_out]
    n_outg = out_g[0].shape[1]
    d_qkv, qkv_g = [], []
    for i in range(2):
        d_heads = mm(d_branch, outw[i], nt).astype(bf16)
        ahead = (block_got, four_flat) if i else (mo_oth,)
        d_qkv.append(attn_bwd(qkv[i], seg, hits[i], feature_proj, *att[i][1:4], heads_out[i], d_heads, ahead))
        part = mm(n1, d_qkv[i], tn)
        if i:
            part = tied(tied(part, qkv_g[0]), mlp_slice)
        part = part.astype(bf16).reshape(4, n_qkv, -1)
        qkv_g.append(sum_plane(part if i else jnp.concatenate([part] + out_g, 1)))
    first, second = qkv_g
    second = tied(second, mlp_grads)
    qkv_g = [first[:n_qkv + n_outg], jnp.concatenate([second, first[n_qkv + n_outg:]], 0)]
    away = (mm(d_qkv[0][half:], wq[0], nt) + mm(d_qkv[1][half:], wq[1], nt)).astype(bf16)
    near = mm(d_qkv[0][:half], wq[0], nt) + mm(d_qkv[1][:half], wq[1], nt)
    d_n1 = near + move(away, 4).astype(f32)
    d_in = norm_back(d_n1, xhat1, scale1, input_norm_gain)
    vec = jnp.stack([jnp.sum(d_n1 * xhat1, 0), jnp.sum(d_n1, 0), jnp.sum(d_n2 * xhat2, 0), jnp.sum(d_n2, 0)])

    def split(v):
        high = v.astype(bf16)
        return jnp.concatenate([high, (v - high.astype(f32)).astype(bf16)], 0)

    ride = 128
    rider = jnp.pad(split(vec).reshape(8, heads_n, quarter).transpose(1, 2, 0), ((0, 0), (0, 0), (0, ride - 8)))
    send = (d_resid + d_in).astype(bf16).T.reshape(heads_n, quarter, half)
    got = deal_z(jnp.concatenate([send, rider], 2))
    input_grad = collect(got[:, :, :half]).astype(f32)
    vec = jnp.sum(got[:, :, half:half + 8].astype(f32), 0).T
    rider = split(vec[:4] + vec[4:]).reshape(-1)
    rider = jnp.pad(rider, (0, extra * cols - rider.shape[0])).reshape(extra, cols)
    got = gather_plane(jnp.concatenate([give_z(*qkv_g), rider], 0))
    n_half = got.shape[1] - extra
    both = got[:, :n_half].reshape(4, 2 * n_half, cols)
    qkv_grad = both[:, :n_qkv].reshape(width, -1).astype(f32)
    out_w_grad = both[:, n_qkv:].reshape(-1, width).astype(f32)
    vec = jnp.sum(got[:, n_half:].astype(f32), 0)
    vec = vec.reshape(-1)[:8 * quarter].reshape(2, 4, quarter)
    vec = vec[0] + vec[1]
    if groups > 1:
        vec = lax.psum(vec, "row", axis_index_groups=[[8 * g + i for g in range(groups)] for i in range(8)])
    return (
        block_out, input_grad, vec[0], vec[1], qkv_grad, out_w_grad, vec[2], vec[3], up_grad, down_grad,
    )


def solution(mesh):
    return jax.shard_map(
        shards,
        mesh=mesh,
        in_specs=(
            P("row", "head"), P("row", None), P("row", "head", None, None), P(), P(), P(), P(None, "head"),
            P("head", None), P(), P(), P(None, "head"), P("head", None), P("row", "head"),
        ),
        out_specs=(
            P("row", "head"), P("row", "head"), P("head"), P("head"), P(None, "head"), P("head", None),
            P("head"), P("head"), P(None, "head"), P("head", None),
        ),
        check_vma=False,
    )
```

```python
from functools import partial

import math
import jax, jax.numpy as jnp
from jax import lax
from jax.experimental import pallas as pl
from jax.experimental.pallas import tpu as pltpu

BLK = 64
LOG2E = 1.4426950408889634

def dot(a, b, dims):
    return lax.dot_general(a, b, (dims, ((), ())), preferred_element_type=jnp.float32)

def meets(seg_ref, r0, tq, c0, tk):
    return (seg_ref[0, r0] <= seg_ref[0, c0 + tk - 1]) & (seg_ref[0, c0] <= seg_ref[0, r0 + tq - 1])

def fwd_kernel(at_ref, seg_s, own_ref, oth_ref, segc_ref, segr_ref, hit_ref, proj_ref, *rest, tq, tk, dh, part):
    out_ref, qf_ref, kf_ref, rinv_ref, qkv_ref, w_ref, wo_ref, *sums, done_ref, vext, sems = rest[-(11 if part == 0 else 12):]
    done_ref[0] = 0
    cut = w_ref.shape[1]
    slots = [at_ref[0] ^ d for d in range(4)]
    copies = [
        pltpu.make_async_copy(piece.at[part, pl.ds(0, cut), :], w_ref.at[slots[d]], sems.at[0, d])
        for d, piece in enumerate(rest[:4])
    ] + [
        pltpu.make_async_copy(piece.at[part, pl.ds(cut, wo_ref.shape[1]), :], wo_ref.at[slots[d]], sems.at[1, d])
        for d, piece in enumerate(rest[:4])
    ]
    for copy in copies:
        copy.start()
    for copy in copies:
        copy.wait()
    weights = w_ref[...].reshape(qkv_ref.shape[1], own_ref.shape[1])
    for side, n_ref in enumerate((own_ref, oth_ref)):
        def project(i, _, base=side * own_ref.shape[0], n_ref=n_ref):
            r0 = pl.multiple_of(i * 256, 256)
            qkv_ref[pl.ds(base + r0, 256), :] = dot(n_ref[pl.ds(r0, 256), :], weights, ((1,), (1,))).astype(jnp.bfloat16)
            return 0

        lax.fori_loop(0, n_ref.shape[0] // 256, project, 0)
    length = qkv_ref.shape[0]
    feats = proj_ref.shape[1]
    quarter = dh ** (-0.25)
    nh = qkv_ref.shape[1] // (3 * dh)
    for h in range(nh):
        base = h * 3 * dh
        for j, f_ref in ((0, qf_ref), (1, kf_ref)):
            def feat_body(i, _, base=base, j=j, f_ref=f_ref, h=h):
                rows = pl.ds(pl.multiple_of(i * 256, 256), 256)
                t = qkv_ref[rows, base + j * dh: base + (j + 1) * dh]
                lin = dot(t, proj_ref[...], ((1,), (0,)))
                tw = t.astype(jnp.float32)
                sq = jnp.sum(tw * tw, axis=1, keepdims=True) * (0.5 * quarter * quarter * LOG2E) + 0.5 * math.log2(feats)
                f_ref[h, rows, :] = jnp.exp2(lin * (quarter * LOG2E) - sq).astype(jnp.bfloat16)
                return 0
            lax.fori_loop(0, length // 256, feat_body, 0)
        v = qkv_ref[:, base + 2 * dh: base + 3 * dh]
        lane = lax.broadcasted_iota(jnp.int32, (length, dh), 1)
        vext[h, :, :] = jnp.concatenate([v, (lane < 1).astype(jnp.bfloat16)], axis=1)

    def q_body(i, _):
        r0 = pl.multiple_of(i * tq, tq)
        qs = [qkv_ref[pl.ds(r0, tq), h * 3 * dh: h * 3 * dh + dh] for h in range(nh)]
        qfs = [qf_ref[h, pl.ds(r0, tq), :] for h in range(nh)]
        segq = segc_ref[pl.ds(r0, tq), :]
        def k_body(j, acc):
            c0 = pl.multiple_of(j * tk, tk)
            same = segq == segr_ref[:, pl.ds(c0, tk)]
            new = []
            for h in range(nh):
                k = qkv_ref[pl.ds(c0, tk), h * 3 * dh + dh: h * 3 * dh + 2 * dh]
                s = dot(qs[h], k, ((1,), (1,)))
                e = jnp.exp2(s * (LOG2E * dh ** -0.5))
                a = dot(qfs[h], kf_ref[h, pl.ds(c0, tk), :], ((1,), (1,)))
                parts = []
                for b in range(tq // BLK):
                    hit = hit_ref[h, pl.ds(i * (tq // BLK) + b, 1), pl.ds(c0, tk)] > 0.5
                    rs = slice(b * BLK, (b + 1) * BLK)
                    parts.append(jnp.where(jnp.broadcast_to(hit, (BLK, tk)), e[rs], a[rs]))
                comb = jnp.where(same, jnp.concatenate(parts, axis=0), 0.0).astype(jnp.bfloat16)
                new.append(acc[h] + dot(comb, vext[h, pl.ds(c0, tk), :], ((1,), (0,))))
            return tuple(new)
        def k_step(j, acc):
            return lax.cond(meets(seg_s, r0, tq, pl.multiple_of(j * tk, tk), tk), lambda a: k_body(j, a), lambda a: a, acc)
        acc = lax.fori_loop(0, length // tk, k_step, tuple(jnp.zeros((tq, 2 * dh), jnp.float32) for _ in range(nh)))
        for h in range(nh):
            rinv = 1.0 / acc[h][:, dh:dh + 1]
            out_ref[pl.ds(r0, tq), h * dh:(h + 1) * dh] = (acc[h][:, :dh] * rinv).astype(jnp.bfloat16)
            rinv_ref[h, pl.ds(r0, tq), :] = rinv
        return 0
    lax.fori_loop(0, length // tq, q_body, 0)

    w_out = wo_ref[...].reshape(out_ref.shape[1], own_ref.shape[1])
    add_parts(lambda rows: dot(out_ref[rows, :], w_out, ((1,), (0,))), None if part == 0 else rest[4], sums, length, part == 0)


def add_parts(product, before, sums, length, first):
    half = length // 2

    def body(i, _):
        rows = pl.ds(pl.multiple_of(i * 256, 256), 256)
        part = product(rows)
        if first:
            sums[0][rows, :] = part
        else:
            total = part + before[rows, :]
            @pl.when(i < half // 256)
            def _():
                sums[0][rows, :] = total
            @pl.when(i >= half // 256)
            def _():
                sums[1][pl.ds(pl.multiple_of(i * 256 - half, 256), 256), :] = total.astype(jnp.bfloat16)
        return 0

    lax.fori_loop(0, length // 256, body, 0)


def sum_shapes(length, width, first):
    whole = lambda n, dtype: jax.ShapeDtypeStruct((n, width), dtype)
    return [whole(length, jnp.float32)] if first else [whole(length // 2, jnp.float32), whole(length // 2, jnp.bfloat16)]


def attn_fwd(at, n_own, n_oth, pieces, part, seg, hit, proj, before=None, ahead=(), *, tq=512, tk=256):
    length, width = 2 * n_own.shape[0], n_own.shape[1]
    dh, feats = proj.shape
    heads = hit.shape[0]
    cols = 3 * heads * dh
    seg2 = seg.reshape(1, length)
    first = before is None
    smem = pl.BlockSpec(memory_space=pltpu.SMEM)
    vmem = pl.BlockSpec(memory_space=pltpu.VMEM)
    anywhere = pl.BlockSpec(memory_space=pltpu.HBM)
    return pl.pallas_call(
        partial(fwd_kernel, tq=tq, tk=tk, dh=dh, part=part),
        in_specs=[smem] * 2 + [vmem] * 6 + [anywhere] * 4 + [vmem] * (not first) + [anywhere] * len(ahead),
        out_specs=[vmem] * (8 if first else 9) + [smem],
        out_shape=[
            jax.ShapeDtypeStruct((length, heads * dh), jnp.bfloat16),
            jax.ShapeDtypeStruct((heads, length, feats), jnp.bfloat16),
            jax.ShapeDtypeStruct((heads, length, feats), jnp.bfloat16),
            jax.ShapeDtypeStruct((heads, length, 1), jnp.float32),
            jax.ShapeDtypeStruct((length, cols), jnp.bfloat16),
            jax.ShapeDtypeStruct((4, cols // 4, width), jnp.bfloat16),
            jax.ShapeDtypeStruct((4, heads * dh // 4, width), jnp.bfloat16),
        ]
        + sum_shapes(length, width, first)
        + [jax.ShapeDtypeStruct((1,), jnp.int32)],
        scratch_shapes=[pltpu.VMEM((heads, length, 2 * dh), jnp.bfloat16), pltpu.SemaphoreType.DMA((2, 4))],
        compiler_params=pltpu.CompilerParams(vmem_limit_bytes=48 * 1024 * 1024),
        cost_estimate=pl.CostEstimate(flops=27 * 10**9, bytes_accessed=10**7, transcendentals=10**6),
        name="attn_fwd",
    )(at, seg2, n_own, n_oth, seg.reshape(length, 1), seg2, hit, proj, *pieces, *(() if first else (before,)), *ahead)


def bwd_kernel(at_ref, seg_s, qkv_ref, segc_ref, segr_ref, hit_ref, proj_ref, pext_ref, qf_ref, kf_ref, rinv_ref, o_ref,
               d_own, d_oth, w_out, n_own, n_oth, w_ref, *rest, tq, tk, dh, first):
    *outs, done_ref, dqkv_ref, do_ref, grad_s, vext, doext, dq, dk, dv, dqf, dkf = rest[-(13 if first else 17):]
    sums = outs[1:] if first else outs[4:]
    done_ref[0] = 0
    length = qkv_ref.shape[0]
    half = length // 2
    quarter = dh ** (-0.25)
    nh = qkv_ref.shape[1] // (3 * dh)
    for side, d_ref in enumerate((d_own, d_oth)):
        do_ref[side * half:(side + 1) * half, :] = dot(d_ref[...], w_out[...], ((1,), (1,))).astype(jnp.bfloat16)
    lane = lax.broadcasted_iota(jnp.int32, (length, dh), 1)
    for h in range(nh):
        base = h * 3 * dh
        v = qkv_ref[:, base + 2 * dh: base + 3 * dh]
        vext[h, :, :] = jnp.concatenate([v, (lane < 2).astype(jnp.bfloat16)], axis=1)
        d_o = do_ref[:, h * dh:(h + 1) * dh].astype(jnp.float32)
        o = o_ref[:, h * dh:(h + 1) * dh].astype(jnp.float32)
        rinv = rinv_ref[h]
        delta = -jnp.sum(d_o * o, axis=1, keepdims=True) * rinv
        high = delta.astype(jnp.bfloat16).astype(jnp.float32)
        low = delta - high
        tail = jnp.where(lane == 0, high, jnp.where(lane == 1, low, 0.0))
        doext[h, :, :] = jnp.concatenate([d_o * rinv, tail], axis=1).astype(jnp.bfloat16)
    dq[...] = jnp.zeros_like(dq)
    dk[...] = jnp.zeros_like(dk)
    dv[...] = jnp.zeros_like(dv)
    dqf[...] = jnp.zeros_like(dqf)
    dkf[...] = jnp.zeros_like(dkf)

    def q_body(i, _):
        r0 = pl.multiple_of(i * tq, tq)
        rows = pl.ds(r0, tq)
        segq = segc_ref[rows, :]
        def k_body(j, _):
            c0 = pl.multiple_of(j * tk, tk)
            cols = pl.ds(c0, tk)
            same = segq == segr_ref[:, cols]
            for h in range(nh):
                base = h * 3 * dh
                q = qkv_ref[rows, base: base + dh]
                k = qkv_ref[cols, base + dh: base + 2 * dh]
                qf = qf_ref[h, rows, :]
                kf = kf_ref[h, cols, :]
                s = dot(q, k, ((1,), (1,)))
                e = jnp.exp2(s * (LOG2E * dh ** -0.5))
                a = dot(qf, kf, ((1,), (1,)))
                dc = dot(doext[h, rows, :], vext[h, cols, :], ((1,), (1,)))
                dc = jnp.where(same, dc, 0.0)
                combs, dss, das = [], [], []
                for b in range(tq // BLK):
                    hit = hit_ref[h, pl.ds(i * (tq // BLK) + b, 1), cols] > 0.5
                    hit = jnp.broadcast_to(hit, (BLK, tk))
                    rs = slice(b * BLK, (b + 1) * BLK)
                    combs.append(jnp.where(hit, e[rs], a[rs]))
                    dss.append(jnp.where(hit, dc[rs] * e[rs], 0.0))
                    das.append(jnp.where(hit, 0.0, dc[rs]))
                comb = jnp.where(same, jnp.concatenate(combs, axis=0), 0.0).astype(jnp.bfloat16)
                ds = jnp.concatenate(dss, axis=0).astype(jnp.bfloat16)
                da = jnp.concatenate(das, axis=0).astype(jnp.bfloat16)
                dq[h, rows, :] += dot(ds, k, ((1,), (0,)))
                dqf[h, rows, :] += dot(da, kf, ((1,), (0,)))
                dk[h, cols, :] += dot(ds, q, ((0,), (0,)))
                dkf[h, cols, :] += dot(da, qf, ((0,), (0,)))
                dv[h, cols, :] += dot(comb, doext[h, rows, :dh], ((0,), (0,)))
            return 0
        def k_step(j, _):
            @pl.when(meets(seg_s, r0, tq, pl.multiple_of(j * tk, tk), tk))
            def _():
                k_body(j, 0)
            return 0
        lax.fori_loop(0, length // tk, k_step, 0)
        return 0
    lax.fori_loop(0, length // tq, q_body, 0)

    for h in range(nh):
        base = h * 3 * dh
        for j, dt, dfeat, f_ref in ((0, dq, dqf, qf_ref), (1, dk, dkf, kf_ref)):
            def back(i, _, base=base, j=j, dt=dt, dfeat=dfeat, f_ref=f_ref, h=h):
                rows = pl.ds(pl.multiple_of(i * 256, 256), 256)
                dpre = dfeat[h, rows, :] * f_ref[h, rows, :].astype(jnp.float32)
                hi_ = dpre.astype(jnp.bfloat16)
                lo_ = (dpre - hi_.astype(jnp.float32)).astype(jnp.bfloat16)
                thr = dot(hi_, pext_ref[...], ((1,), (0,))) + dot(lo_, pext_ref[...], ((1,), (0,)))
                t = qkv_ref[rows, base + j * dh: base + (j + 1) * dh].astype(jnp.float32)
                g = dt[h, rows, :] * dh ** -0.5 + quarter * thr[:, :dh] - (quarter * quarter) * t * thr[:, dh:dh + 1]
                dqkv_ref[rows, base + j * dh: base + (j + 1) * dh] = g.astype(jnp.bfloat16)
                return 0
            lax.fori_loop(0, length // 256, back, 0)
        dqkv_ref[:, base + 2 * dh: base + 3 * dh] = dv[h].astype(jnp.bfloat16)

    weights = w_ref[...].reshape(qkv_ref.shape[1], n_own.shape[1])
    add_parts(lambda rows: dot(dqkv_ref[rows, :], weights, ((1,), (0,))), rest[0], sums, length, first)

    tn = ((0,), (0,))
    cut = w_ref.shape[1]
    grad = dot(dqkv_ref[:half, :], n_own[...], tn) + dot(dqkv_ref[half:, :], n_oth[...], tn)
    grad_s[:, :cut, :] = grad.astype(jnp.bfloat16).reshape(4, cut, n_own.shape[1])
    out = dot(o_ref[:half, :], d_own[...], tn) + dot(o_ref[half:, :], d_oth[...], tn)
    grad_s[:, cut:, :] = out.astype(jnp.bfloat16).reshape(4, o_ref.shape[1] // 4, n_own.shape[1])
    if first:
        outs[0][...] = grad_s[...]
    else:
        for d in range(4):
            outs[d][...] = grad_s[at_ref[0] ^ d]


def attn_bwd(at, qkv, seg, hit, proj, qf, kf, rinv, o, d_own, d_oth, w_out, n_own, n_oth, wq, before=None, ahead=(), *, tq=512, tk=256):
    length = qkv.shape[0]
    dh, feats = proj.shape
    width = n_own.shape[1]
    heads = qkv.shape[1] // (3 * dh)
    seg2 = seg.reshape(1, length)
    pext = jnp.concatenate([proj.T, jnp.ones((feats, 1), proj.dtype), jnp.zeros((feats, dh - 1), proj.dtype)], axis=1)
    f32, bf16 = jnp.float32, jnp.bfloat16
    smem = pl.BlockSpec(memory_space=pltpu.SMEM)
    vmem = pl.BlockSpec(memory_space=pltpu.VMEM)
    anywhere = pl.BlockSpec(memory_space=pltpu.HBM)
    first = before is None
    piece = jax.ShapeDtypeStruct(((qkv.shape[1] + o.shape[1]) // 4, width), bf16)
    return pl.pallas_call(
        partial(bwd_kernel, tq=tq, tk=tk, dh=dh, first=first),
        in_specs=[smem] * 2 + [vmem] * (16 if first else 17) + [anywhere] * len(ahead),
        out_specs=[vmem] * (2 if first else 6) + [smem],
        out_shape=([jax.ShapeDtypeStruct((4,) + piece.shape, bf16)] if first else [piece] * 4) + sum_shapes(length, width, first)
        + [jax.ShapeDtypeStruct((1,), jnp.int32)],
        scratch_shapes=[
            pltpu.VMEM(qkv.shape, bf16),
            pltpu.VMEM(o.shape, bf16),
            pltpu.VMEM((4,) + piece.shape, bf16),
            pltpu.VMEM((heads, length, 2 * dh), bf16),
            pltpu.VMEM((heads, length, 2 * dh), bf16),
            pltpu.VMEM((heads, length, dh), f32),
            pltpu.VMEM((heads, length, dh), f32),
            pltpu.VMEM((heads, length, dh), f32),
            pltpu.VMEM((heads, length, feats), f32),
            pltpu.VMEM((heads, length, feats), f32),
        ],
        compiler_params=pltpu.CompilerParams(vmem_limit_bytes=56 * 1024 * 1024),
        cost_estimate=pl.CostEstimate(flops=42 * 10**9, bytes_accessed=2 * 10**7, transcendentals=10**6),
        name="attn_bwd",
    )(at, seg2, qkv, seg.reshape(length, 1), seg2, hit, proj, pext, qf, kf, rinv, o, d_own, d_oth, w_out, n_own, n_oth, wq,
      *(() if first else (before,)), *ahead)


def hit_lanes(lists, length):
    nb = lists.shape[1]
    ids = lax.broadcasted_iota(jnp.int32, (1, 1, length), 2) // BLK
    out = lists[:, :, 0:1] == ids
    for s in range(1, lists.shape[2]):
        out = out | (lists[:, :, s:s + 1] == ids)
    return out.astype(jnp.float32)

from jax.sharding import PartitionSpec as P


def gelu_pair(u):
    mag = jnp.abs(u)
    t = 1.0 / (1.0 + (0.3275911 * 0.7071067811865476) * mag)
    bell = jnp.exp2(u * u * (-0.5 * LOG2E))
    poly = t * (0.127414796 + t * (-0.142248368 + t * (0.7107068705 + t * (-0.7265760135 + t * 0.5307027145))))
    tail = poly * bell
    cdf = jnp.where(u >= 0.0, 1.0 - tail, tail)
    return u * cdf, cdf + u * bell * 0.3989422804014327


def mlp_kernel(n_own, n_oth, dy_own, dy_oth, w_ref, *rest, tile, rows, first):
    act_ref, dpre_ref, *sums, acc = rest[-(4 if first else 5):]
    half, width = n_own.shape
    piece = w_ref.shape[1] // 2
    hid = act_ref.shape[1]
    up = w_ref[:, :piece, :].reshape(width, hid)
    down = w_ref[:, piece:, :].reshape(hid, width)
    for j in range(hid // tile):
        up_t = up[:, j * tile:(j + 1) * tile]
        down_t = down[j * tile:(j + 1) * tile, :]
        for side, (n_ref, dy_ref) in enumerate(((n_own, dy_own), (n_oth, dy_oth))):
            def body(i, _, j=j, up_t=up_t, down_t=down_t, n_ref=n_ref, dy_ref=dy_ref, base=side * half):
                r0 = pl.multiple_of(i * rows, rows)
                src = pl.ds(r0, rows)
                rs = pl.ds(base + r0, rows)
                pre = dot(n_ref[src, :], up_t, ((1,), (0,)))
                d_act = dot(dy_ref[src, :], down_t, ((1,), (1,)))
                act, slope = gelu_pair(pre)
                d_pre = (d_act * slope).astype(jnp.bfloat16)
                act_ref[rs, j * tile:(j + 1) * tile] = act.astype(jnp.bfloat16)
                dpre_ref[rs, j * tile:(j + 1) * tile] = d_pre
                part = dot(d_pre, up_t, ((1,), (1,)))
                if j == 0 and first:
                    acc[rs, :] = part
                elif j == 0:
                    acc[rs, :] = part + rest[0][rs, :]
                else:
                    acc[rs, :] += part
                return 0
            lax.fori_loop(0, half // rows, body, 0)
    if first:
        sums[0][...] = acc[...]
    else:
        sums[0][...] = acc[:half, :]
        sums[1][...] = acc[half:, :].astype(jnp.bfloat16)


def mlp_first(n2, dy, pack, before=None, ahead=(), *, tile=256, rows=256):
    tokens, width = 2 * n2[0].shape[0], n2[0].shape[1]
    hid = pack.shape[0] * pack.shape[1] // 2
    bf16, f32 = jnp.bfloat16, jnp.float32
    first = before is None
    vmem = pl.BlockSpec(memory_space=pltpu.VMEM)
    return pl.pallas_call(
        partial(mlp_kernel, tile=tile, rows=rows, first=first),
        in_specs=[vmem] * (5 if first else 6) + [pl.BlockSpec(memory_space=pltpu.HBM)] * len(ahead),
        out_specs=[vmem] * (3 if first else 4),
        out_shape=[jax.ShapeDtypeStruct((tokens, hid), bf16)] * 2 + sum_shapes(tokens, width, first),
        scratch_shapes=[pltpu.VMEM((tokens, width), f32)],
        compiler_params=pltpu.CompilerParams(vmem_limit_bytes=48 * 1024 * 1024),
        cost_estimate=pl.CostEstimate(flops=12 * 10**9, bytes_accessed=2 * 10**7, transcendentals=10**6),
        name="mlp_first",
    )(*n2, *dy, pack, *(() if first else (before,)), *ahead)


def mlp_grad_kernel(n_own, n_oth, dy_own, dy_oth, act_ref, dpre_ref, w_ref, *rest, first):
    *sums, grad_ref = rest[-(2 if first else 3):]
    half, width = n_own.shape
    piece = w_ref.shape[1] // 2
    hid = act_ref.shape[1]
    down = w_ref[:, piece:, :].reshape(hid, width)
    tn = ((0,), (0,))
    add_parts(lambda rs: dot(act_ref[rs, :], down, ((1,), (0,))), None if first else rest[0], sums, 2 * half, first)
    for j in range(width // (4 * piece)):
        cut = slice(4 * j * piece, 4 * (j + 1) * piece)
        up_g = dot(n_own[:, cut], dpre_ref[:half, :], tn) + dot(n_oth[:, cut], dpre_ref[half:, :], tn)
        grad_ref[2 * j:2 * j + 2, :, 0, :piece, :] = up_g.astype(jnp.bfloat16).reshape(2, 2, piece, hid)
        down_g = dot(act_ref[:half, cut], dy_own[...], tn) + dot(act_ref[half:, cut], dy_oth[...], tn)
        grad_ref[2 * j:2 * j + 2, :, 0, piece:, :] = down_g.astype(jnp.bfloat16).reshape(2, 2, piece, width)


def mlp_second(n2, dy, acted, d_pre, pack, before=None, grads=None):
    tokens, width = 2 * n2[0].shape[0], n2[0].shape[1]
    bf16, f32 = jnp.bfloat16, jnp.float32
    first = before is None
    whole = lambda shape: pl.BlockSpec(shape, lambda i: (0,) * len(shape))
    args = [*n2, *dy, acted, d_pre, pack] + ([] if first else [before])
    sums = sum_shapes(tokens, width, first)
    shape = (4, 2, 2, pack.shape[1], width)
    return pl.pallas_call(
        partial(mlp_grad_kernel, first=first),
        grid=(1,),
        in_specs=[whole(v.shape) for v in args] + [pl.BlockSpec(memory_space=pltpu.HBM)] * (not first),
        out_specs=[whole(v.shape) for v in sums]
        + [pl.BlockSpec((4, 2, 1) + shape[3:], lambda i: (0, 0, 0 if first else 1, 0, 0))],
        out_shape=sums + [jax.ShapeDtypeStruct(shape, bf16)],
        input_output_aliases={} if first else {len(args): len(sums)},
        compiler_params=pltpu.CompilerParams(vmem_limit_bytes=48 * 1024 * 1024),
        cost_estimate=pl.CostEstimate(flops=8 * 10**9, bytes_accessed=2 * 10**7, transcendentals=0),
        name="mlp_second",
    )(*args, *([] if first else [grads]))


def call(kernel, name, args, outs, ahead=(), smem=(), scratch=(), passed=()):
    vmem = pl.BlockSpec(memory_space=pltpu.VMEM)
    anywhere = pl.BlockSpec(memory_space=pltpu.HBM)
    n_in = len(smem) + len(args)
    return pl.pallas_call(
        kernel,
        in_specs=[pl.BlockSpec(memory_space=pltpu.SMEM)] * len(smem)
        + [vmem] * len(args)
        + [anywhere] * (len(passed) + len(ahead)),
        out_specs=[vmem] * len(outs) + [anywhere] * len(passed),
        out_shape=list(outs) + [jax.ShapeDtypeStruct(v.shape, v.dtype) for v in passed],
        input_output_aliases={n_in + i: len(outs) + i for i in range(len(passed))},
        scratch_shapes=list(scratch),
        compiler_params=pltpu.CompilerParams(vmem_limit_bytes=48 * 1024 * 1024),
        cost_estimate=pl.CostEstimate(flops=10**9, bytes_accessed=4 * 10**6, transcendentals=0),
        name=name,
    )(*smem, *args, *passed, *ahead)


norm_eps = 1e-05


def norm_rows(values):
    center = values - jnp.mean(values, axis=1, keepdims=True)
    scale = lax.rsqrt(jnp.mean(center * center, axis=1, keepdims=True) + norm_eps)
    return center * scale, scale


def norm_back(grad, xhat, scale, gain):
    dx = grad * gain
    return scale * (
        dx - jnp.mean(dx, axis=1, keepdims=True) - xhat * jnp.mean(dx * xhat, axis=1, keepdims=True)
    )


ROWS = 128


def enter_kernel(dealt_ref, gain_ref, bias_ref, *rest):
    x_ref, n_ref = rest[-2:]
    width = x_ref.shape[1]
    for i in range(x_ref.shape[0] // ROWS):
        rows = slice(i * ROWS, (i + 1) * ROWS)
        x = dealt_ref[:, :, rows].reshape(width, ROWS).astype(jnp.float32).T
        x_ref[rows, :] = x.astype(jnp.bfloat16)
        n_ref[rows, :] = (norm_rows(x)[0] * gain_ref[...] + bias_ref[...]).astype(jnp.bfloat16)


def turn_kernel(z_ref, d0, d1, d2, d3, *rest):
    out_ref, turned = rest[2], rest[-1]
    for d, part in enumerate((d0, d1, d2, d3)):
        turned[z_ref[0] ^ d] = part[...]
    for i in range(out_ref.shape[0] // ROWS):
        rows = slice(i * ROWS, (i + 1) * ROWS)
        out_ref[rows, :] = turned[:, :, rows].reshape(out_ref.shape[1], ROWS).astype(jnp.float32).T.astype(jnp.bfloat16)


def pick_kernel(which_ref, own_ref, got_ref, *rest):
    out_ref = rest[0]
    rows = pl.ds(pl.multiple_of(which_ref[1] * out_ref.shape[0], 16), out_ref.shape[0])

    @pl.when(which_ref[0] == 1)
    def _():
        out_ref[...] = own_ref[rows, :]

    @pl.when(which_ref[0] == 0)
    def _():
        out_ref[...] = got_ref[rows, :]


def middle_kernel(x_ref, near_ref, got_ref, gain_ref, bias_ref, *rest):
    resid_ref, n_ref = rest[-2:]
    for i in range(x_ref.shape[0] // ROWS):
        rows = slice(i * ROWS, (i + 1) * ROWS)
        resid = x_ref[rows, :].astype(jnp.float32) + near_ref[rows, :] + got_ref[rows, :].astype(jnp.float32)
        resid_ref[rows, :] = resid
        xhat = norm_rows(resid.astype(jnp.bfloat16).astype(jnp.float32))[0]
        n_ref[rows, :] = (xhat * gain_ref[...] + bias_ref[...]).astype(jnp.bfloat16)


def middle_back_kernel(own_ref, got_ref, resid_ref, dy_ref, gain_ref, *rest):
    d_ref, low_ref, vec_ref = rest[-3:]
    total = None
    for i in range(own_ref.shape[0] // ROWS):
        rows = slice(i * ROWS, (i + 1) * ROWS)
        grad = own_ref[rows, :] + got_ref[rows, :].astype(jnp.float32)
        xhat, scale = norm_rows(resid_ref[rows, :].astype(jnp.bfloat16).astype(jnp.float32))
        sums = [jnp.sum(grad * xhat, axis=0, keepdims=True), jnp.sum(grad, axis=0, keepdims=True)]
        total = sums if total is None else [a + b for a, b in zip(total, sums)]
        d = dy_ref[rows, :].astype(jnp.float32) + norm_back(grad, xhat, scale, gain_ref[...])
        d_ref[rows, :] = d
        low_ref[rows, :] = d.astype(jnp.bfloat16)
    vec_ref[0:1, :] = total[0]
    vec_ref[1:2, :] = total[1]


def block_kernel(resid_ref, own_ref, got_ref, *rest):
    out_ref = rest[-1]
    parts, quarter, _ = out_ref.shape
    for i in range(own_ref.shape[0] // ROWS):
        rows = slice(i * ROWS, (i + 1) * ROWS)
        out = resid_ref[rows, :] + own_ref[rows, :] + got_ref[rows, :].astype(jnp.float32)
        out_ref[:, :, rows] = out.T.astype(jnp.bfloat16).reshape(parts, quarter, ROWS)


def leave_kernel(near_ref, got_ref, x_ref, d_ref, gain_ref, vec_ref, *rest):
    out_ref = rest[-1]
    parts, quarter = out_ref.shape[0], near_ref.shape[1] // out_ref.shape[0]
    total = None
    for i in range(near_ref.shape[0] // ROWS):
        rows = slice(i * ROWS, (i + 1) * ROWS)
        grad = near_ref[rows, :] + got_ref[rows, :].astype(jnp.float32)
        xhat, scale = norm_rows(x_ref[rows, :].astype(jnp.float32))
        sums = [jnp.sum(grad * xhat, axis=0, keepdims=True), jnp.sum(grad, axis=0, keepdims=True)]
        total = sums if total is None else [a + b for a, b in zip(total, sums)]
        out = d_ref[rows, :] + norm_back(grad, xhat, scale, gain_ref[...])
        out_ref[:, :quarter, rows] = out.T.astype(jnp.bfloat16).reshape(parts, quarter, ROWS)
    vec = jnp.concatenate(total + [vec_ref[0:1, :], vec_ref[1:2, :]], axis=0)
    high = vec.astype(jnp.bfloat16).astype(jnp.float32)
    both = jnp.concatenate([high, vec - high], axis=0)
    tail = out_ref.shape[1] - quarter
    for k in range(parts):
        mine = both[:, k * quarter:(k + 1) * quarter]
        mine = jnp.concatenate([mine, jnp.zeros((8, out_ref.shape[2] - quarter), jnp.float32)], axis=1)
        mine = jnp.concatenate([mine, jnp.zeros((tail - 8, out_ref.shape[2]), jnp.float32)], axis=0)
        out_ref[k, quarter:, :] = mine.astype(jnp.bfloat16)


def sum_kernel(a, b, c, d, *rest, out_at):
    total = a[...].astype(jnp.float32) + b[...].astype(jnp.float32) + c[...].astype(jnp.float32) + d[...].astype(jnp.float32)
    rest[out_at][...] = total.astype(jnp.bfloat16)


def sum_slices_kernel(a, *rest):
    rest[-2][...] = jnp.sum(a[...].astype(jnp.float32), axis=0).astype(jnp.bfloat16)


def sum_four(pieces, name, ahead=(), passed=()):
    out = [jax.ShapeDtypeStruct(pieces[0].shape, jnp.bfloat16)]
    at = len(passed) + len(ahead)
    return call(partial(sum_kernel, out_at=at), name, pieces, out, ahead=ahead, passed=passed)


def own_group(i):
    return (i & 3) // 2 == (i >> 2) & 1


def far_group(i):
    return not own_group(i)


def shards(
    activations, segment_ids, block_lists, feature_proj, input_norm_gain, input_norm_bias, qkv_weight,
    out_weight, middle_norm_gain, middle_norm_bias, up_weight, down_weight, out_grad,
):
    rows_n, heads_n = lax.axis_size("row"), lax.axis_size("head")
    total = rows_n * heads_n
    r, z = lax.axis_index("row"), lax.axis_index("head")
    c, p = r % 2, (r // 2) % 4
    groups = rows_n // 8
    pairs = [[2 * i, 2 * i + 1] for i in range(rows_n // 2)]
    planes = [[8 * g + i for i in range(8)] for g in range(groups)]
    quads = [[8 * g + 2 * i + k for i in range(4)] for g in range(groups) for k in range(2)]
    width = input_norm_gain.shape[0]
    quarter = width // heads_n
    seq_count, length = segment_ids.shape
    half = length // 2
    lists_here = block_lists.shape[1]
    bf16, f32 = jnp.bfloat16, jnp.float32
    local = (z // 2) == c
    par = z % 2

    def move(v, mask, only=None):
        moves = [(i, i ^ mask) for i in range(total) if only is None or only(i)]
        return lax.ppermute(v, ("row", "head"), moves)

    def later(i, dep):
        one = lax.slice(dep, (0,) * dep.ndim, (1,) * dep.ndim).reshape(())
        return i + (one != one).astype(jnp.int32)

    def deal_z(v):
        return lax.all_to_all(v, "head", 0, 0, tiled=True)

    def tied(v, dep):
        one = lax.slice(dep, (0,) * dep.ndim, (1,) * dep.ndim).reshape(())
        return v + (one != one).astype(v.dtype)

    def deal(v, side):
        v = v.T

        def token_half(k):
            return jnp.stack([lax.dynamic_slice_in_dim(v, s * length + k * half, half, 1) for s in range(seq_count)])

        keep, got = token_half(side), move(token_half(1 - side), 4)
        return jnp.concatenate([jnp.where(side == 0, keep, got), jnp.where(side == 0, got, keep)], 0)

    def collect(v):
        v = v.reshape(2, seq_count, quarter, half)
        keep = lax.dynamic_index_in_dim(v, c, 0, keepdims=False)
        got = move(lax.dynamic_index_in_dim(v, 1 - c, 0, keepdims=False), 4)
        low, high = jnp.where(c == 0, keep, got), jnp.where(c == 0, got, keep)
        return jnp.concatenate([w[s] for s in range(seq_count) for w in (low, high)], 1).T

    def fetch_z(mine):
        return [mine] + [move(mine, d, own_group) for d in (1, 2, 3)]

    def choose(got, here):
        return jnp.stack([jnp.where(here, got[0], got[2]), jnp.where(here, got[1], got[3])])

    def fetch_plane(both):
        return [both] + [move(both, 8 * d) for d in (1, 2, 3)]

    def give_z(same, other, ahead):
        parts = (same, move(other, 1, own_group), move(same, 2, far_group), move(other, 3, far_group))
        (fin,) = sum_four(parts, "sum_z", ahead=(ahead,))
        if groups > 1:
            fin = lax.psum(fin.astype(f32), "row", axis_index_groups=[[8 * g + i for g in range(groups)] for i in range(8)])
            fin = fin.astype(bf16)
        return call(
            pick_kernel, "pick", (fin, move(fin, 4)), (jax.ShapeDtypeStruct((fin.shape[0] // 2, width), bf16),),
            smem=(jnp.stack([local.astype(jnp.int32), c]),),
        )[0]

    def gather_plane(v):
        return lax.all_gather(v, "row", axis=0, axis_index_groups=planes)

    cut = lambda w, n, at: lax.dynamic_slice_in_dim(w, at * n, n, 0)

    aux = jnp.concatenate([block_lists.reshape(seq_count, -1), segment_ids], 1).astype(bf16)
    aux_got = move(aux, 4)
    aux = jnp.where(c == 0, jnp.concatenate([aux, aux_got], 0), jnp.concatenate([aux_got, aux], 0))
    n_list = aux.shape[1] - length
    seg = lax.dynamic_index_in_dim(aux[:, n_list:], z, 0, keepdims=False).astype(jnp.int32)

    four = deal(activations, c)
    gain1, bias1, gain2, bias2 = (
        v.reshape(1, width) for v in (input_norm_gain, input_norm_bias, middle_norm_gain, middle_norm_bias)
    )
    shape_of = jax.ShapeDtypeStruct
    half_low, half_wide = shape_of((half, width), bf16), shape_of((half, width), f32)
    dy_four = deal(out_grad, c)
    x_half, n1_half = call(enter_kernel, "enter", (deal_z(four), gain1, bias1), (half_low, half_low), ahead=(dy_four,))

    n_qkv, n_out = qkv_weight.shape[1] // 4, out_weight.shape[0] // 4
    extra = 16
    rider = aux[:, :n_list].reshape(-1)
    rider = jnp.pad(rider, (0, extra * width - rider.shape[0])).reshape(extra, width)
    p_late = later(p, four)
    mine = [cut(qkv_weight.T, n_qkv, p_late), cut(out_weight, n_out, p_late), rider]
    both = choose(fetch_z(jnp.concatenate(mine, 0)), local)
    lists = both[:, n_qkv + n_out:].reshape(2, -1)[:, :4 * n_list].reshape(2, 4, n_list).astype(jnp.int32)
    lists = lax.dynamic_index_in_dim(lists, z, 1, keepdims=False).reshape((2, lists_here) + block_lists.shape[2:])
    pieces = fetch_plane(both[:, :n_qkv + n_out])
    at = jnp.full((1,), p, jnp.int32)

    n_up, n_hid = width // 8, down_weight.shape[0] // 8
    q8 = later(r % 8, x_half)
    mine = jnp.concatenate([cut(up_weight, n_up, q8), cut(down_weight, n_hid, q8)], 0)
    all_z = lax.all_gather(mine, "head", axis=0).reshape((1, 2, 2) + mine.shape)
    send = [jnp.broadcast_to(all_z[:, :, i], (4, 2) + mine.shape).reshape((8,) + mine.shape) for i in range(2)]
    packs = [lax.all_to_all(v, "row", 0, 0, axis_index_groups=planes, tiled=True) for v in send]

    shift = c * half
    seg = lax.dynamic_slice_in_dim(jnp.concatenate([seg, seg]), shift, length, 0)
    hits = []
    for own in lists:
        own = lax.dynamic_slice_in_dim(jnp.concatenate([own, own], 1), shift // BLK, length // BLK, 1)
        hit = hit_lanes(own, length)
        hits.append(lax.dynamic_slice_in_dim(jnp.concatenate([hit, hit], 2), shift, length, 2))

    n1 = (n1_half, move(n1_half, 4))
    att = [attn_fwd(at, *n1, pieces, 0, seg, hits[0], feature_proj)]
    z_late = z + att[0][-1][0]
    dy_parts = [lax.dynamic_index_in_dim(dy_four, z_late ^ d, 0, keepdims=False) for d in range(heads_n)]
    dy_got = [move(v, d) if d else v for d, v in enumerate(dy_parts)]
    att.append(attn_fwd(at, *n1, pieces, 1, seg, hits[1], feature_proj, att[0][7], (send[0], *dy_parts)))
    heads_out = [v[0] for v in att]
    qkv = [v[4] for v in att]
    wq = [v[5] for v in att]
    outw = [v[6].reshape(-1, width) for v in att]
    dy_half, near, away = call(
        turn_kernel, "turn", dy_got, (half_low,), smem=(z.reshape(1),), passed=att[1][7:9],
        scratch=(pltpu.VMEM((heads_n, quarter, half), bf16),),
    )
    resid, n2_half = call(
        middle_kernel, "middle", (x_half, near, move(away, 4), gain2, bias2), (half_wide, half_low), ahead=(packs[0],)
    )
    n2 = (n2_half, move(n2_half, 4))
    dy = (dy_half, move(dy_half, 4))
    acted, d_pre, dn = mlp_first(n2, dy, packs[0])
    mo, grads = mlp_second(n2, dy, acted, d_pre, packs[0])
    acted, d_pre, dn_own, dn_oth = mlp_first(n2, dy, packs[1], dn, (mo,))
    mo_own, mo_oth, grads = mlp_second(n2, dy, acted, d_pre, packs[1], mo, grads)
    d_resid, d_half, vec2 = call(
        middle_back_kernel, "middle_back", (dn_own, move(dn_oth, 4), resid, dy_half, gain2),
        (half_wide, half_low, shape_of((2, width), f32)),
    )
    (block_send,) = call(
        block_kernel, "block", (resid, mo_own, move(mo_oth, 4)), (shape_of((heads_n, quarter, half), bf16),)
    )
    block_got = deal_z(block_send)
    block_out = collect(block_got)
    d_branch = (d_half, move(d_half, 4))
    grads = lax.psum_scatter(
        grads.reshape(-1, width), "row", scatter_dimension=0, axis_index_groups=quads, tiled=True
    ).reshape(2, 2, -1, width)
    back = [
        attn_bwd(at, qkv[0], seg, hits[0], feature_proj, *att[0][1:4], heads_out[0], *d_branch, outw[0], *n1, wq[0], None, (mo_oth,))
    ]
    c_late = later(c + back[0][2][0], block_got)
    keep = lax.dynamic_index_in_dim(grads, c_late, 0, keepdims=False)
    got = move(lax.dynamic_index_in_dim(grads, 1 - c_late, 0, keepdims=False), 4)
    four = jnp.concatenate([jnp.where(c == 0, keep, got), jnp.where(c == 0, got, keep)], 0)
    four_flat = four.reshape(-1, width)
    mlp_slice = mlp_grads = lax.psum_scatter(four_flat, "head", scatter_dimension=0, tiled=True)
    if groups > 1:
        mlp_grads = lax.psum(mlp_grads, "row", axis_index_groups=[[8 * g + i for g in range(groups)] for i in range(8)])

    back.append(
        attn_bwd(
            at, qkv[1], seg, hits[1], feature_proj, *att[1][1:4], heads_out[1], *d_branch, outw[1], *n1, wq[1], back[0][1],
            (block_got, four_flat),
        )
    )
    def across(pieces):
        return [pieces[0]] + [move(pieces[d], 8 * d) for d in (1, 2, 3)]

    first = lax.all_to_all(back[0][0], "row", 0, 0, axis_index_groups=quads, tiled=True)
    first, *passed = call(
        sum_slices_kernel, "sum_first", (first,), (shape_of(first.shape[1:], bf16),), passed=(mlp_grads,), ahead=(back[1][0],)
    )
    (mlp_grads,) = passed
    pieces, (near, away) = back[1][:4], back[1][4:6]
    mlp_grads = gather_plane(mlp_grads)
    up_grad = mlp_grads[:, :n_up].reshape(width, -1).astype(f32)
    down_grad = mlp_grads[:, n_up:].reshape(-1, width).astype(f32)
    (send,) = call(
        leave_kernel, "leave", (near, move(away, 4), x_half, d_resid, gain1, vec2),
        (shape_of((heads_n, quarter + 16, half), bf16),), ahead=(first,),
    )
    (second,) = sum_four(across(pieces), "sum_second", ahead=(send,))
    got = deal_z(send)
    qkv_slice = give_z(first, second, got)
    input_grad = collect(got[:, :quarter]).astype(f32)
    vec = jnp.sum(got[:, quarter:quarter + 8, :quarter].astype(f32), 0)
    qkv_slice = tied(qkv_slice, mlp_grads)
    got = gather_plane(qkv_slice)
    vec = tied(vec[:4] + vec[4:], qkv_slice)
    for mask in (4, 8, 16):
        vec = vec + move(vec, mask)
    if groups > 1:
        vec = lax.psum(vec, "row", axis_index_groups=[[8 * g + i for g in range(groups)] for i in range(8)])
    both = got.reshape(4, n_qkv + n_out, width)
    qkv_grad = both[:, :n_qkv].reshape(-1, width).astype(f32).T
    out_w_grad = both[:, n_qkv:].reshape(-1, width).astype(f32)
    return (
        block_out, input_grad, vec[0], vec[1], qkv_grad, out_w_grad, vec[2], vec[3], up_grad, down_grad,
    )


def solution(mesh):
    return jax.shard_map(
        shards,
        mesh=mesh,
        in_specs=(
            P("row", "head"), P("row", None), P("row", "head", None, None), P(), P(), P(), P(None, "head"),
            P("head", None), P(), P(), P(None, "head"), P("head", None), P("row", "head"),
        ),
        out_specs=(
            P("row", "head"), P("row", "head"), P("head"), P("head"), P(None, "head"), P("head", None),
            P("head"), P("head"), P(None, "head"), P("head", None),
        ),
        check_vma=False,
    )
```

```python
from functools import partial

import math
import jax, jax.numpy as jnp
from jax import lax
from jax.experimental import pallas as pl
from jax.experimental.pallas import tpu as pltpu

BLK = 64
CHUNK = 1024
LOG2E = 1.4426950408889634

def dot(a, b, dims):
    return lax.dot_general(a, b, (dims, ((), ())), preferred_element_type=jnp.float32)

def meets(seg_ref, r0, tq, c0, tk):
    return (seg_ref[0, r0] <= seg_ref[0, c0 + tk - 1]) & (seg_ref[0, c0] <= seg_ref[0, r0 + tq - 1])

def fwd_kernel(at_ref, seg_s, own_ref, oth_ref, segc_ref, segr_ref, hit_ref, proj_ref, *rest, tq, tk, dh, part):
    (out_ref, rinv_ref, *early, done_ref, vext, qf_ref, kf_ref, qkv_ref, w_ref, wo_ref, sems) = rest[-(15 if part == 0 else 17):]
    sums, early = early[:-5], early[-5:]
    done_ref[0] = 0
    cut = w_ref.shape[1]
    slots = [at_ref[0] ^ d for d in range(4)]
    copies = [
        pltpu.make_async_copy(piece.at[part, pl.ds(0, cut), :], w_ref.at[slots[d]], sems.at[0, d])
        for d, piece in enumerate(rest[:4])
    ] + [
        pltpu.make_async_copy(piece.at[part, pl.ds(cut, wo_ref.shape[1]), :], wo_ref.at[slots[d]], sems.at[1, d])
        for d, piece in enumerate(rest[:4])
    ]
    for copy in copies:
        copy.start()
    for copy in copies:
        copy.wait()
    leaving = [
        pltpu.make_async_copy(src, dst, sems.at[2 + i // 4, i % 4])
        for i, (src, dst) in enumerate(zip((qf_ref, kf_ref, qkv_ref, w_ref, wo_ref), early))
    ]
    leaving[3].start()
    leaving[4].start()
    weights = w_ref[...].reshape(qkv_ref.shape[1], own_ref.shape[1])
    for side, n_ref in enumerate((own_ref, oth_ref)):
        def project(i, _, base=side * own_ref.shape[0], n_ref=n_ref):
            r0 = pl.multiple_of(i * 256, 256)
            qkv_ref[pl.ds(base + r0, 256), :] = dot(n_ref[pl.ds(r0, 256), :], weights, ((1,), (1,))).astype(jnp.bfloat16)
            return 0

        lax.fori_loop(0, n_ref.shape[0] // 256, project, 0)
    length = qkv_ref.shape[0]
    feats = proj_ref.shape[1]
    quarter = dh ** (-0.25)
    nh = qkv_ref.shape[1] // (3 * dh)
    for h in range(nh):
        base = h * 3 * dh
        for j, f_ref in ((0, qf_ref), (1, kf_ref)):
            for r0 in range(0, length, CHUNK):
                rows = slice(r0, r0 + CHUNK)
                t = qkv_ref[rows, base + j * dh: base + (j + 1) * dh]
                lin = dot(t, proj_ref[...], ((1,), (0,)))
                tw = t.astype(jnp.float32)
                sq = jnp.sum(tw * tw, axis=1, keepdims=True) * (0.5 * quarter * quarter * LOG2E) + 0.5 * math.log2(feats)
                f_ref[h, rows, :] = jnp.exp2(lin * (quarter * LOG2E) - sq).astype(jnp.bfloat16)
        v = qkv_ref[:, base + 2 * dh: base + 3 * dh]
        lane = lax.broadcasted_iota(jnp.int32, (length, dh), 1)
        vext[h, :, :] = jnp.concatenate([v, (lane < 1).astype(jnp.bfloat16)], axis=1)

    for copy in leaving[:3]:
        copy.start()

    def q_body(i, _):
        r0 = pl.multiple_of(i * tq, tq)
        qs = [qkv_ref[pl.ds(r0, tq), h * 3 * dh: h * 3 * dh + dh] for h in range(nh)]
        qfs = [qf_ref[h, pl.ds(r0, tq), :] for h in range(nh)]
        segq = segc_ref[pl.ds(r0, tq), :]
        def k_body(j, acc):
            c0 = pl.multiple_of(j * tk, tk)
            same = segq == segr_ref[:, pl.ds(c0, tk)]
            new = []
            for h in range(nh):
                k = qkv_ref[pl.ds(c0, tk), h * 3 * dh + dh: h * 3 * dh + 2 * dh]
                s = dot(qs[h], k, ((1,), (1,)))
                e = jnp.exp2(s * (LOG2E * dh ** -0.5))
                a = dot(qfs[h], kf_ref[h, pl.ds(c0, tk), :], ((1,), (1,)))
                parts = []
                for b in range(tq // BLK):
                    hit = hit_ref[h, pl.ds(i * (tq // BLK) + b, 1), pl.ds(c0, tk)] > 0.5
                    rs = slice(b * BLK, (b + 1) * BLK)
                    parts.append(jnp.where(jnp.broadcast_to(hit, (BLK, tk)), e[rs], a[rs]))
                comb = jnp.where(same, jnp.concatenate(parts, axis=0), 0.0).astype(jnp.bfloat16)
                new.append(acc[h] + dot(comb, vext[h, pl.ds(c0, tk), :], ((1,), (0,))))
            return tuple(new)
        def k_step(j, acc):
            return lax.cond(meets(seg_s, r0, tq, pl.multiple_of(j * tk, tk), tk), lambda a: k_body(j, a), lambda a: a, acc)
        acc = lax.fori_loop(0, length // tk, k_step, tuple(jnp.zeros((tq, 2 * dh), jnp.float32) for _ in range(nh)))
        for h in range(nh):
            rinv = 1.0 / acc[h][:, dh:dh + 1]
            out_ref[pl.ds(r0, tq), h * dh:(h + 1) * dh] = (acc[h][:, :dh] * rinv).astype(jnp.bfloat16)
            rinv_ref[pl.ds(r0, tq), h:h + 1] = rinv
        return 0
    lax.fori_loop(0, length // tq, q_body, 0)

    if part:
        other, w_other = rest[4], rest[5]
        w_first = w_other[...].reshape(out_ref.shape[1], own_ref.shape[1])
        w_out = wo_ref[...].reshape(out_ref.shape[1], own_ref.shape[1])
        add_parts(
            lambda rows: dot(other[rows, :], w_first, ((1,), (0,))) + dot(out_ref[rows, :], w_out, ((1,), (0,))),
            None, sums, length, False,
        )
    for copy in leaving:
        copy.wait()


def add_parts(product, before, sums, length, first):
    half = length // 2

    def body(i, _):
        rows = pl.ds(pl.multiple_of(i * 256, 256), 256)
        part = product(rows)
        if first:
            sums[0][rows, :] = part
        else:
            total = part if before is None else part + before[rows, :]
            @pl.when(i < half // 256)
            def _():
                sums[0][rows, :] = total
            @pl.when(i >= half // 256)
            def _():
                sums[1][pl.ds(pl.multiple_of(i * 256 - half, 256), 256), :] = total.astype(jnp.bfloat16)
        return 0

    lax.fori_loop(0, length // 256, body, 0)


def sum_shapes(length, width, first):
    whole = lambda n, dtype: jax.ShapeDtypeStruct((n, width), dtype)
    return [whole(length, jnp.float32)] if first else [whole(length // 2, jnp.float32), whole(length // 2, jnp.bfloat16)]


def attn_fwd(at, n_own, n_oth, pieces, part, seg, hit, proj, before=(), ahead=(), *, tq=512, tk=256):
    length, width = 2 * n_own.shape[0], n_own.shape[1]
    dh, feats = proj.shape
    heads = hit.shape[0]
    cols = 3 * heads * dh
    seg2 = seg.reshape(1, length)
    bf16 = jnp.bfloat16
    smem = pl.BlockSpec(memory_space=pltpu.SMEM)
    vmem = pl.BlockSpec(memory_space=pltpu.VMEM)
    anywhere = pl.BlockSpec(memory_space=pltpu.HBM)
    early = [
        ((heads, length, feats), bf16), ((heads, length, feats), bf16), ((length, cols), bf16),
        ((4, cols // 4, width), bf16), ((4, heads * dh // 4, width), bf16),
    ]
    sums = sum_shapes(length, width, False) if part else []
    return pl.pallas_call(
        partial(fwd_kernel, tq=tq, tk=tk, dh=dh, part=part),
        in_specs=[smem] * 2 + [vmem] * 6 + [anywhere] * 4 + [vmem] * len(before) + [anywhere] * len(ahead),
        out_specs=[vmem] * (2 + len(sums)) + [anywhere] * 5 + [smem],
        out_shape=[jax.ShapeDtypeStruct((length, heads * dh), bf16), jax.ShapeDtypeStruct((length, 8), jnp.float32)]
        + sums
        + [jax.ShapeDtypeStruct(*v) for v in early]
        + [jax.ShapeDtypeStruct((1,), jnp.int32)],
        scratch_shapes=[pltpu.VMEM((heads, length, 2 * dh), bf16)]
        + [pltpu.VMEM(*v) for v in early]
        + [pltpu.SemaphoreType.DMA((4, 4))],
        compiler_params=pltpu.CompilerParams(vmem_limit_bytes=48 * 1024 * 1024),
        cost_estimate=pl.CostEstimate(flops=27 * 10**9, bytes_accessed=10**7, transcendentals=10**6),
        name="attn_fwd",
    )(at, seg2, n_own, n_oth, seg.reshape(length, 1), seg2, hit, proj, *pieces, *before, *ahead)


def bwd_kernel(at_ref, seg_s, qkv_ref, segc_ref, segr_ref, hit_ref, proj_ref, pext_ref, qf_ref, kf_ref, rinv_ref, o_ref,
               d_own, d_oth, w_out, *rest, tq, tk, dh, first):
    n_late = 3 if first else 5
    (*outs, done_ref, dqkv_s, do_ref, grad_s, vext, doext, dq, dk, dv, dqf, dkf, late_sem) = rest[-(14 if first else 18) - n_late:-n_late]
    late = rest[-n_late:]
    n_own, n_oth, w_ref = late[:3]
    arriving = [pltpu.make_async_copy(src, dst, late_sem.at[i]) for i, (src, dst) in enumerate(zip(rest, late))]
    for copy in arriving:
        copy.start()
    dqkv_ref = outs[1] if first else dqkv_s
    done_ref[0] = 0
    length = qkv_ref.shape[0]
    half = length // 2
    quarter = dh ** (-0.25)
    nh = qkv_ref.shape[1] // (3 * dh)
    for side, d_ref in enumerate((d_own, d_oth)):
        do_ref[side * half:(side + 1) * half, :] = dot(d_ref[...], w_out[...], ((1,), (1,))).astype(jnp.bfloat16)
    lane = lax.broadcasted_iota(jnp.int32, (length, dh), 1)
    for h in range(nh):
        base = h * 3 * dh
        v = qkv_ref[:, base + 2 * dh: base + 3 * dh]
        vext[h, :, :] = jnp.concatenate([v, (lane < 2).astype(jnp.bfloat16)], axis=1)
        d_o = do_ref[:, h * dh:(h + 1) * dh].astype(jnp.float32)
        o = o_ref[:, h * dh:(h + 1) * dh].astype(jnp.float32)
        rinv = rinv_ref[:, h:h + 1]
        delta = -jnp.sum(d_o * o, axis=1, keepdims=True) * rinv
        high = delta.astype(jnp.bfloat16).astype(jnp.float32)
        low = delta - high
        tail = jnp.where(lane == 0, high, jnp.where(lane == 1, low, 0.0))
        doext[h, :, :] = jnp.concatenate([d_o * rinv, tail], axis=1).astype(jnp.bfloat16)
    dq[...] = jnp.zeros_like(dq)
    dk[...] = jnp.zeros_like(dk)
    dv[...] = jnp.zeros_like(dv)
    dqf[...] = jnp.zeros_like(dqf)
    dkf[...] = jnp.zeros_like(dkf)

    def q_body(i, _):
        r0 = pl.multiple_of(i * tq, tq)
        rows = pl.ds(r0, tq)
        segq = segc_ref[rows, :]
        def k_body(j, _):
            c0 = pl.multiple_of(j * tk, tk)
            cols = pl.ds(c0, tk)
            same = segq == segr_ref[:, cols]
            for h in range(nh):
                base = h * 3 * dh
                q = qkv_ref[rows, base: base + dh]
                k = qkv_ref[cols, base + dh: base + 2 * dh]
                qf = qf_ref[h, rows, :]
                kf = kf_ref[h, cols, :]
                s = dot(q, k, ((1,), (1,)))
                e = jnp.exp2(s * (LOG2E * dh ** -0.5))
                a = dot(qf, kf, ((1,), (1,)))
                dc = dot(doext[h, rows, :], vext[h, cols, :], ((1,), (1,)))
                dc = jnp.where(same, dc, 0.0)
                combs, dss, das = [], [], []
                for b in range(tq // BLK):
                    hit = hit_ref[h, pl.ds(i * (tq // BLK) + b, 1), cols] > 0.5
                    hit = jnp.broadcast_to(hit, (BLK, tk))
                    rs = slice(b * BLK, (b + 1) * BLK)
                    combs.append(jnp.where(hit, e[rs], a[rs]))
                    dss.append(jnp.where(hit, dc[rs] * e[rs], 0.0))
                    das.append(jnp.where(hit, 0.0, dc[rs]))
                comb = jnp.where(same, jnp.concatenate(combs, axis=0), 0.0).astype(jnp.bfloat16)
                ds = jnp.concatenate(dss, axis=0).astype(jnp.bfloat16)
                da = jnp.concatenate(das, axis=0).astype(jnp.bfloat16)
                dq[h, rows, :] += dot(ds, k, ((1,), (0,)))
                dqf[h, rows, :] += dot(da, kf, ((1,), (0,)))
                dk[h, cols, :] += dot(ds, q, ((0,), (0,)))
                dkf[h, cols, :] += dot(da, qf, ((0,), (0,)))
                dv[h, cols, :] += dot(comb, doext[h, rows, :dh], ((0,), (0,)))
            return 0
        def k_step(j, _):
            @pl.when(meets(seg_s, r0, tq, pl.multiple_of(j * tk, tk), tk))
            def _():
                k_body(j, 0)
            return 0
        lax.fori_loop(0, length // tk, k_step, 0)
        return 0
    lax.fori_loop(0, length // tq, q_body, 0)

    for h in range(nh):
        base = h * 3 * dh
        for j, dt, dfeat, f_ref in ((0, dq, dqf, qf_ref), (1, dk, dkf, kf_ref)):
            for r0 in range(0, length, CHUNK):
                rows = slice(r0, r0 + CHUNK)
                dpre = (dfeat[h, rows, :] * f_ref[h, rows, :].astype(jnp.float32)).astype(jnp.bfloat16)
                thr = dot(dpre, pext_ref[...], ((1,), (0,)))
                t = qkv_ref[rows, base + j * dh: base + (j + 1) * dh].astype(jnp.float32)
                g = dt[h, rows, :] * dh ** -0.5 + quarter * thr[:, :dh] - (quarter * quarter) * t * thr[:, dh:dh + 1]
                dqkv_ref[rows, base + j * dh: base + (j + 1) * dh] = g.astype(jnp.bfloat16)
        dqkv_ref[:, base + 2 * dh: base + 3 * dh] = dv[h].astype(jnp.bfloat16)

    for copy in arriving:
        copy.wait()
    if not first:
        dqkv_first, w_first = late[3:]
        weights = w_ref[...].reshape(qkv_ref.shape[1], n_own.shape[1])
        weights_first = w_first[...].reshape(qkv_ref.shape[1], n_own.shape[1])
        add_parts(
            lambda rows: dot(dqkv_first[rows, :], weights_first, ((1,), (0,))) + dot(dqkv_ref[rows, :], weights, ((1,), (0,))),
            None, outs[4:], length, False,
        )

    tn = ((0,), (0,))
    cut = w_ref.shape[1]
    grad = dot(dqkv_ref[:half, :], n_own[...], tn) + dot(dqkv_ref[half:, :], n_oth[...], tn)
    grad_s[:, :cut, :] = grad.astype(jnp.bfloat16).reshape(4, cut, n_own.shape[1])
    out = dot(o_ref[:half, :], d_own[...], tn) + dot(o_ref[half:, :], d_oth[...], tn)
    grad_s[:, cut:, :] = out.astype(jnp.bfloat16).reshape(4, o_ref.shape[1] // 4, n_own.shape[1])
    if first:
        outs[0][...] = grad_s[...]
    else:
        for d in range(4):
            outs[d][...] = grad_s[at_ref[0] ^ d]


def attn_bwd(at, qkv, seg, hit, proj, qf, kf, rinv, o, d_own, d_oth, w_out, late, ahead=(), *, tq=512, tk=256):
    length = qkv.shape[0]
    dh, feats = proj.shape
    width = d_own.shape[1]
    heads = qkv.shape[1] // (3 * dh)
    seg2 = seg.reshape(1, length)
    pext = jnp.concatenate([proj.T, jnp.ones((feats, 1), proj.dtype), jnp.zeros((feats, dh - 1), proj.dtype)], axis=1)
    f32, bf16 = jnp.float32, jnp.bfloat16
    smem = pl.BlockSpec(memory_space=pltpu.SMEM)
    vmem = pl.BlockSpec(memory_space=pltpu.VMEM)
    anywhere = pl.BlockSpec(memory_space=pltpu.HBM)
    first = len(late) == 3
    piece = jax.ShapeDtypeStruct(((qkv.shape[1] + o.shape[1]) // 4, width), bf16)
    if first:
        outs = [jax.ShapeDtypeStruct((4,) + piece.shape, bf16), jax.ShapeDtypeStruct(qkv.shape, bf16)]
    else:
        outs = [piece] * 4 + sum_shapes(length, width, False)
    return pl.pallas_call(
        partial(bwd_kernel, tq=tq, tk=tk, dh=dh, first=first),
        in_specs=[smem] * 2 + [vmem] * 13 + [anywhere] * (len(late) + len(ahead)),
        out_specs=[vmem] * len(outs) + [smem],
        out_shape=outs + [jax.ShapeDtypeStruct((1,), jnp.int32)],
        scratch_shapes=[
            pltpu.VMEM((16, 128) if first else qkv.shape, bf16),
            pltpu.VMEM(o.shape, bf16),
            pltpu.VMEM((4,) + piece.shape, bf16),
            pltpu.VMEM((heads, length, 2 * dh), bf16),
            pltpu.VMEM((heads, length, 2 * dh), bf16),
            pltpu.VMEM((heads, length, dh), f32),
            pltpu.VMEM((heads, length, dh), f32),
            pltpu.VMEM((heads, length, dh), f32),
            pltpu.VMEM((heads, length, feats), f32),
            pltpu.VMEM((heads, length, feats), f32),
            pltpu.SemaphoreType.DMA((5,)),
        ]
        + [pltpu.VMEM(v.shape, v.dtype) for v in late],
        compiler_params=pltpu.CompilerParams(vmem_limit_bytes=56 * 1024 * 1024),
        cost_estimate=pl.CostEstimate(flops=42 * 10**9, bytes_accessed=2 * 10**7, transcendentals=10**6),
        name="attn_bwd",
    )(at, seg2, qkv, seg.reshape(length, 1), seg2, hit, proj, pext, qf, kf, rinv, o, d_own, d_oth, w_out, *late, *ahead)


def hit_lanes(lists, length):
    nb = lists.shape[1]
    ids = lax.broadcasted_iota(jnp.int32, (1, 1, length), 2) // BLK
    out = lists[:, :, 0:1] == ids
    for s in range(1, lists.shape[2]):
        out = out | (lists[:, :, s:s + 1] == ids)
    return out.astype(jnp.float32)

from jax.sharding import PartitionSpec as P


def gelu_pair(u):
    mag = jnp.abs(u)
    t = 1.0 / (1.0 + (0.3275911 * 0.7071067811865476) * mag)
    bell = jnp.exp2(u * u * (-0.5 * LOG2E))
    poly = t * (0.127414796 + t * (-0.142248368 + t * (0.7107068705 + t * (-0.7265760135 + t * 0.5307027145))))
    tail = poly * bell
    cdf = jnp.where(u >= 0.0, 1.0 - tail, tail)
    return u * cdf, cdf + u * bell * 0.3989422804014327


def mlp_kernel(n_own, n_oth, dy_own, dy_oth, w_ref, *rest, tile, rows, first):
    act_ref, dpre_ref, *sums, acc = rest[-(4 if first else 5):]
    half, width = n_own.shape
    piece = w_ref.shape[1] // 2
    hid = act_ref.shape[1]
    up = w_ref[:, :piece, :].reshape(width, hid)
    down = w_ref[:, piece:, :].reshape(hid, width)
    for j in range(hid // tile):
        up_t = up[:, j * tile:(j + 1) * tile]
        down_t = down[j * tile:(j + 1) * tile, :]
        for side, (n_ref, dy_ref) in enumerate(((n_own, dy_own), (n_oth, dy_oth))):
            def body(i, _, j=j, up_t=up_t, down_t=down_t, n_ref=n_ref, dy_ref=dy_ref, base=side * half):
                r0 = pl.multiple_of(i * rows, rows)
                src = pl.ds(r0, rows)
                rs = pl.ds(base + r0, rows)
                pre = dot(n_ref[src, :], up_t, ((1,), (0,)))
                d_act = dot(dy_ref[src, :], down_t, ((1,), (1,)))
                act, slope = gelu_pair(pre)
                d_pre = (d_act * slope).astype(jnp.bfloat16)
                act_ref[rs, j * tile:(j + 1) * tile] = act.astype(jnp.bfloat16)
                dpre_ref[rs, j * tile:(j + 1) * tile] = d_pre
                part = dot(d_pre, up_t, ((1,), (1,)))
                if j == 0 and first:
                    acc[rs, :] = part
                elif j == 0:
                    acc[rs, :] = part + rest[0][rs, :]
                else:
                    acc[rs, :] += part
                return 0
            lax.fori_loop(0, half // rows, body, 0)
    if first:
        sums[0][...] = acc[...]
    else:
        sums[0][...] = acc[:half, :]
        sums[1][...] = acc[half:, :].astype(jnp.bfloat16)


def mlp_first(n2, dy, pack, before=None, ahead=(), *, tile=256, rows=256):
    tokens, width = 2 * n2[0].shape[0], n2[0].shape[1]
    hid = pack.shape[0] * pack.shape[1] // 2
    bf16, f32 = jnp.bfloat16, jnp.float32
    first = before is None
    vmem = pl.BlockSpec(memory_space=pltpu.VMEM)
    return pl.pallas_call(
        partial(mlp_kernel, tile=tile, rows=rows, first=first),
        in_specs=[vmem] * (5 if first else 6) + [pl.BlockSpec(memory_space=pltpu.HBM)] * len(ahead),
        out_specs=[vmem] * (3 if first else 4),
        out_shape=[jax.ShapeDtypeStruct((tokens, hid), bf16)] * 2 + sum_shapes(tokens, width, first),
        scratch_shapes=[pltpu.VMEM((tokens, width), f32)],
        compiler_params=pltpu.CompilerParams(vmem_limit_bytes=48 * 1024 * 1024),
        cost_estimate=pl.CostEstimate(flops=12 * 10**9, bytes_accessed=2 * 10**7, transcendentals=10**6),
        name="mlp_first",
    )(*n2, *dy, pack, *(() if first else (before,)), *ahead)


def mlp_grad_kernel(n_own, n_oth, dy_own, dy_oth, act_ref, dpre_ref, w_ref, *rest, first):
    *sums, grad_ref = rest[-(2 if first else 3):]
    half, width = n_own.shape
    piece = w_ref.shape[1] // 2
    hid = act_ref.shape[1]
    down = w_ref[:, piece:, :].reshape(hid, width)
    tn = ((0,), (0,))
    add_parts(lambda rs: dot(act_ref[rs, :], down, ((1,), (0,))), None if first else rest[0], sums, 2 * half, first)
    for j in range(width // (4 * piece)):
        cut = slice(4 * j * piece, 4 * (j + 1) * piece)
        up_g = dot(n_own[:, cut], dpre_ref[:half, :], tn) + dot(n_oth[:, cut], dpre_ref[half:, :], tn)
        grad_ref[2 * j:2 * j + 2, :, 0, :piece, :] = up_g.astype(jnp.bfloat16).reshape(2, 2, piece, hid)
        down_g = dot(act_ref[:half, cut], dy_own[...], tn) + dot(act_ref[half:, cut], dy_oth[...], tn)
        grad_ref[2 * j:2 * j + 2, :, 0, piece:, :] = down_g.astype(jnp.bfloat16).reshape(2, 2, piece, width)


def mlp_second(n2, dy, acted, d_pre, pack, before=None, grads=None):
    tokens, width = 2 * n2[0].shape[0], n2[0].shape[1]
    bf16, f32 = jnp.bfloat16, jnp.float32
    first = before is None
    whole = lambda shape: pl.BlockSpec(shape, lambda i: (0,) * len(shape))
    args = [*n2, *dy, acted, d_pre, pack] + ([] if first else [before])
    sums = sum_shapes(tokens, width, first)
    shape = (4, 2, 2, pack.shape[1], width)
    return pl.pallas_call(
        partial(mlp_grad_kernel, first=first),
        grid=(1,),
        in_specs=[whole(v.shape) for v in args] + [pl.BlockSpec(memory_space=pltpu.HBM)] * (not first),
        out_specs=[whole(v.shape) for v in sums]
        + [pl.BlockSpec((4, 2, 1) + shape[3:], lambda i: (0, 0, 0 if first else 1, 0, 0))],
        out_shape=sums + [jax.ShapeDtypeStruct(shape, bf16)],
        input_output_aliases={} if first else {len(args): len(sums)},
        compiler_params=pltpu.CompilerParams(vmem_limit_bytes=48 * 1024 * 1024),
        cost_estimate=pl.CostEstimate(flops=8 * 10**9, bytes_accessed=2 * 10**7, transcendentals=0),
        name="mlp_second",
    )(*args, *([] if first else [grads]))


def call(kernel, name, args, outs, ahead=(), smem=(), scratch=(), passed=()):
    vmem = pl.BlockSpec(memory_space=pltpu.VMEM)
    anywhere = pl.BlockSpec(memory_space=pltpu.HBM)
    n_in = len(smem) + len(args)
    return pl.pallas_call(
        kernel,
        in_specs=[pl.BlockSpec(memory_space=pltpu.SMEM)] * len(smem)
        + [vmem] * len(args)
        + [anywhere] * (len(passed) + len(ahead)),
        out_specs=[vmem] * len(outs) + [anywhere] * len(passed),
        out_shape=list(outs) + [jax.ShapeDtypeStruct(v.shape, v.dtype) for v in passed],
        input_output_aliases={n_in + i: len(outs) + i for i in range(len(passed))},
        scratch_shapes=list(scratch),
        compiler_params=pltpu.CompilerParams(vmem_limit_bytes=48 * 1024 * 1024),
        cost_estimate=pl.CostEstimate(flops=10**9, bytes_accessed=4 * 10**6, transcendentals=0),
        name=name,
    )(*smem, *args, *passed, *ahead)


norm_eps = 1e-05


def norm_rows(values):
    center = values - jnp.mean(values, axis=1, keepdims=True)
    scale = lax.rsqrt(jnp.mean(center * center, axis=1, keepdims=True) + norm_eps)
    return center * scale, scale


def norm_back(grad, xhat, scale, gain):
    dx = grad * gain
    return scale * (
        dx - jnp.mean(dx, axis=1, keepdims=True) - xhat * jnp.mean(dx * xhat, axis=1, keepdims=True)
    )


ROWS = 128


def enter_kernel(dealt_ref, gain_ref, bias_ref, *rest):
    x_ref, n_ref = rest[-2:]
    width = x_ref.shape[1]
    for i in range(x_ref.shape[0] // ROWS):
        rows = slice(i * ROWS, (i + 1) * ROWS)
        x = dealt_ref[:, :, rows].reshape(width, ROWS).astype(jnp.float32).T
        x_ref[rows, :] = x.astype(jnp.bfloat16)
        n_ref[rows, :] = (norm_rows(x)[0] * gain_ref[...] + bias_ref[...]).astype(jnp.bfloat16)


def turn_kernel(z_ref, d0, d1, d2, d3, *rest):
    out_ref, turned = rest[2], rest[-1]
    for d, part in enumerate((d0, d1, d2, d3)):
        turned[z_ref[0] ^ d] = part[...]
    for i in range(out_ref.shape[0] // ROWS):
        rows = slice(i * ROWS, (i + 1) * ROWS)
        out_ref[rows, :] = turned[:, :, rows].reshape(out_ref.shape[1], ROWS).astype(jnp.float32).T.astype(jnp.bfloat16)


def pick_kernel(which_ref, own_ref, got_ref, *rest):
    out_ref = rest[-1]
    rows = pl.ds(pl.multiple_of(which_ref[1] * out_ref.shape[0], 16), out_ref.shape[0])

    @pl.when(which_ref[0] == 1)
    def _():
        out_ref[...] = own_ref[rows, :]

    @pl.when(which_ref[0] == 0)
    def _():
        out_ref[...] = got_ref[rows, :]


def middle_kernel(x_ref, near_ref, got_ref, gain_ref, bias_ref, *rest):
    resid_ref, n_ref = rest[-2:]
    for i in range(x_ref.shape[0] // ROWS):
        rows = slice(i * ROWS, (i + 1) * ROWS)
        resid = x_ref[rows, :].astype(jnp.float32) + near_ref[rows, :] + got_ref[rows, :].astype(jnp.float32)
        resid_ref[rows, :] = resid
        xhat = norm_rows(resid.astype(jnp.bfloat16).astype(jnp.float32))[0]
        n_ref[rows, :] = (xhat * gain_ref[...] + bias_ref[...]).astype(jnp.bfloat16)


def middle_back_kernel(own_ref, got_ref, resid_ref, dy_ref, gain_ref, *rest):
    d_ref, low_ref, vec_ref = rest[-3:]
    total = None
    for i in range(own_ref.shape[0] // ROWS):
        rows = slice(i * ROWS, (i + 1) * ROWS)
        grad = own_ref[rows, :] + got_ref[rows, :].astype(jnp.float32)
        xhat, scale = norm_rows(resid_ref[rows, :].astype(jnp.bfloat16).astype(jnp.float32))
        sums = [jnp.sum(grad * xhat, axis=0, keepdims=True), jnp.sum(grad, axis=0, keepdims=True)]
        total = sums if total is None else [a + b for a, b in zip(total, sums)]
        d = dy_ref[rows, :].astype(jnp.float32) + norm_back(grad, xhat, scale, gain_ref[...])
        d_ref[rows, :] = d
        low_ref[rows, :] = d.astype(jnp.bfloat16)
    vec_ref[0:1, :] = total[0]
    vec_ref[1:2, :] = total[1]


def block_kernel(resid_ref, own_ref, got_ref, *rest):
    out_ref = rest[-1]
    parts, quarter, _ = out_ref.shape
    for i in range(own_ref.shape[0] // ROWS):
        rows = slice(i * ROWS, (i + 1) * ROWS)
        out = resid_ref[rows, :] + own_ref[rows, :] + got_ref[rows, :].astype(jnp.float32)
        out_ref[:, :, rows] = out.T.astype(jnp.bfloat16).reshape(parts, quarter, ROWS)


def leave_kernel(near_ref, got_ref, x_ref, d_ref, gain_ref, vec_ref, *rest):
    out_ref = rest[-1]
    parts, quarter = out_ref.shape[0], near_ref.shape[1] // out_ref.shape[0]
    total = None
    for i in range(near_ref.shape[0] // ROWS):
        rows = slice(i * ROWS, (i + 1) * ROWS)
        grad = near_ref[rows, :] + got_ref[rows, :].astype(jnp.float32)
        xhat, scale = norm_rows(x_ref[rows, :].astype(jnp.float32))
        sums = [jnp.sum(grad * xhat, axis=0, keepdims=True), jnp.sum(grad, axis=0, keepdims=True)]
        total = sums if total is None else [a + b for a, b in zip(total, sums)]
        out = d_ref[rows, :] + norm_back(grad, xhat, scale, gain_ref[...])
        out_ref[:, :quarter, rows] = out.T.astype(jnp.bfloat16).reshape(parts, quarter, ROWS)
    vec = jnp.concatenate(total + [vec_ref[0:1, :], vec_ref[1:2, :]], axis=0)
    high = vec.astype(jnp.bfloat16).astype(jnp.float32)
    both = jnp.concatenate([high, vec - high], axis=0)
    tail = out_ref.shape[1] - quarter
    for k in range(parts):
        mine = both[:, k * quarter:(k + 1) * quarter]
        mine = jnp.concatenate([mine, jnp.zeros((8, out_ref.shape[2] - quarter), jnp.float32)], axis=1)
        mine = jnp.concatenate([mine, jnp.zeros((tail - 8, out_ref.shape[2]), jnp.float32)], axis=0)
        out_ref[k, quarter:, :] = mine.astype(jnp.bfloat16)


def sum_kernel(a, b, c, d, *rest, out_at):
    total = a[...].astype(jnp.float32) + b[...].astype(jnp.float32) + c[...].astype(jnp.float32) + d[...].astype(jnp.float32)
    rest[out_at][...] = total.astype(jnp.bfloat16)


def split_kernel(both_ref, a_ref, b_ref):
    cut = a_ref.shape[1]
    a_ref[...] = both_ref[:, :cut, :].astype(jnp.float32)
    b_ref[...] = both_ref[:, cut:, :].astype(jnp.float32)


def sum_slices_kernel(a, *rest):
    rest[-2][...] = jnp.sum(a[...].astype(jnp.float32), axis=0).astype(jnp.bfloat16)


def sum_four(pieces, name, ahead=(), passed=()):
    out = [jax.ShapeDtypeStruct(pieces[0].shape, jnp.bfloat16)]
    at = len(passed) + len(ahead)
    return call(partial(sum_kernel, out_at=at), name, pieces, out, ahead=ahead, passed=passed)


def own_group(i):
    return (i & 3) // 2 == (i >> 2) & 1


def far_group(i):
    return not own_group(i)


def shards(
    activations, segment_ids, block_lists, feature_proj, input_norm_gain, input_norm_bias, qkv_weight,
    out_weight, middle_norm_gain, middle_norm_bias, up_weight, down_weight, out_grad,
):
    rows_n, heads_n = lax.axis_size("row"), lax.axis_size("head")
    total = rows_n * heads_n
    r, z = lax.axis_index("row"), lax.axis_index("head")
    c, p = r % 2, (r // 2) % 4
    groups = rows_n // 8
    pairs = [[2 * i, 2 * i + 1] for i in range(rows_n // 2)]
    planes = [[8 * g + i for i in range(8)] for g in range(groups)]
    quads = [[8 * g + 2 * i + k for i in range(4)] for g in range(groups) for k in range(2)]
    width = input_norm_gain.shape[0]
    quarter = width // heads_n
    seq_count, length = segment_ids.shape
    half = length // 2
    lists_here = block_lists.shape[1]
    bf16, f32 = jnp.bfloat16, jnp.float32
    local = (z // 2) == c
    par = z % 2

    def move(v, mask, only=None):
        moves = [(i, i ^ mask) for i in range(total) if only is None or only(i)]
        return lax.ppermute(v, ("row", "head"), moves)

    def later(i, dep):
        one = lax.slice(dep, (0,) * dep.ndim, (1,) * dep.ndim).reshape(())
        return i + (one != one).astype(jnp.int32)

    def deal_z(v):
        return lax.all_to_all(v, "head", 0, 0, tiled=True)

    def tied(v, dep):
        one = lax.slice(dep, (0,) * dep.ndim, (1,) * dep.ndim).reshape(())
        return v + (one != one).astype(v.dtype)

    def deal(v, side):
        v = v.T

        def token_half(k):
            return jnp.stack([lax.dynamic_slice_in_dim(v, s * length + k * half, half, 1) for s in range(seq_count)])

        keep, got = token_half(side), move(token_half(1 - side), 4)
        return jnp.concatenate([jnp.where(side == 0, keep, got), jnp.where(side == 0, got, keep)], 0)

    def collect(v):
        v = v.reshape(2, seq_count, quarter, half)
        keep = lax.dynamic_index_in_dim(v, c, 0, keepdims=False)
        got = move(lax.dynamic_index_in_dim(v, 1 - c, 0, keepdims=False), 4)
        low, high = jnp.where(c == 0, keep, got), jnp.where(c == 0, got, keep)
        return jnp.concatenate([w[s] for s in range(seq_count) for w in (low, high)], 1).T

    def fetch_z(mine):
        return [mine] + [move(mine, d, own_group) for d in (1, 2, 3)]

    def choose(got, here):
        return jnp.stack([jnp.where(here, got[0], got[2]), jnp.where(here, got[1], got[3])])

    def fetch_plane(both):
        return [both] + [move(both, 8 * d) for d in (1, 2, 3)]

    def give_z(same, other, ahead, before_slice):
        parts = (same, move(other, 1, own_group), move(same, 2, far_group), move(other, 3, far_group))
        (fin,) = sum_four(parts, "sum_z", ahead=(ahead,))
        if groups > 1:
            fin = lax.psum(fin.astype(f32), "row", axis_index_groups=[[8 * g + i for g in range(groups)] for i in range(8)])
            fin = fin.astype(bf16)
        return call(
            pick_kernel, "pick", (fin, move(fin, 4)), (jax.ShapeDtypeStruct((fin.shape[0] // 2, width), bf16),),
            smem=(jnp.stack([local.astype(jnp.int32), c]),), ahead=(before_slice,),
        )[0]

    def gather_plane(v):
        return lax.all_gather(v, "row", axis=0, axis_index_groups=planes)

    cut = lambda w, n, at: lax.dynamic_slice_in_dim(w, at * n, n, 0)

    aux = jnp.concatenate([block_lists.reshape(seq_count, -1), segment_ids], 1).astype(bf16)
    aux_got = move(aux, 4)
    aux = jnp.where(c == 0, jnp.concatenate([aux, aux_got], 0), jnp.concatenate([aux_got, aux], 0))
    n_list = aux.shape[1] - length
    seg = lax.dynamic_index_in_dim(aux[:, n_list:], z, 0, keepdims=False).astype(jnp.int32)

    four = deal(activations, c)
    gain1, bias1, gain2, bias2 = (
        v.reshape(1, width) for v in (input_norm_gain, input_norm_bias, middle_norm_gain, middle_norm_bias)
    )
    shape_of = jax.ShapeDtypeStruct
    half_low, half_wide = shape_of((half, width), bf16), shape_of((half, width), f32)
    dy_four = deal(out_grad, c)
    x_half, n1_half = call(enter_kernel, "enter", (deal_z(four), gain1, bias1), (half_low, half_low), ahead=(dy_four,))

    n_qkv, n_out = qkv_weight.shape[1] // 4, out_weight.shape[0] // 4
    extra = 16
    rider = aux[:, :n_list].reshape(-1)
    rider = jnp.pad(rider, (0, extra * width - rider.shape[0])).reshape(extra, width)
    p_late = later(p, four)
    mine = [cut(qkv_weight.T, n_qkv, p_late), cut(out_weight, n_out, p_late), rider]
    both = choose(fetch_z(jnp.concatenate(mine, 0)), local)
    lists = both[:, n_qkv + n_out:].reshape(2, -1)[:, :4 * n_list].reshape(2, 4, n_list).astype(jnp.int32)
    lists = lax.dynamic_index_in_dim(lists, z, 1, keepdims=False).reshape((2, lists_here) + block_lists.shape[2:])
    pieces = fetch_plane(both[:, :n_qkv + n_out])
    at = jnp.full((1,), p, jnp.int32)

    n_up, n_hid = width // 8, down_weight.shape[0] // 8
    q8 = later(r % 8, x_half)
    mine = jnp.concatenate([cut(up_weight, n_up, q8), cut(down_weight, n_hid, q8)], 0)
    all_z = lax.all_gather(mine, "head", axis=0).reshape((1, 2, 2) + mine.shape)
    send = [jnp.broadcast_to(all_z[:, :, i], (4, 2) + mine.shape).reshape((8,) + mine.shape) for i in range(2)]
    packs = [lax.all_to_all(v, "row", 0, 0, axis_index_groups=planes, tiled=True) for v in send]

    shift = c * half
    seg = lax.dynamic_slice_in_dim(jnp.concatenate([seg, seg]), shift, length, 0)
    hits = []
    for own in lists:
        own = lax.dynamic_slice_in_dim(jnp.concatenate([own, own], 1), shift // BLK, length // BLK, 1)
        hit = hit_lanes(own, length)
        hits.append(lax.dynamic_slice_in_dim(jnp.concatenate([hit, hit], 2), shift, length, 2))

    n1 = (n1_half, move(n1_half, 4))
    att = [attn_fwd(at, *n1, pieces, 0, seg, hits[0], feature_proj)]
    z_late = z + att[0][-1][0]
    dy_parts = [lax.dynamic_index_in_dim(dy_four, z_late ^ d, 0, keepdims=False) for d in range(heads_n)]
    dy_got = [move(v, d) if d else v for d, v in enumerate(dy_parts)]
    att.append(attn_fwd(at, *n1, pieces, 1, seg, hits[1], feature_proj, (att[0][0], att[0][6]), (send[0], *dy_parts)))
    heads_out = [v[0] for v in att]
    rinv = [v[1] for v in att]
    feat_q, feat_k, qkv, wq, outw = zip(*(v[-6:-1] for v in att))
    outw = [v.reshape(-1, width) for v in outw]
    dy_half, near, away = call(
        turn_kernel, "turn", dy_got, (half_low,), smem=(z.reshape(1),), passed=att[1][2:4],
        scratch=(pltpu.VMEM((heads_n, quarter, half), bf16),),
    )
    resid, n2_half = call(
        middle_kernel, "middle", (x_half, near, move(away, 4), gain2, bias2), (half_wide, half_low), ahead=(packs[0],)
    )
    n2 = (n2_half, move(n2_half, 4))
    dy = (dy_half, move(dy_half, 4))
    acted, d_pre, dn = mlp_first(n2, dy, packs[0])
    mo, grads = mlp_second(n2, dy, acted, d_pre, packs[0])
    acted, d_pre, dn_own, dn_oth = mlp_first(n2, dy, packs[1], dn, (mo,))
    mo_own, mo_oth, grads = mlp_second(n2, dy, acted, d_pre, packs[1], mo, grads)
    d_resid, d_half, vec2 = call(
        middle_back_kernel, "middle_back", (dn_own, move(dn_oth, 4), resid, dy_half, gain2),
        (half_wide, half_low, shape_of((2, width), f32)),
    )
    (block_send,) = call(
        block_kernel, "block", (resid, mo_own, move(mo_oth, 4)), (shape_of((heads_n, quarter, half), bf16),)
    )
    block_got = deal_z(block_send)
    block_out = collect(block_got)
    d_branch = (d_half, move(d_half, 4))
    grads = lax.psum_scatter(
        grads.reshape(-1, width), "row", scatter_dimension=0, axis_index_groups=quads, tiled=True
    ).reshape(2, 2, -1, width)
    def attn_back(i, late, ahead):
        return attn_bwd(
            at, qkv[i], seg, hits[i], feature_proj, feat_q[i], feat_k[i], rinv[i], heads_out[i], *d_branch, outw[i],
            (*n1, wq[i], *late), ahead,
        )

    back = [attn_back(0, (), (mo_oth,))]
    c_late = later(c + back[0][2][0], block_got)
    keep = lax.dynamic_index_in_dim(grads, c_late, 0, keepdims=False)
    got = move(lax.dynamic_index_in_dim(grads, 1 - c_late, 0, keepdims=False), 4)
    four = jnp.concatenate([jnp.where(c == 0, keep, got), jnp.where(c == 0, got, keep)], 0)
    four_flat = four.reshape(-1, width)
    mlp_slice = mlp_grads = lax.psum_scatter(four_flat, "head", scatter_dimension=0, tiled=True)
    if groups > 1:
        mlp_grads = lax.psum(mlp_grads, "row", axis_index_groups=[[8 * g + i for g in range(groups)] for i in range(8)])

    back.append(attn_back(1, (back[0][1], wq[0]), (block_got, four_flat)))

    def across(pieces):
        return [pieces[0]] + [move(pieces[d], 8 * d) for d in (1, 2, 3)]

    first = lax.all_to_all(back[0][0], "row", 0, 0, axis_index_groups=quads, tiled=True)
    first, *passed = call(
        sum_slices_kernel, "sum_first", (first,), (shape_of(first.shape[1:], bf16),), passed=(mlp_grads,), ahead=(back[1][0],)
    )
    (mlp_grads,) = passed
    pieces, (near, away) = back[1][:4], back[1][4:6]
    mlp_grads = gather_plane(mlp_grads)
    up_grad = mlp_grads[:, :n_up].reshape(width, -1).astype(f32)
    down_grad = mlp_grads[:, n_up:].reshape(-1, width).astype(f32)
    (send,) = call(
        leave_kernel, "leave", (near, move(away, 4), x_half, d_resid, gain1, vec2),
        (shape_of((heads_n, quarter + 16, half), bf16),), ahead=(first,),
    )
    (second,) = sum_four(across(pieces), "sum_second", ahead=(send,))
    got = deal_z(send)
    qkv_slice = give_z(first, second, got, mlp_grads)
    input_grad = collect(got[:, :quarter]).astype(f32)
    vec = jnp.sum(got[:, quarter:quarter + 8, :quarter].astype(f32), 0)
    got = gather_plane(qkv_slice)
    vec = tied(vec[:4] + vec[4:], qkv_slice)
    for mask in (4, 8, 16):
        vec = vec + move(vec, mask)
    if groups > 1:
        vec = lax.psum(vec, "row", axis_index_groups=[[8 * g + i for g in range(groups)] for i in range(8)])
    qkv_grad, out_w_grad = call(
        split_kernel, "split", (got.reshape(4, n_qkv + n_out, width),),
        (shape_of((4, n_qkv, width), f32), shape_of((4, n_out, width), f32)),
    )
    qkv_grad = qkv_grad.reshape(-1, width).T
    out_w_grad = out_w_grad.reshape(-1, width)
    return (
        block_out, input_grad, vec[0], vec[1], qkv_grad, out_w_grad, vec[2], vec[3], up_grad, down_grad,
    )


def solution(mesh):
    return jax.shard_map(
        shards,
        mesh=mesh,
        in_specs=(
            P("row", "head"), P("row", None), P("row", "head", None, None), P(), P(), P(), P(None, "head"),
            P("head", None), P(), P(), P(None, "head"), P("head", None), P("row", "head"),
        ),
        out_specs=(
            P("row", "head"), P("row", "head"), P("head"), P("head"), P(None, "head"), P("head", None),
            P("head"), P("head"), P(None, "head"), P("head", None),
        ),
        check_vma=False,
    )
```

```python
from functools import partial

import math
import jax, jax.numpy as jnp
from jax import lax
from jax.experimental import pallas as pl
from jax.experimental.pallas import tpu as pltpu

BLK = 64
CHUNK = 1024
LOG2E = 1.4426950408889634

def dot(a, b, dims):
    return lax.dot_general(a, b, (dims, ((), ())), preferred_element_type=jnp.float32)

def meets(seg_ref, r0, tq, c0, tk):
    return (seg_ref[0, r0] <= seg_ref[0, c0 + tk - 1]) & (seg_ref[0, c0] <= seg_ref[0, r0 + tq - 1])

def fwd_kernel(at_ref, seg_s, own_ref, oth_ref, segc_ref, segr_ref, hit_ref, proj_ref, *rest, tq, tk, dh, part):
    (out_ref, rinv_ref, *early, done_ref, vext, qf_ref, kf_ref, qkv_ref, w_ref, wo_ref, sems) = rest[-(15 if part == 0 else 17):]
    sums, early = early[:-5], early[-5:]
    done_ref[0] = 0
    cut = w_ref.shape[1]
    slots = [at_ref[0] ^ d for d in range(4)]
    copies = [
        pltpu.make_async_copy(piece.at[part, pl.ds(0, cut), :], w_ref.at[slots[d]], sems.at[0, d])
        for d, piece in enumerate(rest[:4])
    ] + [
        pltpu.make_async_copy(piece.at[part, pl.ds(cut, wo_ref.shape[1]), :], wo_ref.at[slots[d]], sems.at[1, d])
        for d, piece in enumerate(rest[:4])
    ]
    for copy in copies:
        copy.start()
    for copy in copies:
        copy.wait()
    leaving = [
        pltpu.make_async_copy(src, dst, sems.at[2 + i // 4, i % 4])
        for i, (src, dst) in enumerate(zip((qf_ref, kf_ref, qkv_ref, w_ref, wo_ref), early))
    ]
    leaving[3].start()
    leaving[4].start()
    weights = w_ref[...].reshape(qkv_ref.shape[1], own_ref.shape[1])
    for side, n_ref in enumerate((own_ref, oth_ref)):
        half = n_ref.shape[0]
        qkv_ref[side * half:(side + 1) * half, :] = dot(n_ref[...], weights, ((1,), (1,))).astype(jnp.bfloat16)
    length = qkv_ref.shape[0]
    feats = proj_ref.shape[1]
    quarter = dh ** (-0.25)
    nh = qkv_ref.shape[1] // (3 * dh)
    for h in range(nh):
        base = h * 3 * dh
        for j, f_ref in ((0, qf_ref), (1, kf_ref)):
            for r0 in range(0, length, CHUNK):
                rows = slice(r0, r0 + CHUNK)
                t = qkv_ref[rows, base + j * dh: base + (j + 1) * dh]
                lin = dot(t, proj_ref[...], ((1,), (0,)))
                tw = t.astype(jnp.float32)
                sq = jnp.sum(tw * tw, axis=1, keepdims=True) * (0.5 * quarter * quarter * LOG2E) + 0.5 * math.log2(feats)
                f_ref[h, rows, :] = jnp.exp2(lin * (quarter * LOG2E) - sq).astype(jnp.bfloat16)
        v = qkv_ref[:, base + 2 * dh: base + 3 * dh]
        lane = lax.broadcasted_iota(jnp.int32, (length, dh), 1)
        vext[h, :, :] = jnp.concatenate([v, (lane < 1).astype(jnp.bfloat16)], axis=1)

    for copy in leaving[:3]:
        copy.start()

    def q_body(i, _):
        r0 = pl.multiple_of(i * tq, tq)
        qs = [qkv_ref[pl.ds(r0, tq), h * 3 * dh: h * 3 * dh + dh] for h in range(nh)]
        qfs = [qf_ref[h, pl.ds(r0, tq), :] for h in range(nh)]
        segq = segc_ref[pl.ds(r0, tq), :]
        def k_body(j, acc):
            c0 = pl.multiple_of(j * tk, tk)
            same = segq == segr_ref[:, pl.ds(c0, tk)]
            new = []
            for h in range(nh):
                k = qkv_ref[pl.ds(c0, tk), h * 3 * dh + dh: h * 3 * dh + 2 * dh]
                s = dot(qs[h], k, ((1,), (1,)))
                e = jnp.exp2(s * (LOG2E * dh ** -0.5))
                a = dot(qfs[h], kf_ref[h, pl.ds(c0, tk), :], ((1,), (1,)))
                parts = []
                for b in range(tq // BLK):
                    hit = hit_ref[h, pl.ds(i * (tq // BLK) + b, 1), pl.ds(c0, tk)] > 0.5
                    rs = slice(b * BLK, (b + 1) * BLK)
                    parts.append(jnp.where(jnp.broadcast_to(hit, (BLK, tk)), e[rs], a[rs]))
                comb = jnp.where(same, jnp.concatenate(parts, axis=0), 0.0).astype(jnp.bfloat16)
                new.append(acc[h] + dot(comb, vext[h, pl.ds(c0, tk), :], ((1,), (0,))))
            return tuple(new)
        def k_step(j, acc):
            return lax.cond(meets(seg_s, r0, tq, pl.multiple_of(j * tk, tk), tk), lambda a: k_body(j, a), lambda a: a, acc)
        acc = lax.fori_loop(0, length // tk, k_step, tuple(jnp.zeros((tq, 2 * dh), jnp.float32) for _ in range(nh)))
        for h in range(nh):
            rinv = 1.0 / acc[h][:, dh:dh + 1]
            out_ref[pl.ds(r0, tq), h * dh:(h + 1) * dh] = (acc[h][:, :dh] * rinv).astype(jnp.bfloat16)
            rinv_ref[pl.ds(r0, tq), h:h + 1] = rinv
        return 0
    lax.fori_loop(0, length // tq, q_body, 0)

    if part:
        other, w_other = rest[4], rest[5]
        w_first = w_other[...].reshape(out_ref.shape[1], own_ref.shape[1])
        w_out = wo_ref[...].reshape(out_ref.shape[1], own_ref.shape[1])
        add_parts(
            lambda rows: dot(other[rows, :], w_first, ((1,), (0,))) + dot(out_ref[rows, :], w_out, ((1,), (0,))),
            None, sums, length, False,
        )
    for copy in leaving:
        copy.wait()


def add_parts(product, before, sums, length, first):
    half = length // 2
    for side in range(2):
        rows = slice(side * half, (side + 1) * half)
        part = product(rows)
        if first:
            sums[0][rows, :] = part
        else:
            total = part if before is None else part + before[rows, :]
            sums[side][...] = total.astype(sums[side].dtype)


def sum_shapes(length, width, first):
    whole = lambda n, dtype: jax.ShapeDtypeStruct((n, width), dtype)
    return [whole(length, jnp.float32)] if first else [whole(length // 2, jnp.float32), whole(length // 2, jnp.bfloat16)]


def attn_fwd(at, n_own, n_oth, pieces, part, seg, hit, proj, before=(), ahead=(), *, tq=512, tk=256):
    length, width = 2 * n_own.shape[0], n_own.shape[1]
    dh, feats = proj.shape
    heads = hit.shape[0]
    cols = 3 * heads * dh
    seg2 = seg.reshape(1, length)
    bf16 = jnp.bfloat16
    smem = pl.BlockSpec(memory_space=pltpu.SMEM)
    vmem = pl.BlockSpec(memory_space=pltpu.VMEM)
    anywhere = pl.BlockSpec(memory_space=pltpu.HBM)
    early = [
        ((heads, length, feats), bf16), ((heads, length, feats), bf16), ((length, cols), bf16),
        ((4, cols // 4, width), bf16), ((4, heads * dh // 4, width), bf16),
    ]
    sums = sum_shapes(length, width, False) if part else []
    return pl.pallas_call(
        partial(fwd_kernel, tq=tq, tk=tk, dh=dh, part=part),
        in_specs=[smem] * 2 + [vmem] * 6 + [anywhere] * 4 + [vmem] * len(before) + [anywhere] * len(ahead),
        out_specs=[vmem] * (2 + len(sums)) + [anywhere] * 5 + [smem],
        out_shape=[jax.ShapeDtypeStruct((length, heads * dh), bf16), jax.ShapeDtypeStruct((length, 8), jnp.float32)]
        + sums
        + [jax.ShapeDtypeStruct(*v) for v in early]
        + [jax.ShapeDtypeStruct((1,), jnp.int32)],
        scratch_shapes=[pltpu.VMEM((heads, length, 2 * dh), bf16)]
        + [pltpu.VMEM(*v) for v in early]
        + [pltpu.SemaphoreType.DMA((4, 4))],
        compiler_params=pltpu.CompilerParams(vmem_limit_bytes=48 * 1024 * 1024),
        cost_estimate=pl.CostEstimate(flops=27 * 10**9, bytes_accessed=10**7, transcendentals=10**6),
        name="attn_fwd",
    )(at, seg2, n_own, n_oth, seg.reshape(length, 1), seg2, hit, proj, *pieces, *before, *ahead)


def bwd_kernel(at_ref, seg_s, qkv_ref, segc_ref, segr_ref, hit_ref, proj_ref, pext_ref, qf_ref, kf_ref, rinv_ref, o_ref,
               d_own, d_oth, w_out, *rest, tq, tk, dh, first):
    n_late = 3 if first else 5
    (*outs, done_ref, dqkv_s, do_ref, grad_s, vext, doext, dq, dk, dv, dqf, dkf, late_sem) = rest[-(14 if first else 18) - n_late:-n_late]
    late = rest[-n_late:]
    n_own, n_oth, w_ref = late[:3]
    arriving = [pltpu.make_async_copy(src, dst, late_sem.at[i]) for i, (src, dst) in enumerate(zip(rest, late))]
    for copy in arriving:
        copy.start()
    dqkv_ref = outs[1] if first else dqkv_s
    done_ref[0] = 0
    length = qkv_ref.shape[0]
    half = length // 2
    quarter = dh ** (-0.25)
    nh = qkv_ref.shape[1] // (3 * dh)
    for side, d_ref in enumerate((d_own, d_oth)):
        do_ref[side * half:(side + 1) * half, :] = dot(d_ref[...], w_out[...], ((1,), (1,))).astype(jnp.bfloat16)
    lane = lax.broadcasted_iota(jnp.int32, (length, dh), 1)
    for h in range(nh):
        base = h * 3 * dh
        v = qkv_ref[:, base + 2 * dh: base + 3 * dh]
        vext[h, :, :] = jnp.concatenate([v, (lane < 2).astype(jnp.bfloat16)], axis=1)
        d_o = do_ref[:, h * dh:(h + 1) * dh].astype(jnp.float32)
        o = o_ref[:, h * dh:(h + 1) * dh].astype(jnp.float32)
        rinv = rinv_ref[:, h:h + 1]
        delta = -jnp.sum(d_o * o, axis=1, keepdims=True) * rinv
        high = delta.astype(jnp.bfloat16).astype(jnp.float32)
        low = delta - high
        tail = jnp.where(lane == 0, high, jnp.where(lane == 1, low, 0.0))
        doext[h, :, :] = jnp.concatenate([d_o * rinv, tail], axis=1).astype(jnp.bfloat16)
    dq[...] = jnp.zeros_like(dq)
    dk[...] = jnp.zeros_like(dk)
    dv[...] = jnp.zeros_like(dv)
    dqf[...] = jnp.zeros_like(dqf)
    dkf[...] = jnp.zeros_like(dkf)

    def q_body(i, _):
        r0 = pl.multiple_of(i * tq, tq)
        rows = pl.ds(r0, tq)
        segq = segc_ref[rows, :]
        def k_body(j, _):
            c0 = pl.multiple_of(j * tk, tk)
            cols = pl.ds(c0, tk)
            same = segq == segr_ref[:, cols]
            for h in range(nh):
                base = h * 3 * dh
                q = qkv_ref[rows, base: base + dh]
                k = qkv_ref[cols, base + dh: base + 2 * dh]
                qf = qf_ref[h, rows, :]
                kf = kf_ref[h, cols, :]
                s = dot(q, k, ((1,), (1,)))
                e = jnp.exp2(s * (LOG2E * dh ** -0.5))
                a = dot(qf, kf, ((1,), (1,)))
                dc = dot(doext[h, rows, :], vext[h, cols, :], ((1,), (1,)))
                dc = jnp.where(same, dc, 0.0)
                combs, dss, das = [], [], []
                for b in range(tq // BLK):
                    hit = hit_ref[h, pl.ds(i * (tq // BLK) + b, 1), cols] > 0.5
                    hit = jnp.broadcast_to(hit, (BLK, tk))
                    rs = slice(b * BLK, (b + 1) * BLK)
                    combs.append(jnp.where(hit, e[rs], a[rs]))
                    dss.append(jnp.where(hit, dc[rs] * e[rs], 0.0))
                    das.append(jnp.where(hit, 0.0, dc[rs]))
                comb = jnp.where(same, jnp.concatenate(combs, axis=0), 0.0).astype(jnp.bfloat16)
                ds = jnp.concatenate(dss, axis=0).astype(jnp.bfloat16)
                da = jnp.concatenate(das, axis=0).astype(jnp.bfloat16)
                dq[h, rows, :] += dot(ds, k, ((1,), (0,)))
                dqf[h, rows, :] += dot(da, kf, ((1,), (0,)))
                dk[h, cols, :] += dot(ds, q, ((0,), (0,)))
                dkf[h, cols, :] += dot(da, qf, ((0,), (0,)))
                dv[h, cols, :] += dot(comb, doext[h, rows, :dh], ((0,), (0,)))
            return 0
        def k_step(j, _):
            @pl.when(meets(seg_s, r0, tq, pl.multiple_of(j * tk, tk), tk))
            def _():
                k_body(j, 0)
            return 0
        lax.fori_loop(0, length // tk, k_step, 0)
        return 0
    lax.fori_loop(0, length // tq, q_body, 0)

    for h in range(nh):
        base = h * 3 * dh
        for j, dt, dfeat, f_ref in ((0, dq, dqf, qf_ref), (1, dk, dkf, kf_ref)):
            for r0 in range(0, length, CHUNK):
                rows = slice(r0, r0 + CHUNK)
                dpre = (dfeat[h, rows, :] * f_ref[h, rows, :].astype(jnp.float32)).astype(jnp.bfloat16)
                thr = dot(dpre, pext_ref[...], ((1,), (0,)))
                t = qkv_ref[rows, base + j * dh: base + (j + 1) * dh].astype(jnp.float32)
                g = dt[h, rows, :] * dh ** -0.5 + quarter * thr[:, :dh] - (quarter * quarter) * t * thr[:, dh:dh + 1]
                dqkv_ref[rows, base + j * dh: base + (j + 1) * dh] = g.astype(jnp.bfloat16)
        dqkv_ref[:, base + 2 * dh: base + 3 * dh] = dv[h].astype(jnp.bfloat16)

    for copy in arriving:
        copy.wait()
    if not first:
        dqkv_first, w_first = late[3:]
        weights = w_ref[...].reshape(qkv_ref.shape[1], n_own.shape[1])
        weights_first = w_first[...].reshape(qkv_ref.shape[1], n_own.shape[1])
        add_parts(
            lambda rows: dot(dqkv_first[rows, :], weights_first, ((1,), (0,))) + dot(dqkv_ref[rows, :], weights, ((1,), (0,))),
            None, outs[4:], length, False,
        )

    tn = ((0,), (0,))
    cut = w_ref.shape[1]
    grad = dot(dqkv_ref[:half, :], n_own[...], tn) + dot(dqkv_ref[half:, :], n_oth[...], tn)
    grad_s[:, :cut, :] = grad.astype(jnp.bfloat16).reshape(4, cut, n_own.shape[1])
    out = dot(o_ref[:half, :], d_own[...], tn) + dot(o_ref[half:, :], d_oth[...], tn)
    grad_s[:, cut:, :] = out.astype(jnp.bfloat16).reshape(4, o_ref.shape[1] // 4, n_own.shape[1])
    if first:
        outs[0][...] = grad_s[...]
    else:
        for d in range(4):
            outs[d][...] = grad_s[at_ref[0] ^ d]


def attn_bwd(at, qkv, seg, hit, proj, qf, kf, rinv, o, d_own, d_oth, w_out, late, ahead=(), *, tq=512, tk=256):
    length = qkv.shape[0]
    dh, feats = proj.shape
    width = d_own.shape[1]
    heads = qkv.shape[1] // (3 * dh)
    seg2 = seg.reshape(1, length)
    pext = jnp.concatenate([proj.T, jnp.ones((feats, 1), proj.dtype), jnp.zeros((feats, dh - 1), proj.dtype)], axis=1)
    f32, bf16 = jnp.float32, jnp.bfloat16
    smem = pl.BlockSpec(memory_space=pltpu.SMEM)
    vmem = pl.BlockSpec(memory_space=pltpu.VMEM)
    anywhere = pl.BlockSpec(memory_space=pltpu.HBM)
    first = len(late) == 3
    piece = jax.ShapeDtypeStruct(((qkv.shape[1] + o.shape[1]) // 4, width), bf16)
    if first:
        outs = [jax.ShapeDtypeStruct((4,) + piece.shape, bf16), jax.ShapeDtypeStruct(qkv.shape, bf16)]
    else:
        outs = [piece] * 4 + sum_shapes(length, width, False)
    return pl.pallas_call(
        partial(bwd_kernel, tq=tq, tk=tk, dh=dh, first=first),
        in_specs=[smem] * 2 + [vmem] * 13 + [anywhere] * (len(late) + len(ahead)),
        out_specs=[vmem] * len(outs) + [smem],
        out_shape=outs + [jax.ShapeDtypeStruct((1,), jnp.int32)],
        scratch_shapes=[
            pltpu.VMEM((16, 128) if first else qkv.shape, bf16),
            pltpu.VMEM(o.shape, bf16),
            pltpu.VMEM((4,) + piece.shape, bf16),
            pltpu.VMEM((heads, length, 2 * dh), bf16),
            pltpu.VMEM((heads, length, 2 * dh), bf16),
            pltpu.VMEM((heads, length, dh), f32),
            pltpu.VMEM((heads, length, dh), f32),
            pltpu.VMEM((heads, length, dh), f32),
            pltpu.VMEM((heads, length, feats), f32),
            pltpu.VMEM((heads, length, feats), f32),
            pltpu.SemaphoreType.DMA((5,)),
        ]
        + [pltpu.VMEM(v.shape, v.dtype) for v in late],
        compiler_params=pltpu.CompilerParams(vmem_limit_bytes=56 * 1024 * 1024),
        cost_estimate=pl.CostEstimate(flops=42 * 10**9, bytes_accessed=2 * 10**7, transcendentals=10**6),
        name="attn_bwd",
    )(at, seg2, qkv, seg.reshape(length, 1), seg2, hit, proj, pext, qf, kf, rinv, o, d_own, d_oth, w_out, *late, *ahead)


def hit_lanes(lists, length):
    nb = lists.shape[1]
    ids = lax.broadcasted_iota(jnp.int32, (1, 1, length), 2) // BLK
    out = lists[:, :, 0:1] == ids
    for s in range(1, lists.shape[2]):
        out = out | (lists[:, :, s:s + 1] == ids)
    return out.astype(jnp.float32)

from jax.sharding import PartitionSpec as P


def gelu_pair(u):
    mag = jnp.abs(u)
    t = 1.0 / (1.0 + (0.3275911 * 0.7071067811865476) * mag)
    bell = jnp.exp2(u * u * (-0.5 * LOG2E))
    poly = t * (0.127414796 + t * (-0.142248368 + t * (0.7107068705 + t * (-0.7265760135 + t * 0.5307027145))))
    tail = poly * bell
    cdf = jnp.where(u >= 0.0, 1.0 - tail, tail)
    return u * cdf, cdf + u * bell * 0.3989422804014327


def mlp_kernel(n_own, n_oth, dy_own, dy_oth, w_ref, *rest, first):
    act_ref, dpre_ref, *sums = rest[-(3 if first else 4):]
    half, width = n_own.shape
    piece = w_ref.shape[1] // 2
    hid = act_ref.shape[1]
    up = w_ref[:, :piece, :].reshape(width, hid)
    down = w_ref[:, piece:, :].reshape(hid, width)
    for side, (n_ref, dy_ref) in enumerate(((n_own, dy_own), (n_oth, dy_oth))):
        rs = slice(side * half, (side + 1) * half)
        pre = dot(n_ref[...], up, ((1,), (0,)))
        d_act = dot(dy_ref[...], down, ((1,), (1,)))
        act, slope = gelu_pair(pre)
        d_pre = (d_act * slope).astype(jnp.bfloat16)
        act_ref[rs, :] = act.astype(jnp.bfloat16)
        dpre_ref[rs, :] = d_pre
        part = dot(d_pre, up, ((1,), (1,)))
        if first:
            sums[0][rs, :] = part
        else:
            sums[side][...] = (part + rest[0][rs, :]).astype(sums[side].dtype)


def mlp_first(n2, dy, pack, before=None, ahead=()):
    tokens, width = 2 * n2[0].shape[0], n2[0].shape[1]
    hid = pack.shape[0] * pack.shape[1] // 2
    bf16, f32 = jnp.bfloat16, jnp.float32
    first = before is None
    vmem = pl.BlockSpec(memory_space=pltpu.VMEM)
    return pl.pallas_call(
        partial(mlp_kernel, first=first),
        in_specs=[vmem] * (5 if first else 6) + [pl.BlockSpec(memory_space=pltpu.HBM)] * len(ahead),
        out_specs=[vmem] * (3 if first else 4),
        out_shape=[jax.ShapeDtypeStruct((tokens, hid), bf16)] * 2 + sum_shapes(tokens, width, first),
        compiler_params=pltpu.CompilerParams(vmem_limit_bytes=48 * 1024 * 1024),
        cost_estimate=pl.CostEstimate(flops=2 * 10**9, bytes_accessed=2 * 10**6, transcendentals=10**6),
        name="mlp_first",
    )(*n2, *dy, pack, *(() if first else (before,)), *ahead)


def mlp_grad_kernel(n_own, n_oth, dy_own, dy_oth, act_ref, dpre_ref, w_ref, *rest, first):
    *sums, grad_ref = rest[-(2 if first else 3):]
    half, width = n_own.shape
    piece = w_ref.shape[1] // 2
    hid = act_ref.shape[1]
    down = w_ref[:, piece:, :].reshape(hid, width)
    tn = ((0,), (0,))
    add_parts(lambda rs: dot(act_ref[rs, :], down, ((1,), (0,))), None if first else rest[0], sums, 2 * half, first)
    for j in range(width // (4 * piece)):
        cut = slice(4 * j * piece, 4 * (j + 1) * piece)
        up_g = dot(n_own[:, cut], dpre_ref[:half, :], tn) + dot(n_oth[:, cut], dpre_ref[half:, :], tn)
        grad_ref[2 * j:2 * j + 2, :, 0, :piece, :] = up_g.astype(jnp.bfloat16).reshape(2, 2, piece, hid)
        down_g = dot(act_ref[:half, cut], dy_own[...], tn) + dot(act_ref[half:, cut], dy_oth[...], tn)
        grad_ref[2 * j:2 * j + 2, :, 0, piece:, :] = down_g.astype(jnp.bfloat16).reshape(2, 2, piece, width)


def mlp_second(n2, dy, acted, d_pre, pack, before=None, grads=None):
    tokens, width = 2 * n2[0].shape[0], n2[0].shape[1]
    bf16, f32 = jnp.bfloat16, jnp.float32
    first = before is None
    whole = lambda shape: pl.BlockSpec(shape, lambda i: (0,) * len(shape))
    args = [*n2, *dy, acted, d_pre, pack] + ([] if first else [before])
    sums = sum_shapes(tokens, width, first)
    shape = (4, 2, 2, pack.shape[1], width)
    return pl.pallas_call(
        partial(mlp_grad_kernel, first=first),
        grid=(1,),
        in_specs=[whole(v.shape) for v in args] + [pl.BlockSpec(memory_space=pltpu.HBM)] * (not first),
        out_specs=[whole(v.shape) for v in sums]
        + [pl.BlockSpec((4, 2, 1) + shape[3:], lambda i: (0, 0, 0 if first else 1, 0, 0))],
        out_shape=sums + [jax.ShapeDtypeStruct(shape, bf16)],
        input_output_aliases={} if first else {len(args): len(sums)},
        compiler_params=pltpu.CompilerParams(vmem_limit_bytes=48 * 1024 * 1024),
        cost_estimate=pl.CostEstimate(flops=2 * 10**9, bytes_accessed=2 * 10**6, transcendentals=0),
        name="mlp_second",
    )(*args, *([] if first else [grads]))


def call(kernel, name, args, outs, ahead=(), smem=(), scratch=(), passed=()):
    vmem = pl.BlockSpec(memory_space=pltpu.VMEM)
    anywhere = pl.BlockSpec(memory_space=pltpu.HBM)
    n_in = len(smem) + len(args)
    return pl.pallas_call(
        kernel,
        in_specs=[pl.BlockSpec(memory_space=pltpu.SMEM)] * len(smem)
        + [vmem] * len(args)
        + [anywhere] * (len(passed) + len(ahead)),
        out_specs=[vmem] * len(outs) + [anywhere] * len(passed),
        out_shape=list(outs) + [jax.ShapeDtypeStruct(v.shape, v.dtype) for v in passed],
        input_output_aliases={n_in + i: len(outs) + i for i in range(len(passed))},
        scratch_shapes=list(scratch),
        compiler_params=pltpu.CompilerParams(vmem_limit_bytes=48 * 1024 * 1024),
        cost_estimate=pl.CostEstimate(flops=10**9, bytes_accessed=4 * 10**6, transcendentals=0),
        name=name,
    )(*smem, *args, *passed, *ahead)


norm_eps = 1e-05


def norm_rows(values):
    center = values - jnp.mean(values, axis=1, keepdims=True)
    scale = lax.rsqrt(jnp.mean(center * center, axis=1, keepdims=True) + norm_eps)
    return center * scale, scale


def norm_back(grad, xhat, scale, gain):
    dx = grad * gain
    return scale * (
        dx - jnp.mean(dx, axis=1, keepdims=True) - xhat * jnp.mean(dx * xhat, axis=1, keepdims=True)
    )


ROWS = 128


def enter_kernel(dealt_ref, gain_ref, bias_ref, *rest):
    x_ref, n_ref = rest[-2:]
    width = x_ref.shape[1]
    for i in range(x_ref.shape[0] // ROWS):
        rows = slice(i * ROWS, (i + 1) * ROWS)
        x = dealt_ref[:, :, rows].reshape(width, ROWS).astype(jnp.float32).T
        x_ref[rows, :] = x.astype(jnp.bfloat16)
        n_ref[rows, :] = (norm_rows(x)[0] * gain_ref[...] + bias_ref[...]).astype(jnp.bfloat16)


def turn_kernel(z_ref, d0, d1, d2, d3, *rest):
    out_ref, turned = rest[-4], rest[-1]
    for d, part in enumerate((d0, d1, d2, d3)):
        turned[z_ref[0] ^ d] = part[...]
    for i in range(out_ref.shape[0] // ROWS):
        rows = slice(i * ROWS, (i + 1) * ROWS)
        out_ref[rows, :] = turned[:, :, rows].reshape(out_ref.shape[1], ROWS).astype(jnp.float32).T.astype(jnp.bfloat16)


def pick_kernel(which_ref, own_ref, got_ref, *rest):
    out_ref = rest[-1]
    rows = pl.ds(pl.multiple_of(which_ref[1] * out_ref.shape[0], 16), out_ref.shape[0])

    @pl.when(which_ref[0] == 1)
    def _():
        out_ref[...] = own_ref[rows, :]

    @pl.when(which_ref[0] == 0)
    def _():
        out_ref[...] = got_ref[rows, :]


def middle_kernel(x_ref, near_ref, got_ref, gain_ref, bias_ref, *rest):
    resid_ref, n_ref = rest[-2:]
    for i in range(x_ref.shape[0] // ROWS):
        rows = slice(i * ROWS, (i + 1) * ROWS)
        resid = x_ref[rows, :].astype(jnp.float32) + near_ref[rows, :] + got_ref[rows, :].astype(jnp.float32)
        resid_ref[rows, :] = resid
        xhat = norm_rows(resid.astype(jnp.bfloat16).astype(jnp.float32))[0]
        n_ref[rows, :] = (xhat * gain_ref[...] + bias_ref[...]).astype(jnp.bfloat16)


def middle_back_kernel(own_ref, got_ref, resid_ref, dy_ref, gain_ref, *rest):
    d_ref, low_ref, vec_ref = rest[-3:]
    total = None
    for i in range(own_ref.shape[0] // ROWS):
        rows = slice(i * ROWS, (i + 1) * ROWS)
        grad = own_ref[rows, :] + got_ref[rows, :].astype(jnp.float32)
        xhat, scale = norm_rows(resid_ref[rows, :].astype(jnp.bfloat16).astype(jnp.float32))
        sums = [jnp.sum(grad * xhat, axis=0, keepdims=True), jnp.sum(grad, axis=0, keepdims=True)]
        total = sums if total is None else [a + b for a, b in zip(total, sums)]
        d = dy_ref[rows, :].astype(jnp.float32) + norm_back(grad, xhat, scale, gain_ref[...])
        d_ref[rows, :] = d
        low_ref[rows, :] = d.astype(jnp.bfloat16)
    vec_ref[0:1, :] = total[0]
    vec_ref[1:2, :] = total[1]


def block_kernel(resid_ref, own_ref, got_ref, *rest):
    out_ref = rest[-1]
    parts, quarter, _ = out_ref.shape
    for i in range(own_ref.shape[0] // ROWS):
        rows = slice(i * ROWS, (i + 1) * ROWS)
        out = resid_ref[rows, :] + own_ref[rows, :] + got_ref[rows, :].astype(jnp.float32)
        out_ref[:, :, rows] = out.T.astype(jnp.bfloat16).reshape(parts, quarter, ROWS)


def leave_kernel(near_ref, got_ref, x_ref, d_ref, gain_ref, vec_ref, *rest):
    out_ref = rest[-1]
    parts, quarter = out_ref.shape[0], near_ref.shape[1] // out_ref.shape[0]
    total = None
    for i in range(near_ref.shape[0] // ROWS):
        rows = slice(i * ROWS, (i + 1) * ROWS)
        grad = near_ref[rows, :] + got_ref[rows, :].astype(jnp.float32)
        xhat, scale = norm_rows(x_ref[rows, :].astype(jnp.float32))
        sums = [jnp.sum(grad * xhat, axis=0, keepdims=True), jnp.sum(grad, axis=0, keepdims=True)]
        total = sums if total is None else [a + b for a, b in zip(total, sums)]
        out = d_ref[rows, :] + norm_back(grad, xhat, scale, gain_ref[...])
        out_ref[:, :quarter, rows] = out.T.astype(jnp.bfloat16).reshape(parts, quarter, ROWS)
    vec = jnp.concatenate(total + [vec_ref[0:1, :], vec_ref[1:2, :]], axis=0)
    high = vec.astype(jnp.bfloat16).astype(jnp.float32)
    both = jnp.concatenate([high, vec - high], axis=0)
    tail = out_ref.shape[1] - quarter
    for k in range(parts):
        mine = both[:, k * quarter:(k + 1) * quarter]
        mine = jnp.concatenate([mine, jnp.zeros((8, out_ref.shape[2] - quarter), jnp.float32)], axis=1)
        mine = jnp.concatenate([mine, jnp.zeros((tail - 8, out_ref.shape[2]), jnp.float32)], axis=0)
        out_ref[k, quarter:, :] = mine.astype(jnp.bfloat16)


def sum_kernel(a, b, c, d, *rest, out_at):
    total = a[...].astype(jnp.float32) + b[...].astype(jnp.float32) + c[...].astype(jnp.float32) + d[...].astype(jnp.float32)
    rest[out_at][...] = total.astype(jnp.bfloat16)


def split_kernel(both_ref, a_ref, b_ref):
    cut = a_ref.shape[1]
    a_ref[...] = both_ref[:, :cut, :].astype(jnp.float32)
    b_ref[...] = both_ref[:, cut:, :].astype(jnp.float32)


def sum_slices_kernel(a, *rest):
    rest[-2][...] = jnp.sum(a[...].astype(jnp.float32), axis=0).astype(jnp.bfloat16)


def sum_four(pieces, name, ahead=(), passed=()):
    out = [jax.ShapeDtypeStruct(pieces[0].shape, jnp.bfloat16)]
    at = len(passed) + len(ahead)
    return call(partial(sum_kernel, out_at=at), name, pieces, out, ahead=ahead, passed=passed)


def own_group(i):
    return (i & 3) // 2 == (i >> 2) & 1


def far_group(i):
    return not own_group(i)


def shards(
    activations, segment_ids, block_lists, feature_proj, input_norm_gain, input_norm_bias, qkv_weight,
    out_weight, middle_norm_gain, middle_norm_bias, up_weight, down_weight, out_grad,
):
    rows_n, heads_n = lax.axis_size("row"), lax.axis_size("head")
    total = rows_n * heads_n
    r, z = lax.axis_index("row"), lax.axis_index("head")
    c, p = r % 2, (r // 2) % 4
    groups = rows_n // 8
    pairs = [[2 * i, 2 * i + 1] for i in range(rows_n // 2)]
    planes = [[8 * g + i for i in range(8)] for g in range(groups)]
    quads = [[8 * g + 2 * i + k for i in range(4)] for g in range(groups) for k in range(2)]
    width = input_norm_gain.shape[0]
    quarter = width // heads_n
    seq_count, length = segment_ids.shape
    half = length // 2
    lists_here = block_lists.shape[1]
    bf16, f32 = jnp.bfloat16, jnp.float32
    local = (z // 2) == c
    par = z % 2

    def move(v, mask, only=None):
        moves = [(i, i ^ mask) for i in range(total) if only is None or only(i)]
        return lax.ppermute(v, ("row", "head"), moves)

    def later(i, dep):
        one = lax.slice(dep, (0,) * dep.ndim, (1,) * dep.ndim).reshape(())
        return i + (one != one).astype(jnp.int32)

    def deal_z(v):
        return lax.all_to_all(v, "head", 0, 0, tiled=True)

    def tied(v, dep):
        one = lax.slice(dep, (0,) * dep.ndim, (1,) * dep.ndim).reshape(())
        return v + (one != one).astype(v.dtype)

    def deal(v, side, order):
        v = v.T

        def token_half(k):
            return jnp.stack([lax.dynamic_slice_in_dim(v, s * length + k * half, half, 1) for s in range(seq_count)])

        keep, got = token_half(side), move(token_half(1 - side), 4)
        return jnp.concatenate([jnp.where(order == 0, keep, got), jnp.where(order == 0, got, keep)], 0)

    def collect(v):
        v = v.reshape(2, seq_count, quarter, half)
        keep = lax.dynamic_index_in_dim(v, c, 0, keepdims=False)
        got = move(lax.dynamic_index_in_dim(v, 1 - c, 0, keepdims=False), 4)
        low, high = jnp.where(c == 0, keep, got), jnp.where(c == 0, got, keep)
        return jnp.concatenate([w[s] for s in range(seq_count) for w in (low, high)], 1).T

    def fetch_z(mine):
        return [mine] + [move(mine, d, own_group) for d in (1, 2, 3)]

    def choose(got, here):
        return jnp.stack([jnp.where(here, got[0], got[2]), jnp.where(here, got[1], got[3])])

    def fetch_plane(both):
        return [both] + [move(both, 8 * d) for d in (1, 2, 3)]

    def give_z(same, other, ahead, before_slice):
        parts = (same, move(other, 1, own_group), move(same, 2, far_group), move(other, 3, far_group))
        (fin,) = sum_four(parts, "sum_z", ahead=(ahead,))
        if groups > 1:
            fin = lax.psum(fin.astype(f32), "row", axis_index_groups=[[8 * g + i for g in range(groups)] for i in range(8)])
            fin = fin.astype(bf16)
        return call(
            pick_kernel, "pick", (fin, move(fin, 4)), (jax.ShapeDtypeStruct((fin.shape[0] // 2, width), bf16),),
            smem=(jnp.stack([local.astype(jnp.int32), c]),), ahead=(before_slice,),
        )[0]

    def gather_plane(v):
        return lax.all_gather(v, "row", axis=0, axis_index_groups=planes)

    cut = lambda w, n, at: lax.dynamic_slice_in_dim(w, at * n, n, 0)

    aux = jnp.concatenate([block_lists.reshape(seq_count, -1), segment_ids], 1).astype(bf16)
    aux_got = move(aux, 4)
    aux = jnp.where(c == 0, jnp.concatenate([aux, aux_got], 0), jnp.concatenate([aux_got, aux], 0))
    n_list = aux.shape[1] - length
    seg = lax.dynamic_index_in_dim(aux[:, n_list:], z, 0, keepdims=False).astype(jnp.int32)

    n_qkv, n_out = qkv_weight.shape[1] // 4, out_weight.shape[0] // 4
    extra = 16
    rider = aux[:, :n_list].reshape(-1)
    rider = jnp.pad(rider, (0, extra * width - rider.shape[0])).reshape(extra, width)
    mine = [cut(qkv_weight.T, n_qkv, p), cut(out_weight, n_out, p), rider]
    both = choose(fetch_z(jnp.concatenate(mine, 0)), local)
    lists = both[:, n_qkv + n_out:].reshape(2, -1)[:, :4 * n_list].reshape(2, 4, n_list).astype(jnp.int32)
    lists = lax.dynamic_index_in_dim(lists, z, 1, keepdims=False).reshape((2, lists_here) + block_lists.shape[2:])
    pieces = fetch_plane(both[:, :n_qkv + n_out])
    at = jnp.full((1,), p, jnp.int32)

    four = deal(activations, c, later(c, both))
    gain1, bias1, gain2, bias2 = (
        v.reshape(1, width) for v in (input_norm_gain, input_norm_bias, middle_norm_gain, middle_norm_bias)
    )
    shape_of = jax.ShapeDtypeStruct
    half_low, half_wide = shape_of((half, width), bf16), shape_of((half, width), f32)
    dy_four = deal(out_grad, c, c)
    x_half, n1_half = call(enter_kernel, "enter", (deal_z(four), gain1, bias1), (half_low, half_low), ahead=(dy_four,))

    n_up, n_hid = width // 8, down_weight.shape[0] // 8
    q8 = later(r % 8, x_half)
    mine = jnp.concatenate([cut(up_weight, n_up, q8), cut(down_weight, n_hid, q8)], 0)
    all_z = lax.all_gather(mine, "head", axis=0).reshape((1, 2, 2) + mine.shape)
    send = [jnp.broadcast_to(all_z[:, :, i], (4, 2) + mine.shape).reshape((8,) + mine.shape) for i in range(2)]
    packs = [lax.all_to_all(v, "row", 0, 0, axis_index_groups=planes, tiled=True) for v in send]

    shift = c * half
    seg = lax.dynamic_slice_in_dim(jnp.concatenate([seg, seg]), shift, length, 0)
    hits = []
    for own in lists:
        own = lax.dynamic_slice_in_dim(jnp.concatenate([own, own], 1), shift // BLK, length // BLK, 1)
        hit = hit_lanes(own, length)
        hits.append(lax.dynamic_slice_in_dim(jnp.concatenate([hit, hit], 2), shift, length, 2))

    n1 = (n1_half, move(n1_half, 4))
    att = [attn_fwd(at, *n1, pieces, 0, seg, hits[0], feature_proj)]
    z_late = z + att[0][-1][0]
    dy_parts = [lax.dynamic_index_in_dim(dy_four, z_late ^ d, 0, keepdims=False) for d in range(heads_n)]
    dy_got = [move(v, d) if d else v for d, v in enumerate(dy_parts)]
    att.append(attn_fwd(at, *n1, pieces, 1, seg, hits[1], feature_proj, (att[0][0], att[0][6]), (*send, *dy_parts)))
    heads_out = [v[0] for v in att]
    rinv = [v[1] for v in att]
    feat_q, feat_k, qkv, wq, outw = zip(*(v[-6:-1] for v in att))
    outw = [v.reshape(-1, width) for v in outw]
    dy_half, near, away = call(
        turn_kernel, "turn", dy_got, (half_low,), smem=(z.reshape(1),), passed=att[1][2:4], ahead=(packs[0],),
        scratch=(pltpu.VMEM((heads_n, quarter, half), bf16),),
    )
    resid, n2_half = call(
        middle_kernel, "middle", (x_half, near, move(away, 4), gain2, bias2), (half_wide, half_low),
    )
    n2 = (n2_half, move(n2_half, 4))
    dy = (dy_half, move(dy_half, 4))
    acted, d_pre, dn = mlp_first(n2, dy, packs[0])
    mo, grads = mlp_second(n2, dy, acted, d_pre, packs[0])
    acted, d_pre, dn_own, dn_oth = mlp_first(n2, dy, packs[1], dn, (mo,))
    mo_own, mo_oth, grads = mlp_second(n2, dy, acted, d_pre, packs[1], mo, grads)
    d_resid, d_half, vec2 = call(
        middle_back_kernel, "middle_back", (dn_own, move(dn_oth, 4), resid, dy_half, gain2),
        (half_wide, half_low, shape_of((2, width), f32)),
    )
    (block_send,) = call(
        block_kernel, "block", (resid, mo_own, move(mo_oth, 4)), (shape_of((heads_n, quarter, half), bf16),)
    )
    block_got = deal_z(block_send)
    block_out = collect(block_got)
    d_branch = (d_half, move(d_half, 4))
    grads = lax.psum_scatter(
        grads.reshape(-1, width), "row", scatter_dimension=0, axis_index_groups=quads, tiled=True
    ).reshape(2, 2, -1, width)
    def attn_back(i, late, ahead):
        return attn_bwd(
            at, qkv[i], seg, hits[i], feature_proj, feat_q[i], feat_k[i], rinv[i], heads_out[i], *d_branch, outw[i],
            (*n1, wq[i], *late), ahead,
        )

    back = [attn_back(0, (), (mo_oth,))]
    c_late = later(c + back[0][2][0], block_got)
    keep = lax.dynamic_index_in_dim(grads, c_late, 0, keepdims=False)
    got = move(lax.dynamic_index_in_dim(grads, 1 - c_late, 0, keepdims=False), 4)
    four = jnp.concatenate([jnp.where(c == 0, keep, got), jnp.where(c == 0, got, keep)], 0)
    four_flat = four.reshape(-1, width)
    mlp_slice = mlp_grads = lax.psum_scatter(four_flat, "head", scatter_dimension=0, tiled=True)
    if groups > 1:
        mlp_grads = lax.psum(mlp_grads, "row", axis_index_groups=[[8 * g + i for g in range(groups)] for i in range(8)])

    back.append(attn_back(1, (back[0][1], wq[0]), (block_got, four_flat)))

    def across(pieces):
        return [pieces[0]] + [move(pieces[d], 8 * d) for d in (1, 2, 3)]

    first = lax.all_to_all(back[0][0], "row", 0, 0, axis_index_groups=quads, tiled=True)
    first, *passed = call(
        sum_slices_kernel, "sum_first", (first,), (shape_of(first.shape[1:], bf16),), passed=(mlp_grads,), ahead=(back[1][0],)
    )
    (mlp_grads,) = passed
    pieces, (near, away) = back[1][:4], back[1][4:6]
    mlp_grads = gather_plane(mlp_grads)
    up_grad = mlp_grads[:, :n_up].reshape(width, -1).astype(f32)
    down_grad = mlp_grads[:, n_up:].reshape(-1, width).astype(f32)
    (send,) = call(
        leave_kernel, "leave", (near, move(away, 4), x_half, d_resid, gain1, vec2),
        (shape_of((heads_n, quarter + 16, half), bf16),), ahead=(first,),
    )
    (second,) = sum_four(across(pieces), "sum_second", ahead=(send,))
    got = deal_z(send)
    qkv_slice = give_z(first, second, got, mlp_grads)
    input_grad = collect(got[:, :quarter]).astype(f32)
    vec = jnp.sum(got[:, quarter:quarter + 8, :quarter].astype(f32), 0)
    got = gather_plane(qkv_slice)
    vec = tied(vec[:4] + vec[4:], qkv_slice)
    for mask in (4, 8, 16):
        vec = vec + move(vec, mask)
    if groups > 1:
        vec = lax.psum(vec, "row", axis_index_groups=[[8 * g + i for g in range(groups)] for i in range(8)])
    qkv_grad, out_w_grad = call(
        split_kernel, "split", (got.reshape(4, n_qkv + n_out, width),),
        (shape_of((4, n_qkv, width), f32), shape_of((4, n_out, width), f32)),
    )
    qkv_grad = qkv_grad.reshape(-1, width).T
    out_w_grad = out_w_grad.reshape(-1, width)
    return (
        block_out, input_grad, vec[0], vec[1], qkv_grad, out_w_grad, vec[2], vec[3], up_grad, down_grad,
    )


def solution(mesh):
    return jax.shard_map(
        shards,
        mesh=mesh,
        in_specs=(
            P("row", "head"), P("row", None), P("row", "head", None, None), P(), P(), P(), P(None, "head"),
            P("head", None), P(), P(), P(None, "head"), P("head", None), P("row", "head"),
        ),
        out_specs=(
            P("row", "head"), P("row", "head"), P("head"), P("head"), P(None, "head"), P("head", None),
            P("head"), P("head"), P(None, "head"), P("head", None),
        ),
        check_vma=False,
    )
```

```python
from functools import partial

import math
import jax, jax.numpy as jnp
from jax import lax
from jax.experimental import pallas as pl
from jax.experimental.pallas import tpu as pltpu

BLK = 64
CHUNK = 1024
LOG2E = 1.4426950408889634

def dot(a, b, dims):
    return lax.dot_general(a, b, (dims, ((), ())), preferred_element_type=jnp.float32)

def meets(seg_ref, r0, tq, c0, tk):
    return (seg_ref[0, r0] <= seg_ref[0, c0 + tk - 1]) & (seg_ref[0, c0] <= seg_ref[0, r0 + tq - 1])

def fwd_kernel(at_ref, seg_s, own_ref, oth_ref, segc_ref, segr_ref, hit_ref, proj_ref, *rest, tq, tk, dh, part):
    (out_ref, rinv_ref, *early, done_ref, vext, qf_ref, kf_ref, qkv_ref, w_ref, wo_ref, sems) = rest[-(15 if part == 0 else 17):]
    sums, early = early[:-5], early[-5:]
    done_ref[0] = 0
    cut = w_ref.shape[1]
    slots = [at_ref[0] ^ d for d in range(4)]
    copies = [
        pltpu.make_async_copy(piece.at[part, pl.ds(0, cut), :], w_ref.at[slots[d]], sems.at[0, d])
        for d, piece in enumerate(rest[:4])
    ] + [
        pltpu.make_async_copy(piece.at[part, pl.ds(cut, wo_ref.shape[1]), :], wo_ref.at[slots[d]], sems.at[1, d])
        for d, piece in enumerate(rest[:4])
    ]
    for copy in copies:
        copy.start()
    for copy in copies:
        copy.wait()
    leaving = [
        pltpu.make_async_copy(src, dst, sems.at[2 + i // 4, i % 4])
        for i, (src, dst) in enumerate(zip((qf_ref, kf_ref, qkv_ref, w_ref, wo_ref), early))
    ]
    leaving[3].start()
    leaving[4].start()
    weights = w_ref[...].reshape(qkv_ref.shape[1], own_ref.shape[1])
    for side, n_ref in enumerate((own_ref, oth_ref)):
        half = n_ref.shape[0]
        qkv_ref[side * half:(side + 1) * half, :] = dot(n_ref[...], weights, ((1,), (1,))).astype(jnp.bfloat16)
    length = qkv_ref.shape[0]
    feats = proj_ref.shape[1]
    quarter = dh ** (-0.25)
    nh = qkv_ref.shape[1] // (3 * dh)
    for h in range(nh):
        base = h * 3 * dh
        for j, f_ref in ((0, qf_ref), (1, kf_ref)):
            for r0 in range(0, length, CHUNK):
                rows = slice(r0, r0 + CHUNK)
                t = qkv_ref[rows, base + j * dh: base + (j + 1) * dh]
                lin = dot(t, proj_ref[...], ((1,), (0,)))
                tw = t.astype(jnp.float32)
                sq = jnp.sum(tw * tw, axis=1, keepdims=True) * (0.5 * quarter * quarter * LOG2E) + 0.5 * math.log2(feats)
                f_ref[h, rows, :] = jnp.exp2(lin * (quarter * LOG2E) - sq).astype(jnp.bfloat16)
        v = qkv_ref[:, base + 2 * dh: base + 3 * dh]
        lane = lax.broadcasted_iota(jnp.int32, (length, dh), 1)
        vext[h, :, :] = jnp.concatenate([v, (lane < 1).astype(jnp.bfloat16)], axis=1)

    for copy in leaving[:3]:
        copy.start()

    def q_body(i, _):
        r0 = pl.multiple_of(i * tq, tq)
        qs = [qkv_ref[pl.ds(r0, tq), h * 3 * dh: h * 3 * dh + dh] for h in range(nh)]
        qfs = [qf_ref[h, pl.ds(r0, tq), :] for h in range(nh)]
        segq = segc_ref[pl.ds(r0, tq), :]
        def k_body(j, acc):
            c0 = pl.multiple_of(j * tk, tk)
            same = segq == segr_ref[:, pl.ds(c0, tk)]
            new = []
            for h in range(nh):
                k = qkv_ref[pl.ds(c0, tk), h * 3 * dh + dh: h * 3 * dh + 2 * dh]
                s = dot(qs[h], k, ((1,), (1,)))
                e = jnp.exp2(s * (LOG2E * dh ** -0.5))
                a = dot(qfs[h], kf_ref[h, pl.ds(c0, tk), :], ((1,), (1,)))
                parts = []
                for b in range(tq // BLK):
                    hit = hit_ref[h, pl.ds(i * (tq // BLK) + b, 1), pl.ds(c0, tk)] > 0.5
                    rs = slice(b * BLK, (b + 1) * BLK)
                    parts.append(jnp.where(jnp.broadcast_to(hit, (BLK, tk)), e[rs], a[rs]))
                comb = jnp.where(same, jnp.concatenate(parts, axis=0), 0.0).astype(jnp.bfloat16)
                new.append(acc[h] + dot(comb, vext[h, pl.ds(c0, tk), :], ((1,), (0,))))
            return tuple(new)
        def k_step(j, acc):
            return lax.cond(meets(seg_s, r0, tq, pl.multiple_of(j * tk, tk), tk), lambda a: k_body(j, a), lambda a: a, acc)
        acc = lax.fori_loop(0, length // tk, k_step, tuple(jnp.zeros((tq, 2 * dh), jnp.float32) for _ in range(nh)))
        for h in range(nh):
            rinv = 1.0 / acc[h][:, dh:dh + 1]
            out_ref[pl.ds(r0, tq), h * dh:(h + 1) * dh] = (acc[h][:, :dh] * rinv).astype(jnp.bfloat16)
            rinv_ref[pl.ds(r0, tq), h:h + 1] = rinv
        return 0
    lax.fori_loop(0, length // tq, q_body, 0)

    if part:
        other, w_other = rest[4], rest[5]
        w_first = w_other[...].reshape(out_ref.shape[1], own_ref.shape[1])
        w_out = wo_ref[...].reshape(out_ref.shape[1], own_ref.shape[1])
        add_parts(
            lambda rows: dot(other[rows, :], w_first, ((1,), (0,))) + dot(out_ref[rows, :], w_out, ((1,), (0,))),
            None, sums, length, False,
        )
    for copy in leaving:
        copy.wait()


def add_parts(product, before, sums, length, first):
    half = length // 2
    for side in range(2):
        rows = slice(side * half, (side + 1) * half)
        part = product(rows)
        if first:
            sums[0][rows, :] = part
        else:
            total = part if before is None else part + before[rows, :]
            sums[side][...] = total.astype(sums[side].dtype)


def sum_shapes(length, width, first):
    whole = lambda n, dtype: jax.ShapeDtypeStruct((n, width), dtype)
    return [whole(length, jnp.float32)] if first else [whole(length // 2, jnp.float32), whole(length // 2, jnp.bfloat16)]


def attn_fwd(at, n_own, n_oth, pieces, part, seg, hit, proj, before=(), ahead=(), *, tq=512, tk=512):
    length, width = 2 * n_own.shape[0], n_own.shape[1]
    dh, feats = proj.shape
    heads = hit.shape[0]
    cols = 3 * heads * dh
    seg2 = seg.reshape(1, length)
    bf16 = jnp.bfloat16
    smem = pl.BlockSpec(memory_space=pltpu.SMEM)
    vmem = pl.BlockSpec(memory_space=pltpu.VMEM)
    anywhere = pl.BlockSpec(memory_space=pltpu.HBM)
    early = [
        ((heads, length, feats), bf16), ((heads, length, feats), bf16), ((length, cols), bf16),
        ((4, cols // 4, width), bf16), ((4, heads * dh // 4, width), bf16),
    ]
    sums = sum_shapes(length, width, False) if part else []
    return pl.pallas_call(
        partial(fwd_kernel, tq=tq, tk=tk, dh=dh, part=part),
        in_specs=[smem] * 2 + [vmem] * 6 + [anywhere] * 4 + [vmem] * len(before) + [anywhere] * len(ahead),
        out_specs=[vmem] * (2 + len(sums)) + [anywhere] * 5 + [smem],
        out_shape=[jax.ShapeDtypeStruct((length, heads * dh), bf16), jax.ShapeDtypeStruct((length, 8), jnp.float32)]
        + sums
        + [jax.ShapeDtypeStruct(*v) for v in early]
        + [jax.ShapeDtypeStruct((1,), jnp.int32)],
        scratch_shapes=[pltpu.VMEM((heads, length, 2 * dh), bf16)]
        + [pltpu.VMEM(*v) for v in early]
        + [pltpu.SemaphoreType.DMA((4, 4))],
        compiler_params=pltpu.CompilerParams(vmem_limit_bytes=48 * 1024 * 1024),
        cost_estimate=pl.CostEstimate(flops=27 * 10**9, bytes_accessed=10**7, transcendentals=10**6),
        name="attn_fwd",
    )(at, seg2, n_own, n_oth, seg.reshape(length, 1), seg2, hit, proj, *pieces, *before, *ahead)


def bwd_kernel(at_ref, seg_s, qkv_ref, segc_ref, segr_ref, hit_ref, proj_ref, pext_ref, qf_ref, kf_ref, rinv_ref, o_ref,
               d_own, d_oth, w_out, *rest, tq, tk, dh, first):
    n_late = 3 if first else 5
    (*outs, done_ref, dqkv_s, do_ref, grad_s, vext, doext, dq, dk, dv, dqf, dkf, late_sem) = rest[-(14 if first else 18) - n_late:-n_late]
    late = rest[-n_late:]
    n_own, n_oth, w_ref = late[:3]
    arriving = [pltpu.make_async_copy(src, dst, late_sem.at[i]) for i, (src, dst) in enumerate(zip(rest, late))]
    for copy in arriving:
        copy.start()
    dqkv_ref = outs[1] if first else dqkv_s
    done_ref[0] = 0
    length = qkv_ref.shape[0]
    half = length // 2
    quarter = dh ** (-0.25)
    nh = qkv_ref.shape[1] // (3 * dh)
    for side, d_ref in enumerate((d_own, d_oth)):
        do_ref[side * half:(side + 1) * half, :] = dot(d_ref[...], w_out[...], ((1,), (1,))).astype(jnp.bfloat16)
    lane = lax.broadcasted_iota(jnp.int32, (length, dh), 1)
    for h in range(nh):
        base = h * 3 * dh
        v = qkv_ref[:, base + 2 * dh: base + 3 * dh]
        vext[h, :, :] = jnp.concatenate([v, (lane < 2).astype(jnp.bfloat16)], axis=1)
        d_o = do_ref[:, h * dh:(h + 1) * dh].astype(jnp.float32)
        o = o_ref[:, h * dh:(h + 1) * dh].astype(jnp.float32)
        rinv = rinv_ref[:, h:h + 1]
        delta = -jnp.sum(d_o * o, axis=1, keepdims=True) * rinv
        high = delta.astype(jnp.bfloat16).astype(jnp.float32)
        low = delta - high
        tail = jnp.where(lane == 0, high, jnp.where(lane == 1, low, 0.0))
        doext[h, :, :] = jnp.concatenate([d_o * rinv, tail], axis=1).astype(jnp.bfloat16)
    dq[...] = jnp.zeros_like(dq)
    dk[...] = jnp.zeros_like(dk)
    dv[...] = jnp.zeros_like(dv)
    dqf[...] = jnp.zeros_like(dqf)
    dkf[...] = jnp.zeros_like(dkf)

    def q_body(i, _):
        r0 = pl.multiple_of(i * tq, tq)
        rows = pl.ds(r0, tq)
        segq = segc_ref[rows, :]
        def k_body(j, _):
            c0 = pl.multiple_of(j * tk, tk)
            cols = pl.ds(c0, tk)
            same = segq == segr_ref[:, cols]
            for h in range(nh):
                base = h * 3 * dh
                q = qkv_ref[rows, base: base + dh]
                k = qkv_ref[cols, base + dh: base + 2 * dh]
                qf = qf_ref[h, rows, :]
                kf = kf_ref[h, cols, :]
                s = dot(q, k, ((1,), (1,)))
                e = jnp.exp2(s * (LOG2E * dh ** -0.5))
                a = dot(qf, kf, ((1,), (1,)))
                dc = dot(doext[h, rows, :], vext[h, cols, :], ((1,), (1,)))
                dc = jnp.where(same, dc, 0.0)
                combs, dss, das = [], [], []
                for b in range(tq // BLK):
                    hit = hit_ref[h, pl.ds(i * (tq // BLK) + b, 1), cols] > 0.5
                    hit = jnp.broadcast_to(hit, (BLK, tk))
                    rs = slice(b * BLK, (b + 1) * BLK)
                    combs.append(jnp.where(hit, e[rs], a[rs]))
                    dss.append(jnp.where(hit, dc[rs] * e[rs], 0.0))
                    das.append(jnp.where(hit, 0.0, dc[rs]))
                comb = jnp.where(same, jnp.concatenate(combs, axis=0), 0.0).astype(jnp.bfloat16)
                ds = jnp.concatenate(dss, axis=0).astype(jnp.bfloat16)
                da = jnp.concatenate(das, axis=0).astype(jnp.bfloat16)
                dq[h, rows, :] += dot(ds, k, ((1,), (0,)))
                dqf[h, rows, :] += dot(da, kf, ((1,), (0,)))
                dk[h, cols, :] += dot(ds, q, ((0,), (0,)))
                dkf[h, cols, :] += dot(da, qf, ((0,), (0,)))
                dv[h, cols, :] += dot(comb, doext[h, rows, :dh], ((0,), (0,)))
            return 0
        def k_step(j, _):
            @pl.when(meets(seg_s, r0, tq, pl.multiple_of(j * tk, tk), tk))
            def _():
                k_body(j, 0)
            return 0
        lax.fori_loop(0, length // tk, k_step, 0)
        return 0
    lax.fori_loop(0, length // tq, q_body, 0)

    for h in range(nh):
        base = h * 3 * dh
        for j, dt, dfeat, f_ref in ((0, dq, dqf, qf_ref), (1, dk, dkf, kf_ref)):
            for r0 in range(0, length, CHUNK):
                rows = slice(r0, r0 + CHUNK)
                dpre = (dfeat[h, rows, :] * f_ref[h, rows, :].astype(jnp.float32)).astype(jnp.bfloat16)
                thr = dot(dpre, pext_ref[...], ((1,), (0,)))
                t = qkv_ref[rows, base + j * dh: base + (j + 1) * dh].astype(jnp.float32)
                g = dt[h, rows, :] * dh ** -0.5 + quarter * thr[:, :dh] - (quarter * quarter) * t * thr[:, dh:dh + 1]
                dqkv_ref[rows, base + j * dh: base + (j + 1) * dh] = g.astype(jnp.bfloat16)
        dqkv_ref[:, base + 2 * dh: base + 3 * dh] = dv[h].astype(jnp.bfloat16)

    for copy in arriving:
        copy.wait()
    if not first:
        dqkv_first, w_first = late[3:]
        weights = w_ref[...].reshape(qkv_ref.shape[1], n_own.shape[1])
        weights_first = w_first[...].reshape(qkv_ref.shape[1], n_own.shape[1])
        add_parts(
            lambda rows: dot(dqkv_first[rows, :], weights_first, ((1,), (0,))) + dot(dqkv_ref[rows, :], weights, ((1,), (0,))),
            None, outs[4:], length, False,
        )

    tn = ((0,), (0,))
    cut = w_ref.shape[1]
    grad = dot(dqkv_ref[:half, :], n_own[...], tn) + dot(dqkv_ref[half:, :], n_oth[...], tn)
    grad_s[:, :cut, :] = grad.astype(jnp.bfloat16).reshape(4, cut, n_own.shape[1])
    out = dot(o_ref[:half, :], d_own[...], tn) + dot(o_ref[half:, :], d_oth[...], tn)
    grad_s[:, cut:, :] = out.astype(jnp.bfloat16).reshape(4, o_ref.shape[1] // 4, n_own.shape[1])
    if first:
        outs[0][...] = grad_s[...]
    else:
        for d in range(4):
            outs[d][...] = grad_s[at_ref[0] ^ d]


def attn_bwd(at, qkv, seg, hit, proj, qf, kf, rinv, o, d_own, d_oth, w_out, late, ahead=(), *, tq=512, tk=256):
    length = qkv.shape[0]
    dh, feats = proj.shape
    width = d_own.shape[1]
    heads = qkv.shape[1] // (3 * dh)
    seg2 = seg.reshape(1, length)
    pext = jnp.concatenate([proj.T, jnp.ones((feats, 1), proj.dtype), jnp.zeros((feats, dh - 1), proj.dtype)], axis=1)
    f32, bf16 = jnp.float32, jnp.bfloat16
    smem = pl.BlockSpec(memory_space=pltpu.SMEM)
    vmem = pl.BlockSpec(memory_space=pltpu.VMEM)
    anywhere = pl.BlockSpec(memory_space=pltpu.HBM)
    first = len(late) == 3
    piece = jax.ShapeDtypeStruct(((qkv.shape[1] + o.shape[1]) // 4, width), bf16)
    if first:
        outs = [jax.ShapeDtypeStruct((4,) + piece.shape, bf16), jax.ShapeDtypeStruct(qkv.shape, bf16)]
    else:
        outs = [piece] * 4 + sum_shapes(length, width, False)
    return pl.pallas_call(
        partial(bwd_kernel, tq=tq, tk=tk, dh=dh, first=first),
        in_specs=[smem] * 2 + [vmem] * 13 + [anywhere] * (len(late) + len(ahead)),
        out_specs=[vmem] * len(outs) + [smem],
        out_shape=outs + [jax.ShapeDtypeStruct((1,), jnp.int32)],
        scratch_shapes=[
            pltpu.VMEM((16, 128) if first else qkv.shape, bf16),
            pltpu.VMEM(o.shape, bf16),
            pltpu.VMEM((4,) + piece.shape, bf16),
            pltpu.VMEM((heads, length, 2 * dh), bf16),
            pltpu.VMEM((heads, length, 2 * dh), bf16),
            pltpu.VMEM((heads, length, dh), f32),
            pltpu.VMEM((heads, length, dh), f32),
            pltpu.VMEM((heads, length, dh), f32),
            pltpu.VMEM((heads, length, feats), f32),
            pltpu.VMEM((heads, length, feats), f32),
            pltpu.SemaphoreType.DMA((5,)),
        ]
        + [pltpu.VMEM(v.shape, v.dtype) for v in late],
        compiler_params=pltpu.CompilerParams(vmem_limit_bytes=56 * 1024 * 1024),
        cost_estimate=pl.CostEstimate(flops=42 * 10**9, bytes_accessed=2 * 10**7, transcendentals=10**6),
        name="attn_bwd",
    )(at, seg2, qkv, seg.reshape(length, 1), seg2, hit, proj, pext, qf, kf, rinv, o, d_own, d_oth, w_out, *late, *ahead)


def hit_lanes(lists, length):
    nb = lists.shape[1]
    ids = lax.broadcasted_iota(jnp.int32, (1, 1, length), 2) // BLK
    out = lists[:, :, 0:1] == ids
    for s in range(1, lists.shape[2]):
        out = out | (lists[:, :, s:s + 1] == ids)
    return out.astype(jnp.float32)

from jax.sharding import PartitionSpec as P


def gelu_pair(u):
    mag = jnp.abs(u)
    t = 1.0 / (1.0 + (0.3275911 * 0.7071067811865476) * mag)
    bell = jnp.exp2(u * u * (-0.5 * LOG2E))
    poly = t * (0.127414796 + t * (-0.142248368 + t * (0.7107068705 + t * (-0.7265760135 + t * 0.5307027145))))
    tail = poly * bell
    cdf = jnp.where(u >= 0.0, 1.0 - tail, tail)
    return u * cdf, cdf + u * bell * 0.3989422804014327


def mlp_kernel(n_own, n_oth, dy_own, dy_oth, w_ref, *rest, first):
    act_ref, dpre_ref, *sums = rest[-(3 if first else 4):]
    half, width = n_own.shape
    piece = w_ref.shape[1] // 2
    hid = act_ref.shape[1]
    up = w_ref[:, :piece, :].reshape(width, hid)
    down = w_ref[:, piece:, :].reshape(hid, width)
    for side, (n_ref, dy_ref) in enumerate(((n_own, dy_own), (n_oth, dy_oth))):
        rs = slice(side * half, (side + 1) * half)
        pre = dot(n_ref[...], up, ((1,), (0,)))
        d_act = dot(dy_ref[...], down, ((1,), (1,)))
        act, slope = gelu_pair(pre)
        d_pre = (d_act * slope).astype(jnp.bfloat16)
        act_ref[rs, :] = act.astype(jnp.bfloat16)
        dpre_ref[rs, :] = d_pre
        part = dot(d_pre, up, ((1,), (1,)))
        if first:
            sums[0][rs, :] = part
        else:
            sums[side][...] = (part + rest[0][rs, :]).astype(sums[side].dtype)


def mlp_first(n2, dy, pack, before=None, ahead=()):
    tokens, width = 2 * n2[0].shape[0], n2[0].shape[1]
    hid = pack.shape[0] * pack.shape[1] // 2
    bf16, f32 = jnp.bfloat16, jnp.float32
    first = before is None
    vmem = pl.BlockSpec(memory_space=pltpu.VMEM)
    return pl.pallas_call(
        partial(mlp_kernel, first=first),
        in_specs=[vmem] * (5 if first else 6) + [pl.BlockSpec(memory_space=pltpu.HBM)] * len(ahead),
        out_specs=[vmem] * (3 if first else 4),
        out_shape=[jax.ShapeDtypeStruct((tokens, hid), bf16)] * 2 + sum_shapes(tokens, width, first),
        compiler_params=pltpu.CompilerParams(vmem_limit_bytes=48 * 1024 * 1024),
        cost_estimate=pl.CostEstimate(flops=2 * 10**9, bytes_accessed=2 * 10**6, transcendentals=10**6),
        name="mlp_first",
    )(*n2, *dy, pack, *(() if first else (before,)), *ahead)


def mlp_grad_kernel(n_own, n_oth, dy_own, dy_oth, act_ref, dpre_ref, *rest):
    grad_ref = rest[-1]
    half, width = n_own.shape
    piece = grad_ref.shape[3] // 2
    hid = act_ref.shape[1]
    tn = ((0,), (0,))
    for j in range(width // (4 * piece)):
        cut = slice(4 * j * piece, 4 * (j + 1) * piece)
        up_g = dot(n_own[:, cut], dpre_ref[:half, :], tn) + dot(n_oth[:, cut], dpre_ref[half:, :], tn)
        grad_ref[2 * j:2 * j + 2, :, 0, :piece, :] = up_g.astype(jnp.bfloat16).reshape(2, 2, piece, hid)
        down_g = dot(act_ref[:half, cut], dy_own[...], tn) + dot(act_ref[half:, cut], dy_oth[...], tn)
        grad_ref[2 * j:2 * j + 2, :, 0, piece:, :] = down_g.astype(jnp.bfloat16).reshape(2, 2, piece, width)


def mlp_second(n2, dy, acted, d_pre, rows, grads=None):
    width = n2[0].shape[1]
    whole = lambda shape: pl.BlockSpec(shape, lambda i: (0,) * len(shape))
    args = [*n2, *dy, acted, d_pre]
    first = grads is None
    shape = (4, 2, 2, rows, width)
    return pl.pallas_call(
        mlp_grad_kernel,
        grid=(1,),
        in_specs=[whole(v.shape) for v in args] + [pl.BlockSpec(memory_space=pltpu.HBM)] * (not first),
        out_specs=pl.BlockSpec((4, 2, 1) + shape[3:], lambda i: (0, 0, 0 if first else 1, 0, 0)),
        out_shape=jax.ShapeDtypeStruct(shape, jnp.bfloat16),
        input_output_aliases={} if first else {len(args): 0},
        compiler_params=pltpu.CompilerParams(vmem_limit_bytes=48 * 1024 * 1024),
        cost_estimate=pl.CostEstimate(flops=2 * 10**9, bytes_accessed=2 * 10**6, transcendentals=0),
        name="mlp_second",
    )(*args, *([] if first else [grads]))


def mlp_out_kernel(act_a, act_b, w_a, w_b, *rest):
    half, width = rest[-1].shape
    piece = w_a.shape[1] // 2
    downs = [w[:, piece:, :].reshape(-1, width) for w in (w_a, w_b)]
    for side, out_ref in enumerate(rest[-2:]):
        rows = slice(side * half, (side + 1) * half)
        total = dot(act_a[rows, :], downs[0], ((1,), (0,))) + dot(act_b[rows, :], downs[1], ((1,), (0,)))
        out_ref[...] = total.astype(out_ref.dtype)


def call(kernel, name, args, outs, ahead=(), smem=(), scratch=(), passed=()):
    vmem = pl.BlockSpec(memory_space=pltpu.VMEM)
    anywhere = pl.BlockSpec(memory_space=pltpu.HBM)
    n_in = len(smem) + len(args)
    return pl.pallas_call(
        kernel,
        in_specs=[pl.BlockSpec(memory_space=pltpu.SMEM)] * len(smem)
        + [vmem] * len(args)
        + [anywhere] * (len(passed) + len(ahead)),
        out_specs=[vmem] * len(outs) + [anywhere] * len(passed),
        out_shape=list(outs) + [jax.ShapeDtypeStruct(v.shape, v.dtype) for v in passed],
        input_output_aliases={n_in + i: len(outs) + i for i in range(len(passed))},
        scratch_shapes=list(scratch),
        compiler_params=pltpu.CompilerParams(vmem_limit_bytes=48 * 1024 * 1024),
        cost_estimate=pl.CostEstimate(flops=10**9, bytes_accessed=4 * 10**6, transcendentals=0),
        name=name,
    )(*smem, *args, *passed, *ahead)


norm_eps = 1e-05


def norm_rows(values):
    center = values - jnp.mean(values, axis=1, keepdims=True)
    scale = lax.rsqrt(jnp.mean(center * center, axis=1, keepdims=True) + norm_eps)
    return center * scale, scale


def norm_back(grad, xhat, scale, gain):
    dx = grad * gain
    return scale * (
        dx - jnp.mean(dx, axis=1, keepdims=True) - xhat * jnp.mean(dx * xhat, axis=1, keepdims=True)
    )


ROWS = 128


def enter_kernel(dealt_ref, gain_ref, bias_ref, *rest):
    x_ref, n_ref = rest[-2:]
    width = x_ref.shape[1]
    for i in range(x_ref.shape[0] // ROWS):
        rows = slice(i * ROWS, (i + 1) * ROWS)
        x = dealt_ref[:, :, rows].reshape(width, ROWS).astype(jnp.float32).T
        x_ref[rows, :] = x.astype(jnp.bfloat16)
        n_ref[rows, :] = (norm_rows(x)[0] * gain_ref[...] + bias_ref[...]).astype(jnp.bfloat16)


def turn_kernel(z_ref, d0, d1, d2, d3, *rest):
    out_ref, turned = rest[-4], rest[-1]
    for d, part in enumerate((d0, d1, d2, d3)):
        turned[z_ref[0] ^ d] = part[...]
    for i in range(out_ref.shape[0] // ROWS):
        rows = slice(i * ROWS, (i + 1) * ROWS)
        out_ref[rows, :] = turned[:, :, rows].reshape(out_ref.shape[1], ROWS).astype(jnp.float32).T.astype(jnp.bfloat16)


def pick_kernel(which_ref, own_ref, got_ref, *rest):
    out_ref = rest[-1]
    rows = pl.ds(pl.multiple_of(which_ref[1] * out_ref.shape[0], 16), out_ref.shape[0])

    @pl.when(which_ref[0] == 1)
    def _():
        out_ref[...] = own_ref[rows, :]

    @pl.when(which_ref[0] == 0)
    def _():
        out_ref[...] = got_ref[rows, :]


def middle_kernel(x_ref, near_ref, got_ref, gain_ref, bias_ref, *rest):
    resid_ref, n_ref = rest[-2:]
    for i in range(x_ref.shape[0] // ROWS):
        rows = slice(i * ROWS, (i + 1) * ROWS)
        resid = x_ref[rows, :].astype(jnp.float32) + near_ref[rows, :] + got_ref[rows, :].astype(jnp.float32)
        resid_ref[rows, :] = resid
        xhat = norm_rows(resid.astype(jnp.bfloat16).astype(jnp.float32))[0]
        n_ref[rows, :] = (xhat * gain_ref[...] + bias_ref[...]).astype(jnp.bfloat16)


def middle_back_kernel(own_ref, got_ref, resid_ref, dy_ref, gain_ref, *rest):
    d_ref, low_ref, vec_ref = rest[-3:]
    total = None
    for i in range(own_ref.shape[0] // ROWS):
        rows = slice(i * ROWS, (i + 1) * ROWS)
        grad = own_ref[rows, :] + got_ref[rows, :].astype(jnp.float32)
        xhat, scale = norm_rows(resid_ref[rows, :].astype(jnp.bfloat16).astype(jnp.float32))
        sums = [jnp.sum(grad * xhat, axis=0, keepdims=True), jnp.sum(grad, axis=0, keepdims=True)]
        total = sums if total is None else [a + b for a, b in zip(total, sums)]
        d = dy_ref[rows, :].astype(jnp.float32) + norm_back(grad, xhat, scale, gain_ref[...])
        d_ref[rows, :] = d
        low_ref[rows, :] = d.astype(jnp.bfloat16)
    vec_ref[0:1, :] = total[0]
    vec_ref[1:2, :] = total[1]


def block_kernel(resid_ref, own_ref, got_ref, *rest):
    out_ref = rest[-1]
    parts, quarter, _ = out_ref.shape
    for i in range(own_ref.shape[0] // ROWS):
        rows = slice(i * ROWS, (i + 1) * ROWS)
        out = resid_ref[rows, :] + own_ref[rows, :] + got_ref[rows, :].astype(jnp.float32)
        out_ref[:, :, rows] = out.T.astype(jnp.bfloat16).reshape(parts, quarter, ROWS)


def leave_kernel(near_ref, got_ref, x_ref, d_ref, gain_ref, vec_ref, *rest):
    out_ref = rest[-1]
    parts, quarter = out_ref.shape[0], near_ref.shape[1] // out_ref.shape[0]
    total = None
    for i in range(near_ref.shape[0] // ROWS):
        rows = slice(i * ROWS, (i + 1) * ROWS)
        grad = near_ref[rows, :] + got_ref[rows, :].astype(jnp.float32)
        xhat, scale = norm_rows(x_ref[rows, :].astype(jnp.float32))
        sums = [jnp.sum(grad * xhat, axis=0, keepdims=True), jnp.sum(grad, axis=0, keepdims=True)]
        total = sums if total is None else [a + b for a, b in zip(total, sums)]
        out = d_ref[rows, :] + norm_back(grad, xhat, scale, gain_ref[...])
        out_ref[:, :quarter, rows] = out.T.astype(jnp.bfloat16).reshape(parts, quarter, ROWS)
    vec = jnp.concatenate(total + [vec_ref[0:1, :], vec_ref[1:2, :]], axis=0)
    high = vec.astype(jnp.bfloat16).astype(jnp.float32)
    both = jnp.concatenate([high, vec - high], axis=0)
    tail = out_ref.shape[1] - quarter
    for k in range(parts):
        mine = both[:, k * quarter:(k + 1) * quarter]
        mine = jnp.concatenate([mine, jnp.zeros((8, out_ref.shape[2] - quarter), jnp.float32)], axis=1)
        mine = jnp.concatenate([mine, jnp.zeros((tail - 8, out_ref.shape[2]), jnp.float32)], axis=0)
        out_ref[k, quarter:, :] = mine.astype(jnp.bfloat16)


def sum_kernel(a, b, c, d, *rest, out_at):
    total = a[...].astype(jnp.float32) + b[...].astype(jnp.float32) + c[...].astype(jnp.float32) + d[...].astype(jnp.float32)
    rest[out_at][...] = total.astype(jnp.bfloat16)


def split_kernel(both_ref, a_ref, b_ref):
    cut = a_ref.shape[1]
    a_ref[...] = both_ref[:, :cut, :].astype(jnp.float32)
    b_ref[...] = both_ref[:, cut:, :].astype(jnp.float32)


def sum_slices_kernel(a, *rest):
    rest[-2][...] = jnp.sum(a[...].astype(jnp.float32), axis=0).astype(jnp.bfloat16)


def sum_four(pieces, name, ahead=(), passed=()):
    out = [jax.ShapeDtypeStruct(pieces[0].shape, jnp.bfloat16)]
    at = len(passed) + len(ahead)
    return call(partial(sum_kernel, out_at=at), name, pieces, out, ahead=ahead, passed=passed)


def own_group(i):
    return (i & 3) // 2 == (i >> 2) & 1


def far_group(i):
    return not own_group(i)


def shards(
    activations, segment_ids, block_lists, feature_proj, input_norm_gain, input_norm_bias, qkv_weight,
    out_weight, middle_norm_gain, middle_norm_bias, up_weight, down_weight, out_grad,
):
    rows_n, heads_n = lax.axis_size("row"), lax.axis_size("head")
    total = rows_n * heads_n
    r, z = lax.axis_index("row"), lax.axis_index("head")
    c, p = r % 2, (r // 2) % 4
    groups = rows_n // 8
    pairs = [[2 * i, 2 * i + 1] for i in range(rows_n // 2)]
    planes = [[8 * g + i for i in range(8)] for g in range(groups)]
    quads = [[8 * g + 2 * i + k for i in range(4)] for g in range(groups) for k in range(2)]
    width = input_norm_gain.shape[0]
    quarter = width // heads_n
    seq_count, length = segment_ids.shape
    half = length // 2
    lists_here = block_lists.shape[1]
    bf16, f32 = jnp.bfloat16, jnp.float32
    local = (z // 2) == c
    par = z % 2

    def move(v, mask, only=None):
        moves = [(i, i ^ mask) for i in range(total) if only is None or only(i)]
        return lax.ppermute(v, ("row", "head"), moves)

    def later(i, dep):
        one = lax.slice(dep, (0,) * dep.ndim, (1,) * dep.ndim).reshape(())
        return i + (one != one).astype(jnp.int32)

    def deal_z(v):
        return lax.all_to_all(v, "head", 0, 0, tiled=True)

    def tied(v, dep):
        one = lax.slice(dep, (0,) * dep.ndim, (1,) * dep.ndim).reshape(())
        return v + (one != one).astype(v.dtype)

    def deal(v, side, order):
        v = v.T

        def token_half(k):
            return jnp.stack([lax.dynamic_slice_in_dim(v, s * length + k * half, half, 1) for s in range(seq_count)])

        keep, got = token_half(side), move(token_half(1 - side), 4)
        return jnp.concatenate([jnp.where(order == 0, keep, got), jnp.where(order == 0, got, keep)], 0)

    def collect(v):
        v = v.reshape(2, seq_count, quarter, half)
        keep = lax.dynamic_index_in_dim(v, c, 0, keepdims=False)
        got = move(lax.dynamic_index_in_dim(v, 1 - c, 0, keepdims=False), 4)
        low, high = jnp.where(c == 0, keep, got), jnp.where(c == 0, got, keep)
        return jnp.concatenate([w[s] for s in range(seq_count) for w in (low, high)], 1).T

    def fetch_z(mine):
        return [mine] + [move(mine, d, own_group) for d in (1, 2, 3)]

    def choose(got, here):
        return jnp.stack([jnp.where(here, got[0], got[2]), jnp.where(here, got[1], got[3])])

    def fetch_plane(both):
        return [both] + [move(both, 8 * d) for d in (1, 2, 3)]

    def give_z(same, other, ahead, before_slice):
        parts = (same, move(other, 1, own_group), move(same, 2, far_group), move(other, 3, far_group))
        (fin,) = sum_four(parts, "sum_z", ahead=(ahead,))
        if groups > 1:
            fin = lax.psum(fin.astype(f32), "row", axis_index_groups=[[8 * g + i for g in range(groups)] for i in range(8)])
            fin = fin.astype(bf16)
        return call(
            pick_kernel, "pick", (fin, move(fin, 4)), (jax.ShapeDtypeStruct((fin.shape[0] // 2, width), bf16),),
            smem=(jnp.stack([local.astype(jnp.int32), c]),), ahead=(before_slice,),
        )[0]

    def gather_plane(v):
        return lax.all_gather(v, "row", axis=0, axis_index_groups=planes)

    cut = lambda w, n, at: lax.dynamic_slice_in_dim(w, at * n, n, 0)

    aux = jnp.concatenate([block_lists.reshape(seq_count, -1), segment_ids], 1).astype(bf16)
    aux_got = move(aux, 4)
    aux = jnp.where(c == 0, jnp.concatenate([aux, aux_got], 0), jnp.concatenate([aux_got, aux], 0))
    n_list = aux.shape[1] - length
    seg = lax.dynamic_index_in_dim(aux[:, n_list:], z, 0, keepdims=False).astype(jnp.int32)

    n_qkv, n_out = qkv_weight.shape[1] // 4, out_weight.shape[0] // 4
    extra = 16
    rider = aux[:, :n_list].reshape(-1)
    rider = jnp.pad(rider, (0, extra * width - rider.shape[0])).reshape(extra, width)
    mine = [cut(qkv_weight.T, n_qkv, p), cut(out_weight, n_out, p), rider]
    both = choose(fetch_z(jnp.concatenate(mine, 0)), local)
    lists = both[:, n_qkv + n_out:].reshape(2, -1)[:, :4 * n_list].reshape(2, 4, n_list).astype(jnp.int32)
    lists = lax.dynamic_index_in_dim(lists, z, 1, keepdims=False).reshape((2, lists_here) + block_lists.shape[2:])
    pieces = fetch_plane(both[:, :n_qkv + n_out])
    at = jnp.full((1,), p, jnp.int32)

    four = deal(activations, c, later(c, both))
    gain1, bias1, gain2, bias2 = (
        v.reshape(1, width) for v in (input_norm_gain, input_norm_bias, middle_norm_gain, middle_norm_bias)
    )
    shape_of = jax.ShapeDtypeStruct
    half_low, half_wide = shape_of((half, width), bf16), shape_of((half, width), f32)
    dy_four = deal(out_grad, c, c)
    x_half, n1_half = call(enter_kernel, "enter", (deal_z(four), gain1, bias1), (half_low, half_low), ahead=(dy_four,))

    n_up, n_hid = width // 8, down_weight.shape[0] // 8
    q8 = later(r % 8, both)
    mine = jnp.concatenate([cut(up_weight, n_up, q8), cut(down_weight, n_hid, q8)], 0)
    all_z = lax.all_gather(mine, "head", axis=0).reshape((1, 2, 2) + mine.shape)
    send = [jnp.broadcast_to(all_z[:, :, i], (4, 2) + mine.shape).reshape((8,) + mine.shape) for i in range(2)]
    packs = [lax.all_to_all(v, "row", 0, 0, axis_index_groups=planes, tiled=True) for v in send]

    shift = c * half
    seg = lax.dynamic_slice_in_dim(jnp.concatenate([seg, seg]), shift, length, 0)
    hits = []
    for own in lists:
        own = lax.dynamic_slice_in_dim(jnp.concatenate([own, own], 1), shift // BLK, length // BLK, 1)
        hit = hit_lanes(own, length)
        hits.append(lax.dynamic_slice_in_dim(jnp.concatenate([hit, hit], 2), shift, length, 2))

    n1 = (n1_half, move(n1_half, 4))
    att = [attn_fwd(at, *n1, pieces, 0, seg, hits[0], feature_proj)]
    z_late = z + att[0][-1][0]
    dy_parts = [lax.dynamic_index_in_dim(dy_four, z_late ^ d, 0, keepdims=False) for d in range(heads_n)]
    dy_got = [move(v, d) if d else v for d, v in enumerate(dy_parts)]
    att.append(attn_fwd(at, *n1, pieces, 1, seg, hits[1], feature_proj, (att[0][0], att[0][6]), (*send, *dy_parts)))
    heads_out = [v[0] for v in att]
    rinv = [v[1] for v in att]
    feat_q, feat_k, qkv, wq, outw = zip(*(v[-6:-1] for v in att))
    outw = [v.reshape(-1, width) for v in outw]
    dy_half, near, away = call(
        turn_kernel, "turn", dy_got, (half_low,), smem=(z.reshape(1),), passed=att[1][2:4], ahead=(packs[0],),
        scratch=(pltpu.VMEM((heads_n, quarter, half), bf16),),
    )
    resid, n2_half = call(
        middle_kernel, "middle", (x_half, near, move(away, 4), gain2, bias2), (half_wide, half_low),
    )
    n2 = (n2_half, move(n2_half, 4))
    dy = (dy_half, move(dy_half, 4))
    acted, d_pre, dn = mlp_first(n2, dy, packs[0])
    grads = mlp_second(n2, dy, acted, d_pre, packs[0].shape[1])
    acted_a = acted
    acted, d_pre, dn_own, dn_oth = mlp_first(n2, dy, packs[1], dn, (grads,))
    grads = mlp_second(n2, dy, acted, d_pre, packs[1].shape[1], grads)
    mo_own, mo_oth = call(
        mlp_out_kernel, "mlp_out", (acted_a, acted, *packs), (half_wide, half_low), ahead=(grads,)
    )
    d_resid, d_half, vec2 = call(
        middle_back_kernel, "middle_back", (dn_own, move(dn_oth, 4), resid, dy_half, gain2),
        (half_wide, half_low, shape_of((2, width), f32)),
    )
    (block_send,) = call(
        block_kernel, "block", (resid, mo_own, move(mo_oth, 4)), (shape_of((heads_n, quarter, half), bf16),)
    )
    block_got = deal_z(block_send)
    block_out = collect(block_got)
    d_branch = (d_half, move(d_half, 4))
    grads = lax.psum_scatter(
        grads.reshape(-1, width), "row", scatter_dimension=0, axis_index_groups=quads, tiled=True
    ).reshape(2, 2, -1, width)
    def attn_back(i, late, ahead):
        return attn_bwd(
            at, qkv[i], seg, hits[i], feature_proj, feat_q[i], feat_k[i], rinv[i], heads_out[i], *d_branch, outw[i],
            (*n1, wq[i], *late), ahead,
        )

    back = [attn_back(0, (), (mo_oth,))]
    c_late = later(c + back[0][2][0], block_got)
    keep = lax.dynamic_index_in_dim(grads, c_late, 0, keepdims=False)
    got = move(lax.dynamic_index_in_dim(grads, 1 - c_late, 0, keepdims=False), 4)
    four = jnp.concatenate([jnp.where(c == 0, keep, got), jnp.where(c == 0, got, keep)], 0)
    four_flat = four.reshape(-1, width)
    mlp_slice = mlp_grads = lax.psum_scatter(four_flat, "head", scatter_dimension=0, tiled=True)
    if groups > 1:
        mlp_grads = lax.psum(mlp_grads, "row", axis_index_groups=[[8 * g + i for g in range(groups)] for i in range(8)])

    back.append(attn_back(1, (back[0][1], wq[0]), (block_got, four_flat)))

    def across(pieces):
        return [pieces[0]] + [move(pieces[d], 8 * d) for d in (1, 2, 3)]

    first = lax.all_to_all(back[0][0], "row", 0, 0, axis_index_groups=quads, tiled=True)
    first, *passed = call(
        sum_slices_kernel, "sum_first", (first,), (shape_of(first.shape[1:], bf16),), passed=(mlp_grads,), ahead=(back[1][0],)
    )
    (mlp_grads,) = passed
    pieces, (near, away) = back[1][:4], back[1][4:6]
    mlp_grads = gather_plane(mlp_grads)
    up_grad = mlp_grads[:, :n_up].reshape(width, -1).astype(f32)
    down_grad = mlp_grads[:, n_up:].reshape(-1, width).astype(f32)
    (send,) = call(
        leave_kernel, "leave", (near, move(away, 4), x_half, d_resid, gain1, vec2),
        (shape_of((heads_n, quarter + 16, half), bf16),), ahead=(first,),
    )
    (second,) = sum_four(across(pieces), "sum_second", ahead=(send,))
    got = deal_z(send)
    qkv_slice = give_z(first, second, got, mlp_grads)
    input_grad = collect(got[:, :quarter]).astype(f32)
    vec = jnp.sum(got[:, quarter:quarter + 8, :quarter].astype(f32), 0)
    got = gather_plane(qkv_slice)
    vec = tied(vec[:4] + vec[4:], qkv_slice)
    for mask in (4, 8, 16):
        vec = vec + move(vec, mask)
    if groups > 1:
        vec = lax.psum(vec, "row", axis_index_groups=[[8 * g + i for g in range(groups)] for i in range(8)])
    qkv_grad, out_w_grad = call(
        split_kernel, "split", (got.reshape(4, n_qkv + n_out, width),),
        (shape_of((4, n_qkv, width), f32), shape_of((4, n_out, width), f32)),
    )
    qkv_grad = qkv_grad.reshape(-1, width).T
    out_w_grad = out_w_grad.reshape(-1, width)
    return (
        block_out, input_grad, vec[0], vec[1], qkv_grad, out_w_grad, vec[2], vec[3], up_grad, down_grad,
    )


def solution(mesh):
    return jax.shard_map(
        shards,
        mesh=mesh,
        in_specs=(
            P("row", "head"), P("row", None), P("row", "head", None, None), P(), P(), P(), P(None, "head"),
            P("head", None), P(), P(), P(None, "head"), P("head", None), P("row", "head"),
        ),
        out_specs=(
            P("row", "head"), P("row", "head"), P("head"), P("head"), P(None, "head"), P("head", None),
            P("head"), P("head"), P(None, "head"), P("head", None),
        ),
        check_vma=False,
    )
```

```python
from functools import partial

import math
import jax, jax.numpy as jnp
from jax import lax
from jax.experimental import pallas as pl
from jax.experimental.pallas import tpu as pltpu

BLK = 64
CHUNK = 1024
LOG2E = 1.4426950408889634

def dot(a, b, dims):
    return lax.dot_general(a, b, (dims, ((), ())), preferred_element_type=jnp.float32)

def meets(seg_ref, r0, tq, c0, tk):
    return (seg_ref[0, r0] <= seg_ref[0, c0 + tk - 1]) & (seg_ref[0, c0] <= seg_ref[0, r0 + tq - 1])

def fwd_kernel(at_ref, seg_s, own_ref, oth_ref, segc_ref, segr_ref, hit_ref, proj_ref, *rest, tq, tk, dh, part):
    (out_ref, rinv_ref, *early, done_ref, vext, qf_ref, kf_ref, qkv_ref, w_ref, wo_ref, sems) = rest[-(15 if part == 0 else 17):]
    sums, early = early[:-5], early[-5:]
    done_ref[0] = 0
    cut = w_ref.shape[1]
    slots = [at_ref[0] ^ d for d in range(4)]
    copies = [
        pltpu.make_async_copy(piece.at[part, pl.ds(0, cut), :], w_ref.at[slots[d]], sems.at[0, d])
        for d, piece in enumerate(rest[:4])
    ] + [
        pltpu.make_async_copy(piece.at[part, pl.ds(cut, wo_ref.shape[1]), :], wo_ref.at[slots[d]], sems.at[1, d])
        for d, piece in enumerate(rest[:4])
    ]
    for copy in copies:
        copy.start()
    for copy in copies:
        copy.wait()
    leaving = [
        pltpu.make_async_copy(src, dst, sems.at[2 + i // 4, i % 4])
        for i, (src, dst) in enumerate(zip((qf_ref, kf_ref, qkv_ref, w_ref, wo_ref), early))
    ]
    leaving[3].start()
    leaving[4].start()
    weights = w_ref[...].reshape(qkv_ref.shape[1], own_ref.shape[1])
    for side, n_ref in enumerate((own_ref, oth_ref)):
        half = n_ref.shape[0]
        qkv_ref[side * half:(side + 1) * half, :] = dot(n_ref[...], weights, ((1,), (1,))).astype(jnp.bfloat16)
    length = qkv_ref.shape[0]
    feats = proj_ref.shape[1]
    quarter = dh ** (-0.25)
    nh = qkv_ref.shape[1] // (3 * dh)
    for h in range(nh):
        base = h * 3 * dh
        for j, f_ref in ((0, qf_ref), (1, kf_ref)):
            for r0 in range(0, length, CHUNK):
                rows = slice(r0, r0 + CHUNK)
                t = qkv_ref[rows, base + j * dh: base + (j + 1) * dh]
                lin = dot(t, proj_ref[...], ((1,), (0,)))
                tw = t.astype(jnp.float32)
                sq = jnp.sum(tw * tw, axis=1, keepdims=True) * (0.5 * quarter * quarter * LOG2E) + 0.5 * math.log2(feats)
                f_ref[h, rows, :] = jnp.exp2(lin * (quarter * LOG2E) - sq).astype(jnp.bfloat16)
        v = qkv_ref[:, base + 2 * dh: base + 3 * dh]
        lane = lax.broadcasted_iota(jnp.int32, (length, dh), 1)
        vext[h, :, :] = jnp.concatenate([v, (lane < 1).astype(jnp.bfloat16)], axis=1)

    for copy in leaving[:3]:
        copy.start()

    def q_body(i, _):
        r0 = pl.multiple_of(i * tq, tq)
        qs = [qkv_ref[pl.ds(r0, tq), h * 3 * dh: h * 3 * dh + dh] for h in range(nh)]
        qfs = [qf_ref[h, pl.ds(r0, tq), :] for h in range(nh)]
        segq = segc_ref[pl.ds(r0, tq), :]
        def k_body(j, acc):
            c0 = pl.multiple_of(j * tk, tk)
            same = segq == segr_ref[:, pl.ds(c0, tk)]
            new = []
            for h in range(nh):
                k = qkv_ref[pl.ds(c0, tk), h * 3 * dh + dh: h * 3 * dh + 2 * dh]
                s = dot(qs[h], k, ((1,), (1,)))
                e = jnp.exp2(s * (LOG2E * dh ** -0.5))
                a = dot(qfs[h], kf_ref[h, pl.ds(c0, tk), :], ((1,), (1,)))
                parts = []
                for b in range(tq // BLK):
                    hit = hit_ref[h, pl.ds(i * (tq // BLK) + b, 1), pl.ds(c0, tk)] > 0.5
                    rs = slice(b * BLK, (b + 1) * BLK)
                    parts.append(jnp.where(jnp.broadcast_to(hit, (BLK, tk)), e[rs], a[rs]))
                comb = jnp.where(same, jnp.concatenate(parts, axis=0), 0.0).astype(jnp.bfloat16)
                new.append(acc[h] + dot(comb, vext[h, pl.ds(c0, tk), :], ((1,), (0,))))
            return tuple(new)
        def k_step(j, acc):
            return lax.cond(meets(seg_s, r0, tq, pl.multiple_of(j * tk, tk), tk), lambda a: k_body(j, a), lambda a: a, acc)
        acc = lax.fori_loop(0, length // tk, k_step, tuple(jnp.zeros((tq, 2 * dh), jnp.float32) for _ in range(nh)))
        for h in range(nh):
            rinv = 1.0 / acc[h][:, dh:dh + 1]
            out_ref[pl.ds(r0, tq), h * dh:(h + 1) * dh] = (acc[h][:, :dh] * rinv).astype(jnp.bfloat16)
            rinv_ref[pl.ds(r0, tq), h:h + 1] = rinv
        return 0
    lax.fori_loop(0, length // tq, q_body, 0)

    if part:
        other, w_other = rest[4], rest[5]
        w_first = w_other[...].reshape(out_ref.shape[1], own_ref.shape[1])
        w_out = wo_ref[...].reshape(out_ref.shape[1], own_ref.shape[1])
        add_parts(
            lambda rows: dot(other[rows, :], w_first, ((1,), (0,))) + dot(out_ref[rows, :], w_out, ((1,), (0,))),
            None, sums, length, False,
        )
    for copy in leaving:
        copy.wait()


def add_parts(product, before, sums, length, first):
    half = length // 2
    for side in range(2):
        rows = slice(side * half, (side + 1) * half)
        part = product(rows)
        if first:
            sums[0][rows, :] = part
        else:
            total = part if before is None else part + before[rows, :]
            sums[side][...] = total.astype(sums[side].dtype)


def sum_shapes(length, width, first):
    whole = lambda n, dtype: jax.ShapeDtypeStruct((n, width), dtype)
    return [whole(length, jnp.float32)] if first else [whole(length // 2, jnp.float32), whole(length // 2, jnp.bfloat16)]


def attn_fwd(at, n_own, n_oth, pieces, part, seg, hit, proj, before=(), ahead=(), *, tq=512, tk=512):
    length, width = 2 * n_own.shape[0], n_own.shape[1]
    dh, feats = proj.shape
    heads = hit.shape[0]
    cols = 3 * heads * dh
    seg2 = seg.reshape(1, length)
    bf16 = jnp.bfloat16
    smem = pl.BlockSpec(memory_space=pltpu.SMEM)
    vmem = pl.BlockSpec(memory_space=pltpu.VMEM)
    anywhere = pl.BlockSpec(memory_space=pltpu.HBM)
    early = [
        ((heads, length, feats), bf16), ((heads, length, feats), bf16), ((length, cols), bf16),
        ((4, cols // 4, width), bf16), ((4, heads * dh // 4, width), bf16),
    ]
    sums = sum_shapes(length, width, False) if part else []
    return pl.pallas_call(
        partial(fwd_kernel, tq=tq, tk=tk, dh=dh, part=part),
        in_specs=[smem] * 2 + [vmem] * 6 + [anywhere] * 4 + [vmem] * len(before) + [anywhere] * len(ahead),
        out_specs=[vmem] * (2 + len(sums)) + [anywhere] * 5 + [smem],
        out_shape=[jax.ShapeDtypeStruct((length, heads * dh), bf16), jax.ShapeDtypeStruct((length, 8), jnp.float32)]
        + sums
        + [jax.ShapeDtypeStruct(*v) for v in early]
        + [jax.ShapeDtypeStruct((1,), jnp.int32)],
        scratch_shapes=[pltpu.VMEM((heads, length, 2 * dh), bf16)]
        + [pltpu.VMEM(*v) for v in early]
        + [pltpu.SemaphoreType.DMA((4, 4))],
        compiler_params=pltpu.CompilerParams(vmem_limit_bytes=48 * 1024 * 1024),
        cost_estimate=pl.CostEstimate(flops=27 * 10**9, bytes_accessed=10**7, transcendentals=10**6),
        name="attn_fwd",
    )(at, seg2, n_own, n_oth, seg.reshape(length, 1), seg2, hit, proj, *pieces, *before, *ahead)


def bwd_kernel(at_ref, seg_s, qkv_ref, segc_ref, segr_ref, hit_ref, proj_ref, pext_ref, qf_ref, kf_ref, rinv_ref, o_ref,
               d_own, d_oth, w_out, *rest, tq, tk, dh, first):
    n_late = 3 if first else 5
    (*outs, done_ref, dqkv_s, do_ref, grad_s, vext, doext, dq, dk, dv, dqf, dkf, late_sem) = rest[-(14 if first else 18) - n_late:-n_late]
    late = rest[-n_late:]
    n_own, n_oth, w_ref = late[:3]
    arriving = [pltpu.make_async_copy(src, dst, late_sem.at[i]) for i, (src, dst) in enumerate(zip(rest, late))]
    for copy in arriving:
        copy.start()
    dqkv_ref = outs[1] if first else dqkv_s
    done_ref[0] = 0
    length = qkv_ref.shape[0]
    half = length // 2
    quarter = dh ** (-0.25)
    nh = qkv_ref.shape[1] // (3 * dh)
    for side, d_ref in enumerate((d_own, d_oth)):
        do_ref[side * half:(side + 1) * half, :] = dot(d_ref[...], w_out[...], ((1,), (1,))).astype(jnp.bfloat16)
    lane = lax.broadcasted_iota(jnp.int32, (length, dh), 1)
    for h in range(nh):
        base = h * 3 * dh
        v = qkv_ref[:, base + 2 * dh: base + 3 * dh]
        vext[h, :, :] = jnp.concatenate([v, (lane < 2).astype(jnp.bfloat16)], axis=1)
        d_o = do_ref[:, h * dh:(h + 1) * dh].astype(jnp.float32)
        o = o_ref[:, h * dh:(h + 1) * dh].astype(jnp.float32)
        rinv = rinv_ref[:, h:h + 1]
        delta = -jnp.sum(d_o * o, axis=1, keepdims=True) * rinv
        high = delta.astype(jnp.bfloat16).astype(jnp.float32)
        low = delta - high
        tail = jnp.where(lane == 0, high, jnp.where(lane == 1, low, 0.0))
        doext[h, :, :] = jnp.concatenate([d_o * rinv, tail], axis=1).astype(jnp.bfloat16)
    dq[...] = jnp.zeros_like(dq)
    dk[...] = jnp.zeros_like(dk)
    dv[...] = jnp.zeros_like(dv)
    dqf[...] = jnp.zeros_like(dqf)
    dkf[...] = jnp.zeros_like(dkf)

    def q_body(i, _):
        r0 = pl.multiple_of(i * tq, tq)
        rows = pl.ds(r0, tq)
        segq = segc_ref[rows, :]
        def k_body(j, _):
            c0 = pl.multiple_of(j * tk, tk)
            cols = pl.ds(c0, tk)
            same = segq == segr_ref[:, cols]
            for h in range(nh):
                base = h * 3 * dh
                q = qkv_ref[rows, base: base + dh]
                k = qkv_ref[cols, base + dh: base + 2 * dh]
                qf = qf_ref[h, rows, :]
                kf = kf_ref[h, cols, :]
                s = dot(q, k, ((1,), (1,)))
                e = jnp.exp2(s * (LOG2E * dh ** -0.5))
                a = dot(qf, kf, ((1,), (1,)))
                dc = dot(doext[h, rows, :], vext[h, cols, :], ((1,), (1,)))
                dc = jnp.where(same, dc, 0.0)
                combs, dss, das = [], [], []
                for b in range(tq // BLK):
                    hit = hit_ref[h, pl.ds(i * (tq // BLK) + b, 1), cols] > 0.5
                    hit = jnp.broadcast_to(hit, (BLK, tk))
                    rs = slice(b * BLK, (b + 1) * BLK)
                    combs.append(jnp.where(hit, e[rs], a[rs]))
                    dss.append(jnp.where(hit, dc[rs] * e[rs], 0.0))
                    das.append(jnp.where(hit, 0.0, dc[rs]))
                comb = jnp.where(same, jnp.concatenate(combs, axis=0), 0.0).astype(jnp.bfloat16)
                ds = jnp.concatenate(dss, axis=0).astype(jnp.bfloat16)
                da = jnp.concatenate(das, axis=0).astype(jnp.bfloat16)
                dq[h, rows, :] += dot(ds, k, ((1,), (0,)))
                dqf[h, rows, :] += dot(da, kf, ((1,), (0,)))
                dk[h, cols, :] += dot(ds, q, ((0,), (0,)))
                dkf[h, cols, :] += dot(da, qf, ((0,), (0,)))
                dv[h, cols, :] += dot(comb, doext[h, rows, :dh], ((0,), (0,)))
            return 0
        def k_step(j, _):
            @pl.when(meets(seg_s, r0, tq, pl.multiple_of(j * tk, tk), tk))
            def _():
                k_body(j, 0)
            return 0
        lax.fori_loop(0, length // tk, k_step, 0)
        return 0
    lax.fori_loop(0, length // tq, q_body, 0)

    for h in range(nh):
        base = h * 3 * dh
        for j, dt, dfeat, f_ref in ((0, dq, dqf, qf_ref), (1, dk, dkf, kf_ref)):
            for r0 in range(0, length, CHUNK):
                rows = slice(r0, r0 + CHUNK)
                dpre = (dfeat[h, rows, :] * f_ref[h, rows, :].astype(jnp.float32)).astype(jnp.bfloat16)
                thr = dot(dpre, pext_ref[...], ((1,), (0,)))
                t = qkv_ref[rows, base + j * dh: base + (j + 1) * dh].astype(jnp.float32)
                g = dt[h, rows, :] * dh ** -0.5 + quarter * thr[:, :dh] - (quarter * quarter) * t * thr[:, dh:dh + 1]
                dqkv_ref[rows, base + j * dh: base + (j + 1) * dh] = g.astype(jnp.bfloat16)
        dqkv_ref[:, base + 2 * dh: base + 3 * dh] = dv[h].astype(jnp.bfloat16)

    for copy in arriving:
        copy.wait()
    if not first:
        dqkv_first, w_first = late[3:]
        weights = w_ref[...].reshape(qkv_ref.shape[1], n_own.shape[1])
        weights_first = w_first[...].reshape(qkv_ref.shape[1], n_own.shape[1])
        add_parts(
            lambda rows: dot(dqkv_first[rows, :], weights_first, ((1,), (0,))) + dot(dqkv_ref[rows, :], weights, ((1,), (0,))),
            None, outs[4:], length, False,
        )

    tn = ((0,), (0,))
    cut = w_ref.shape[1]
    grad = dot(dqkv_ref[:half, :], n_own[...], tn) + dot(dqkv_ref[half:, :], n_oth[...], tn)
    grad_s[:, :cut, :] = grad.astype(jnp.bfloat16).reshape(4, cut, n_own.shape[1])
    out = dot(o_ref[:half, :], d_own[...], tn) + dot(o_ref[half:, :], d_oth[...], tn)
    grad_s[:, cut:, :] = out.astype(jnp.bfloat16).reshape(4, o_ref.shape[1] // 4, n_own.shape[1])
    if first:
        outs[0][...] = grad_s[...]
    else:
        for d in range(4):
            outs[d][...] = grad_s[at_ref[0] ^ d]


def attn_bwd(at, qkv, seg, hit, proj, qf, kf, rinv, o, d_own, d_oth, w_out, late, ahead=(), *, tq=512, tk=256):
    length = qkv.shape[0]
    dh, feats = proj.shape
    width = d_own.shape[1]
    heads = qkv.shape[1] // (3 * dh)
    seg2 = seg.reshape(1, length)
    pext = jnp.concatenate([proj.T, jnp.ones((feats, 1), proj.dtype), jnp.zeros((feats, dh - 1), proj.dtype)], axis=1)
    f32, bf16 = jnp.float32, jnp.bfloat16
    smem = pl.BlockSpec(memory_space=pltpu.SMEM)
    vmem = pl.BlockSpec(memory_space=pltpu.VMEM)
    anywhere = pl.BlockSpec(memory_space=pltpu.HBM)
    first = len(late) == 3
    piece = jax.ShapeDtypeStruct(((qkv.shape[1] + o.shape[1]) // 4, width), bf16)
    if first:
        outs = [jax.ShapeDtypeStruct((4,) + piece.shape, bf16), jax.ShapeDtypeStruct(qkv.shape, bf16)]
    else:
        outs = [piece] * 4 + sum_shapes(length, width, False)
    return pl.pallas_call(
        partial(bwd_kernel, tq=tq, tk=tk, dh=dh, first=first),
        in_specs=[smem] * 2 + [vmem] * 13 + [anywhere] * (len(late) + len(ahead)),
        out_specs=[vmem] * len(outs) + [smem],
        out_shape=outs + [jax.ShapeDtypeStruct((1,), jnp.int32)],
        scratch_shapes=[
            pltpu.VMEM((16, 128) if first else qkv.shape, bf16),
            pltpu.VMEM(o.shape, bf16),
            pltpu.VMEM((4,) + piece.shape, bf16),
            pltpu.VMEM((heads, length, 2 * dh), bf16),
            pltpu.VMEM((heads, length, 2 * dh), bf16),
            pltpu.VMEM((heads, length, dh), f32),
            pltpu.VMEM((heads, length, dh), f32),
            pltpu.VMEM((heads, length, dh), f32),
            pltpu.VMEM((heads, length, feats), f32),
            pltpu.VMEM((heads, length, feats), f32),
            pltpu.SemaphoreType.DMA((5,)),
        ]
        + [pltpu.VMEM(v.shape, v.dtype) for v in late],
        compiler_params=pltpu.CompilerParams(vmem_limit_bytes=56 * 1024 * 1024),
        cost_estimate=pl.CostEstimate(flops=42 * 10**9, bytes_accessed=2 * 10**7, transcendentals=10**6),
        name="attn_bwd",
    )(at, seg2, qkv, seg.reshape(length, 1), seg2, hit, proj, pext, qf, kf, rinv, o, d_own, d_oth, w_out, *late, *ahead)


def hit_lanes(lists, length):
    nb = lists.shape[1]
    ids = lax.broadcasted_iota(jnp.int32, (1, 1, length), 2) // BLK
    out = lists[:, :, 0:1] == ids
    for s in range(1, lists.shape[2]):
        out = out | (lists[:, :, s:s + 1] == ids)
    return out.astype(jnp.float32)

from jax.sharding import PartitionSpec as P


def gelu_pair(u):
    mag = jnp.abs(u)
    t = 1.0 / (1.0 + (0.3275911 * 0.7071067811865476) * mag)
    bell = jnp.exp2(u * u * (-0.5 * LOG2E))
    poly = t * (0.127414796 + t * (-0.142248368 + t * (0.7107068705 + t * (-0.7265760135 + t * 0.5307027145))))
    tail = poly * bell
    cdf = jnp.where(u >= 0.0, 1.0 - tail, tail)
    return u * cdf, cdf + u * bell * 0.3989422804014327


def mlp_kernel(n_own, n_oth, dy_own, dy_oth, w_ref, *rest, first):
    act_ref, dpre_ref, *sums = rest[-(3 if first else 4):]
    half, width = n_own.shape
    piece = w_ref.shape[1] // 2
    hid = act_ref.shape[1]
    up = w_ref[:, :piece, :].reshape(width, hid)
    down = w_ref[:, piece:, :].reshape(hid, width)
    for side, (n_ref, dy_ref) in enumerate(((n_own, dy_own), (n_oth, dy_oth))):
        rs = slice(side * half, (side + 1) * half)
        pre = dot(n_ref[...], up, ((1,), (0,)))
        d_act = dot(dy_ref[...], down, ((1,), (1,)))
        act, slope = gelu_pair(pre)
        d_pre = (d_act * slope).astype(jnp.bfloat16)
        act_ref[rs, :] = act.astype(jnp.bfloat16)
        dpre_ref[rs, :] = d_pre
        part = dot(d_pre, up, ((1,), (1,)))
        if first:
            sums[0][rs, :] = part
        else:
            sums[side][...] = (part + rest[0][rs, :]).astype(sums[side].dtype)


def mlp_first(n2, dy, pack, before=None, ahead=()):
    tokens, width = 2 * n2[0].shape[0], n2[0].shape[1]
    hid = pack.shape[0] * pack.shape[1] // 2
    bf16, f32 = jnp.bfloat16, jnp.float32
    first = before is None
    vmem = pl.BlockSpec(memory_space=pltpu.VMEM)
    return pl.pallas_call(
        partial(mlp_kernel, first=first),
        in_specs=[vmem] * (5 if first else 6) + [pl.BlockSpec(memory_space=pltpu.HBM)] * len(ahead),
        out_specs=[vmem] * (3 if first else 4),
        out_shape=[jax.ShapeDtypeStruct((tokens, hid), bf16)] * 2 + sum_shapes(tokens, width, first),
        compiler_params=pltpu.CompilerParams(vmem_limit_bytes=48 * 1024 * 1024),
        cost_estimate=pl.CostEstimate(flops=2 * 10**9, bytes_accessed=2 * 10**6, transcendentals=10**6),
        name="mlp_first",
    )(*n2, *dy, pack, *(() if first else (before,)), *ahead)


def mlp_grad_kernel(n_own, n_oth, dy_own, dy_oth, act_ref, dpre_ref, *rest):
    grad_ref = rest[-1]
    half, width = n_own.shape
    piece = grad_ref.shape[3] // 2
    hid = act_ref.shape[1]
    tn = ((0,), (0,))
    for j in range(width // (4 * piece)):
        cut = slice(4 * j * piece, 4 * (j + 1) * piece)
        up_g = dot(n_own[:, cut], dpre_ref[:half, :], tn) + dot(n_oth[:, cut], dpre_ref[half:, :], tn)
        grad_ref[2 * j:2 * j + 2, :, 0, :piece, :] = up_g.astype(jnp.bfloat16).reshape(2, 2, piece, hid)
        down_g = dot(act_ref[:half, cut], dy_own[...], tn) + dot(act_ref[half:, cut], dy_oth[...], tn)
        grad_ref[2 * j:2 * j + 2, :, 0, piece:, :] = down_g.astype(jnp.bfloat16).reshape(2, 2, piece, width)


def mlp_second(n2, dy, acted, d_pre, rows, grads=None):
    width = n2[0].shape[1]
    whole = lambda shape: pl.BlockSpec(shape, lambda i: (0,) * len(shape))
    args = [*n2, *dy, acted, d_pre]
    first = grads is None
    shape = (4, 2, 2, rows, width)
    return pl.pallas_call(
        mlp_grad_kernel,
        grid=(1,),
        in_specs=[whole(v.shape) for v in args] + [pl.BlockSpec(memory_space=pltpu.HBM)] * (not first),
        out_specs=pl.BlockSpec((4, 2, 1) + shape[3:], lambda i: (0, 0, 0 if first else 1, 0, 0)),
        out_shape=jax.ShapeDtypeStruct(shape, jnp.bfloat16),
        input_output_aliases={} if first else {len(args): 0},
        compiler_params=pltpu.CompilerParams(vmem_limit_bytes=48 * 1024 * 1024),
        cost_estimate=pl.CostEstimate(flops=2 * 10**9, bytes_accessed=2 * 10**6, transcendentals=0),
        name="mlp_second",
    )(*args, *([] if first else [grads]))


def mlp_out_kernel(act_a, act_b, w_a, w_b, *rest):
    half, width = rest[-1].shape
    piece = w_a.shape[1] // 2
    downs = [w[:, piece:, :].reshape(-1, width) for w in (w_a, w_b)]
    for side, out_ref in enumerate(rest[-2:]):
        rows = slice(side * half, (side + 1) * half)
        total = dot(act_a[rows, :], downs[0], ((1,), (0,))) + dot(act_b[rows, :], downs[1], ((1,), (0,)))
        out_ref[...] = total.astype(out_ref.dtype)


def call(kernel, name, args, outs, ahead=(), smem=(), scratch=(), passed=()):
    vmem = pl.BlockSpec(memory_space=pltpu.VMEM)
    anywhere = pl.BlockSpec(memory_space=pltpu.HBM)
    n_in = len(smem) + len(args)
    return pl.pallas_call(
        kernel,
        in_specs=[pl.BlockSpec(memory_space=pltpu.SMEM)] * len(smem)
        + [vmem] * len(args)
        + [anywhere] * (len(passed) + len(ahead)),
        out_specs=[vmem] * len(outs) + [anywhere] * len(passed),
        out_shape=list(outs) + [jax.ShapeDtypeStruct(v.shape, v.dtype) for v in passed],
        input_output_aliases={n_in + i: len(outs) + i for i in range(len(passed))},
        scratch_shapes=list(scratch),
        compiler_params=pltpu.CompilerParams(vmem_limit_bytes=48 * 1024 * 1024),
        cost_estimate=pl.CostEstimate(flops=10**9, bytes_accessed=4 * 10**6, transcendentals=0),
        name=name,
    )(*smem, *args, *passed, *ahead)


norm_eps = 1e-05


def norm_rows(values):
    center = values - jnp.mean(values, axis=1, keepdims=True)
    scale = lax.rsqrt(jnp.mean(center * center, axis=1, keepdims=True) + norm_eps)
    return center * scale, scale


def norm_back(grad, xhat, scale, gain):
    dx = grad * gain
    return scale * (
        dx - jnp.mean(dx, axis=1, keepdims=True) - xhat * jnp.mean(dx * xhat, axis=1, keepdims=True)
    )


ROWS = 128


def enter_kernel(dealt_ref, gain_ref, bias_ref, *rest):
    x_ref, n_ref = rest[-2:]
    width = x_ref.shape[1]
    for i in range(x_ref.shape[0] // ROWS):
        rows = slice(i * ROWS, (i + 1) * ROWS)
        x = dealt_ref[:, :, rows].reshape(width, ROWS).astype(jnp.float32).T
        x_ref[rows, :] = x.astype(jnp.bfloat16)
        n_ref[rows, :] = (norm_rows(x)[0] * gain_ref[...] + bias_ref[...]).astype(jnp.bfloat16)


def turn_kernel(z_ref, d0, d1, d2, d3, *rest):
    out_ref, turned = rest[-4], rest[-1]
    for d, part in enumerate((d0, d1, d2, d3)):
        turned[z_ref[0] ^ d] = part[...]
    for i in range(out_ref.shape[0] // ROWS):
        rows = slice(i * ROWS, (i + 1) * ROWS)
        out_ref[rows, :] = turned[:, :, rows].reshape(out_ref.shape[1], ROWS).astype(jnp.float32).T.astype(jnp.bfloat16)


def pick_kernel(which_ref, own_ref, got_ref, *rest):
    out_ref = rest[-1]
    rows = pl.ds(pl.multiple_of(which_ref[1] * out_ref.shape[0], 16), out_ref.shape[0])

    @pl.when(which_ref[0] == 1)
    def _():
        out_ref[...] = own_ref[rows, :]

    @pl.when(which_ref[0] == 0)
    def _():
        out_ref[...] = got_ref[rows, :]


def middle_kernel(x_ref, near_ref, got_ref, gain_ref, bias_ref, *rest):
    resid_ref, n_ref = rest[-2:]
    for i in range(x_ref.shape[0] // ROWS):
        rows = slice(i * ROWS, (i + 1) * ROWS)
        resid = x_ref[rows, :].astype(jnp.float32) + near_ref[rows, :] + got_ref[rows, :].astype(jnp.float32)
        resid_ref[rows, :] = resid
        xhat = norm_rows(resid.astype(jnp.bfloat16).astype(jnp.float32))[0]
        n_ref[rows, :] = (xhat * gain_ref[...] + bias_ref[...]).astype(jnp.bfloat16)


def middle_back_kernel(own_ref, got_ref, resid_ref, dy_ref, gain_ref, *rest):
    d_ref, low_ref, vec_ref = rest[-3:]
    total = None
    for i in range(own_ref.shape[0] // ROWS):
        rows = slice(i * ROWS, (i + 1) * ROWS)
        grad = own_ref[rows, :] + got_ref[rows, :].astype(jnp.float32)
        xhat, scale = norm_rows(resid_ref[rows, :].astype(jnp.bfloat16).astype(jnp.float32))
        sums = [jnp.sum(grad * xhat, axis=0, keepdims=True), jnp.sum(grad, axis=0, keepdims=True)]
        total = sums if total is None else [a + b for a, b in zip(total, sums)]
        d = dy_ref[rows, :].astype(jnp.float32) + norm_back(grad, xhat, scale, gain_ref[...])
        d_ref[rows, :] = d
        low_ref[rows, :] = d.astype(jnp.bfloat16)
    vec_ref[0:1, :] = total[0]
    vec_ref[1:2, :] = total[1]


def block_kernel(resid_ref, own_ref, got_ref, *rest):
    out_ref = rest[-1]
    parts, quarter, _ = out_ref.shape
    for i in range(own_ref.shape[0] // ROWS):
        rows = slice(i * ROWS, (i + 1) * ROWS)
        out = resid_ref[rows, :] + own_ref[rows, :] + got_ref[rows, :].astype(jnp.float32)
        out_ref[:, :, rows] = out.T.astype(jnp.bfloat16).reshape(parts, quarter, ROWS)


def leave_kernel(near_ref, got_ref, x_ref, d_ref, gain_ref, vec_ref, *rest):
    out_ref = rest[-1]
    parts, quarter = out_ref.shape[0], near_ref.shape[1] // out_ref.shape[0]
    total = None
    for i in range(near_ref.shape[0] // ROWS):
        rows = slice(i * ROWS, (i + 1) * ROWS)
        grad = near_ref[rows, :] + got_ref[rows, :].astype(jnp.float32)
        xhat, scale = norm_rows(x_ref[rows, :].astype(jnp.float32))
        sums = [jnp.sum(grad * xhat, axis=0, keepdims=True), jnp.sum(grad, axis=0, keepdims=True)]
        total = sums if total is None else [a + b for a, b in zip(total, sums)]
        out = d_ref[rows, :] + norm_back(grad, xhat, scale, gain_ref[...])
        out_ref[:, :quarter, rows] = out.T.astype(jnp.bfloat16).reshape(parts, quarter, ROWS)
    vec = jnp.concatenate(total + [vec_ref[0:1, :], vec_ref[1:2, :]], axis=0)
    high = vec.astype(jnp.bfloat16).astype(jnp.float32)
    both = jnp.concatenate([high, vec - high], axis=0)
    tail = out_ref.shape[1] - quarter
    for k in range(parts):
        mine = both[:, k * quarter:(k + 1) * quarter]
        mine = jnp.concatenate([mine, jnp.zeros((8, out_ref.shape[2] - quarter), jnp.float32)], axis=1)
        mine = jnp.concatenate([mine, jnp.zeros((tail - 8, out_ref.shape[2]), jnp.float32)], axis=0)
        out_ref[k, quarter:, :] = mine.astype(jnp.bfloat16)


def sum_kernel(a, b, c, d, *rest, out_at):
    total = a[...].astype(jnp.float32) + b[...].astype(jnp.float32) + c[...].astype(jnp.float32) + d[...].astype(jnp.float32)
    rest[out_at][...] = total.astype(jnp.bfloat16)


def split_kernel(both_ref, a_ref, b_ref):
    cut = a_ref.shape[1]
    a_ref[...] = both_ref[:, :cut, :].astype(jnp.float32)
    b_ref[...] = both_ref[:, cut:, :].astype(jnp.float32)


def sum_slices_kernel(a, *rest):
    rest[-2][...] = jnp.sum(a[...].astype(jnp.float32), axis=0).astype(jnp.bfloat16)


def sum_four(pieces, name, ahead=(), passed=()):
    out = [jax.ShapeDtypeStruct(pieces[0].shape, jnp.bfloat16)]
    at = len(passed) + len(ahead)
    return call(partial(sum_kernel, out_at=at), name, pieces, out, ahead=ahead, passed=passed)


def own_group(i):
    return (i & 3) // 2 == (i >> 2) & 1


def far_group(i):
    return not own_group(i)


def shards(
    activations, segment_ids, block_lists, feature_proj, input_norm_gain, input_norm_bias, qkv_weight,
    out_weight, middle_norm_gain, middle_norm_bias, up_weight, down_weight, out_grad,
):
    rows_n, heads_n = lax.axis_size("row"), lax.axis_size("head")
    total = rows_n * heads_n
    r, z = lax.axis_index("row"), lax.axis_index("head")
    c, p = r % 2, (r // 2) % 4
    groups = rows_n // 8
    pairs = [[2 * i, 2 * i + 1] for i in range(rows_n // 2)]
    planes = [[8 * g + i for i in range(8)] for g in range(groups)]
    quads = [[8 * g + 2 * i + k for i in range(4)] for g in range(groups) for k in range(2)]
    width = input_norm_gain.shape[0]
    quarter = width // heads_n
    seq_count, length = segment_ids.shape
    half = length // 2
    lists_here = block_lists.shape[1]
    bf16, f32 = jnp.bfloat16, jnp.float32
    local = (z // 2) == c
    par = z % 2

    def move(v, mask, only=None):
        moves = [(i, i ^ mask) for i in range(total) if only is None or only(i)]
        return lax.ppermute(v, ("row", "head"), moves)

    def later(i, dep):
        one = lax.slice(dep, (0,) * dep.ndim, (1,) * dep.ndim).reshape(())
        return i + (one != one).astype(jnp.int32)

    def deal_z(v):
        return lax.all_to_all(v, "head", 0, 0, tiled=True)

    def tied(v, dep):
        one = lax.slice(dep, (0,) * dep.ndim, (1,) * dep.ndim).reshape(())
        return v + (one != one).astype(v.dtype)

    def deal(v, side, order):
        v = v.T

        def token_half(k):
            return jnp.stack([lax.dynamic_slice_in_dim(v, s * length + k * half, half, 1) for s in range(seq_count)])

        keep, got = token_half(side), move(token_half(1 - side), 4)
        return jnp.concatenate([jnp.where(order == 0, keep, got), jnp.where(order == 0, got, keep)], 0)

    def collect(v):
        v = v.reshape(2, seq_count, quarter, half)
        keep = lax.dynamic_index_in_dim(v, c, 0, keepdims=False)
        got = move(lax.dynamic_index_in_dim(v, 1 - c, 0, keepdims=False), 4)
        low, high = jnp.where(c == 0, keep, got), jnp.where(c == 0, got, keep)
        return jnp.concatenate([w[s] for s in range(seq_count) for w in (low, high)], 1).T

    def fetch_z(mine):
        return [mine] + [move(mine, d, own_group) for d in (1, 2, 3)]

    def choose(got, here):
        return jnp.stack([jnp.where(here, got[0], got[2]), jnp.where(here, got[1], got[3])])

    def fetch_plane(both):
        return [both] + [move(both, 8 * d) for d in (1, 2, 3)]

    def give_z(same, other, ahead, before_slice):
        parts = (same, move(other, 1, own_group), move(same, 2, far_group), move(other, 3, far_group))
        (fin,) = sum_four(parts, "sum_z", ahead=(ahead,))
        if groups > 1:
            fin = lax.psum(fin.astype(f32), "row", axis_index_groups=[[8 * g + i for g in range(groups)] for i in range(8)])
            fin = fin.astype(bf16)
        return call(
            pick_kernel, "pick", (fin, move(fin, 4)), (jax.ShapeDtypeStruct((fin.shape[0] // 2, width), bf16),),
            smem=(jnp.stack([local.astype(jnp.int32), c]),), ahead=(before_slice,),
        )[0]

    def gather_plane(v):
        return lax.all_gather(v, "row", axis=0, axis_index_groups=planes)

    cut = lambda w, n, at: lax.dynamic_slice_in_dim(w, at * n, n, 0)

    aux = jnp.concatenate([block_lists.reshape(seq_count, -1), segment_ids], 1).astype(bf16)
    aux_got = move(aux, 4)
    aux = jnp.where(c == 0, jnp.concatenate([aux, aux_got], 0), jnp.concatenate([aux_got, aux], 0))
    n_list = aux.shape[1] - length
    seg = lax.dynamic_index_in_dim(aux[:, n_list:], z, 0, keepdims=False).astype(jnp.int32)

    n_qkv, n_out = qkv_weight.shape[1] // 4, out_weight.shape[0] // 4
    extra = 16
    rider = aux[:, :n_list].reshape(-1)
    rider = jnp.pad(rider, (0, extra * width - rider.shape[0])).reshape(extra, width)
    mine = [cut(qkv_weight.T, n_qkv, p), cut(out_weight, n_out, p), rider]
    both = choose(fetch_z(jnp.concatenate(mine, 0)), local)
    lists = both[:, n_qkv + n_out:].reshape(2, -1)[:, :4 * n_list].reshape(2, 4, n_list).astype(jnp.int32)
    lists = lax.dynamic_index_in_dim(lists, z, 1, keepdims=False).reshape((2, lists_here) + block_lists.shape[2:])
    pieces = fetch_plane(both[:, :n_qkv + n_out])
    at = jnp.full((1,), p, jnp.int32)

    four = deal(activations, c, later(c, both))
    gain1, bias1, gain2, bias2 = (
        v.reshape(1, width) for v in (input_norm_gain, input_norm_bias, middle_norm_gain, middle_norm_bias)
    )
    shape_of = jax.ShapeDtypeStruct
    half_low, half_wide = shape_of((half, width), bf16), shape_of((half, width), f32)
    dy_four = deal(out_grad, c, c)
    x_half, n1_half = call(enter_kernel, "enter", (deal_z(four), gain1, bias1), (half_low, half_low), ahead=(dy_four,))

    n_up, n_hid = width // 8, down_weight.shape[0] // 8
    q8 = later(r % 8, both)
    mine = jnp.concatenate([cut(up_weight, n_up, q8), cut(down_weight, n_hid, q8)], 0)
    all_z = lax.all_gather(mine, "head", axis=0).reshape((1, 2, 2) + mine.shape)
    send = [jnp.broadcast_to(all_z[:, :, i], (4, 2) + mine.shape).reshape((8,) + mine.shape) for i in range(2)]
    packs = [lax.all_to_all(v, "row", 0, 0, axis_index_groups=planes, tiled=True) for v in send]

    shift = c * half
    seg = lax.dynamic_slice_in_dim(jnp.concatenate([seg, seg]), shift, length, 0)
    hits = []
    for own in lists:
        own = lax.dynamic_slice_in_dim(jnp.concatenate([own, own], 1), shift // BLK, length // BLK, 1)
        hit = hit_lanes(own, length)
        hits.append(lax.dynamic_slice_in_dim(jnp.concatenate([hit, hit], 2), shift, length, 2))

    n1 = (n1_half, move(n1_half, 4))
    att = [attn_fwd(at, *n1, pieces, 0, seg, hits[0], feature_proj)]
    z_late = z + att[0][-1][0]
    dy_parts = [lax.dynamic_index_in_dim(dy_four, z_late ^ d, 0, keepdims=False) for d in range(heads_n)]
    dy_got = [move(v, d) if d else v for d, v in enumerate(dy_parts)]
    att.append(attn_fwd(at, *n1, pieces, 1, seg, hits[1], feature_proj, (att[0][0], att[0][6]), (*send, *dy_parts)))
    heads_out = [v[0] for v in att]
    rinv = [v[1] for v in att]
    feat_q, feat_k, qkv, wq, outw = zip(*(v[-6:-1] for v in att))
    outw = [v.reshape(-1, width) for v in outw]
    dy_half, near, away = call(
        turn_kernel, "turn", dy_got, (half_low,), smem=(z.reshape(1),), passed=att[1][2:4], ahead=(packs[0],),
        scratch=(pltpu.VMEM((heads_n, quarter, half), bf16),),
    )
    resid, n2_half = call(
        middle_kernel, "middle", (x_half, near, move(away, 4), gain2, bias2), (half_wide, half_low),
    )
    n2 = (n2_half, move(n2_half, 4))
    dy = (dy_half, move(dy_half, 4))
    acted, d_pre, dn = mlp_first(n2, dy, packs[0])
    grads = mlp_second(n2, dy, acted, d_pre, packs[0].shape[1])
    acted_a = acted
    acted, d_pre, dn_own, dn_oth = mlp_first(n2, dy, packs[1], dn, (grads,))
    grads = mlp_second(n2, dy, acted, d_pre, packs[1].shape[1], grads)
    mo_own, mo_oth = call(
        mlp_out_kernel, "mlp_out", (acted_a, acted, *packs), (half_wide, half_low), ahead=(grads,)
    )
    d_resid, d_half, vec2 = call(
        middle_back_kernel, "middle_back", (dn_own, move(dn_oth, 4), resid, dy_half, gain2),
        (half_wide, half_low, shape_of((2, width), f32)),
    )
    (block_send,) = call(
        block_kernel, "block", (resid, mo_own, move(mo_oth, 4)), (shape_of((heads_n, quarter, half), bf16),)
    )
    block_got = deal_z(block_send)
    block_out = collect(block_got)
    d_branch = (d_half, move(d_half, 4))
    grads = lax.psum_scatter(
        grads.reshape(-1, width), "row", scatter_dimension=0, axis_index_groups=quads, tiled=True
    ).reshape(2, 2, -1, width)
    def attn_back(i, late, ahead):
        return attn_bwd(
            at, qkv[i], seg, hits[i], feature_proj, feat_q[i], feat_k[i], rinv[i], heads_out[i], *d_branch, outw[i],
            (*n1, wq[i], *late), ahead,
        )

    back = [attn_back(0, (), (mo_oth,))]
    c_late = later(c + back[0][2][0], block_got)
    keep = lax.dynamic_index_in_dim(grads, c_late, 0, keepdims=False)
    got = move(lax.dynamic_index_in_dim(grads, 1 - c_late, 0, keepdims=False), 4)
    four = jnp.concatenate([jnp.where(c == 0, keep, got), jnp.where(c == 0, got, keep)], 0)
    four_flat = four.reshape(-1, width)
    mlp_slice = mlp_grads = lax.psum_scatter(four_flat, "head", scatter_dimension=0, tiled=True)
    if groups > 1:
        mlp_grads = lax.psum(mlp_grads, "row", axis_index_groups=[[8 * g + i for g in range(groups)] for i in range(8)])

    back.append(attn_back(1, (back[0][1], wq[0]), (block_got, four_flat)))

    def across(pieces):
        return [pieces[0]] + [move(pieces[d], 8 * d) for d in (1, 2, 3)]

    first = lax.all_to_all(back[0][0], "row", 0, 0, axis_index_groups=quads, tiled=True)
    first, *passed = call(
        sum_slices_kernel, "sum_first", (first,), (shape_of(first.shape[1:], bf16),), passed=(mlp_grads,), ahead=(back[1][0],)
    )
    (mlp_grads,) = passed
    pieces, (near, away) = back[1][:4], back[1][4:6]
    mlp_grads = gather_plane(mlp_grads)
    up_grad = mlp_grads[:, :n_up].reshape(width, -1).astype(f32)
    down_grad = mlp_grads[:, n_up:].reshape(-1, width).astype(f32)
    (send,) = call(
        leave_kernel, "leave", (near, move(away, 4), x_half, d_resid, gain1, vec2),
        (shape_of((heads_n, quarter + 16, half), bf16),), ahead=(first,),
    )
    (second,) = sum_four(across(pieces), "sum_second")
    got = deal_z(send)
    qkv_slice = give_z(first, second, got, mlp_grads)
    input_grad = collect(got[:, :quarter]).astype(f32)
    vec = jnp.sum(got[:, quarter:quarter + 8, :quarter].astype(f32), 0)
    got = gather_plane(qkv_slice)
    vec = tied(vec[:4] + vec[4:], qkv_slice)
    for mask in (4, 8, 16):
        vec = vec + move(vec, mask)
    if groups > 1:
        vec = lax.psum(vec, "row", axis_index_groups=[[8 * g + i for g in range(groups)] for i in range(8)])
    qkv_grad, out_w_grad = call(
        split_kernel, "split", (got.reshape(4, n_qkv + n_out, width),),
        (shape_of((4, n_qkv, width), f32), shape_of((4, n_out, width), f32)),
    )
    qkv_grad = qkv_grad.reshape(-1, width).T
    out_w_grad = out_w_grad.reshape(-1, width)
    return (
        block_out, input_grad, vec[0], vec[1], qkv_grad, out_w_grad, vec[2], vec[3], up_grad, down_grad,
    )


def solution(mesh):
    return jax.shard_map(
        shards,
        mesh=mesh,
        in_specs=(
            P("row", "head"), P("row", None), P("row", "head", None, None), P(), P(), P(), P(None, "head"),
            P("head", None), P(), P(), P(None, "head"), P("head", None), P("row", "head"),
        ),
        out_specs=(
            P("row", "head"), P("row", "head"), P("head"), P("head"), P(None, "head"), P("head", None),
            P("head"), P("head"), P(None, "head"), P("head", None),
        ),
        check_vma=False,
    )
```
